32 devices in a mesh: expert: 4 (over y, core), context: 2 (over x), dp: 4 (over z).
Axes of the slice: x: 2, y: 2, z: 4, core: 2. Of those that a mesh axis runs over, the one named last changes fastest.
Arguments:
- tokens: bfloat16 [8, 8, 1024, 512], P('dp', 'expert', 'context'), may hold values from -6 to 6
- gain_attn: float32 [512], replicated, may hold values from 0.5 to 1.5
- query_key_value_weight: bfloat16 [512, 1536], replicated, may hold values from -0.25 to 0.25
- w_out: bfloat16 [512, 512], replicated, may hold values from -2 to 2
- gain_mix: float32 [512], replicated, may hold values from 0.5 to 1.5
- w_control: bfloat16 [512, 8], replicated, may hold values from -0.25 to 0.25
- w_in: bfloat16 [8, 512, 2048], P('expert'), may hold values from -1.5 to 1.5
- w_back: bfloat16 [8, 2048, 512], P('expert'), may hold values from -1 to 1
- segments: int32 [8, 8, 1024], P('dp', 'expert'), may hold values from 0 to 2, as said below
- valid: int32 [8, 8, 1024], P('dp', 'expert'), may hold values from 0 to 1, as said below
- cotangent: bfloat16 [8, 8, 1024, 512], P('dp', 'expert', 'context'), may hold values from -6 to 6
Outputs:
- output: bfloat16 [8, 8, 1024, 512], P('dp', 'expert', 'context')
- d_tokens: bfloat16 [8, 8, 1024, 512], P('dp', 'expert', 'context')
- grad_gain_attn: float32 [512], replicated
- grad_qkv: float32 [512, 1536], replicated
- grad_out: float32 [512, 512], replicated
- grad_gain_mix: float32 [512], replicated
- grad_control: float32 [512, 8], replicated
- grad_in: float32 [8, 512, 2048], P('expert')
- grad_back: float32 [8, 2048, 512], P('expert')
- stats: float32 [3], replicated
The draws below stay inside these ranges and needn't reach their ends.
Inputs may be any that keep to these rules, and one draw needn't show every extreme that they name: `segments`: never falling along a sequence, starting at 0. Along each sequence the valid slots are the leading ones, and the empty slots after them lie in the sequence's last document; in each replica some sequence is valid in all 1024 slots.
All inputs are finite; a program needn't handle non-finite values.
Results may differ from the reference program's by a relative error of at most 0.033.
Values may be sent and summed in bfloat16 or wider, within the bound.
A program may use at most 448 MiB of HBM per device.

```python
from functools import partial
import jax
import jax.numpy as jnp
from jax import lax

D = 512
HEADS = 8
FF = 2048
LENGTH = 1024
HEAD = 64
GROUP = 8
EXPERTS = 8
REPLICAS = 8


def doc_marks(key):
    key = jax.random.fold_in(key, 11)
    key_first, key_second, key_ends, key_full = jax.random.split(key, 4)
    first_cut = jax.random.randint(key_first, (REPLICAS, GROUP), LENGTH // 8, 3 * LENGTH // 8)
    second_cut = jax.random.randint(key_second, (REPLICAS, GROUP), 5 * LENGTH // 8, 7 * LENGTH // 8)
    seq_ends = jax.random.randint(key_ends, (REPLICAS, GROUP), second_cut + 1, LENGTH + 1)
    full_row = jax.random.randint(key_full, (REPLICAS, 1), 0, GROUP)
    seq_ends = jnp.where(jnp.arange(GROUP)[None, :] == full_row, LENGTH, seq_ends)
    return (first_cut, second_cut, seq_ends)


def draw_segments(key, part):
    first_cut, second_cut, seq_ends = doc_marks(key)
    places = jnp.arange(LENGTH)
    first_part = (places[None, None, :] >= first_cut[..., None]).astype(jnp.int32)
    second_part = (places[None, None, :] >= second_cut[..., None]).astype(jnp.int32)
    return first_part + second_part


def draw_valid(key, part):
    first_cut, second_cut, seq_ends = doc_marks(key)
    places = jnp.arange(LENGTH)
    return (places[None, None, :] < seq_ends[..., None]).astype(jnp.int32)


def levels(own_key, dims, cuts, smallest, high):
    loudness, own = 1.0, jax.random.fold_in(own_key, 6)
    for axis_at, parts in cuts:
        heights = jnp.exp(jax.random.uniform(jax.random.fold_in(own, axis_at), (parts,), jnp.float32, smallest / len(cuts), high / len(cuts)))
        loudness = loudness * jnp.repeat(heights, dims[axis_at] // parts).reshape([-1 if axis == axis_at else 1 for axis in range(len(dims))])
    return loudness


def centred(stream_key, shape, scale, bound, cuts=(), held_as=jnp.bfloat16):
    entries = jax.random.normal(stream_key, shape, jnp.float32) * scale
    if len(cuts) > 0:
        entries = levels(stream_key, shape, cuts, -0.22, 0.18) * entries
    return jnp.clip(entries, min=-bound, max=bound).astype(held_as)


def setup_inputs(seed: int = 0) -> dict:
    seeds = jax.random.split(jax.random.key(seed), 12)
    return {
        "tokens": centred(seeds[0], (REPLICAS, GROUP, LENGTH, D), 1.0, 6.0, ((0, 4), (1, 4), (2, 2))),
        "gain_attn": jnp.clip(1.0 + 0.1 * jax.random.normal(seeds[1], (D,), jnp.float32), 0.5, 1.5),
        "query_key_value_weight": centred(seeds[2], (D, 3 * D), D ** -0.5, 0.25),
        "w_out": centred(seeds[3], (D, D), (D // 64) ** -0.5, 2.0),
        "gain_mix": jnp.clip(1.0 + 0.1 * jax.random.normal(seeds[4], (D,), jnp.float32), 0.5, 1.5),
        "w_control": centred(seeds[5], (D, EXPERTS), D ** -0.5, 0.25),
        "w_in": centred(seeds[6], (EXPERTS, D, FF), (D // 32) ** -0.5, 1.5, ((0, 4),)),
        "w_back": centred(seeds[7], (EXPERTS, FF, D), (FF // 64) ** -0.5, 1.0, ((0, 4),)),
        "segments": draw_segments(jax.random.fold_in(seeds[11], 71), 0),
        "valid": draw_valid(jax.random.fold_in(seeds[11], 71), 0),
        "cotangent": centred(seeds[10], (REPLICAS, GROUP, LENGTH, D), 1.0, 6.0, ((0, 4), (1, 4), (2, 2))),
    }


NEG_FILL = -1e+30
MAXIMUM_PRECISE = lax.Precision.HIGHEST

@jax.custom_vjp
def reduced_width(v):
    return lax.optimization_barrier(v.astype(jnp.bfloat16)).astype(jnp.float32)

@jax.custom_vjp
def reduced_backward(v):
    return v

def low_keep(v):
    return (reduced_width(v), None)

def low_pass(kept, grad):
    return (grad,)

def back_keep(v):
    return (v, None)

def back_low(kept, grad):
    return (reduced_width(grad),)
reduced_width.defvjp(low_keep, low_pass)
reduced_backward.defvjp(back_keep, back_low)

def layer_norm(stream, gain):
    center = stream - lax.optimization_barrier(jnp.mean(stream, -1, keepdims=True))
    spread = lax.optimization_barrier(jnp.mean(center * center, -1, keepdims=True))
    return center * lax.rsqrt(spread + 1e-05) * gain

def attend_sequence(pack):
    queries, keys, values, seg_row, valid_row = pack
    scores = jnp.einsum('qhd,khd->hqk', queries, keys, precision=MAXIMUM_PRECISE) * HEAD ** (-0.5)
    scores = reduced_backward(scores)
    places = jnp.arange(LENGTH)
    allowed = (places[None, :] <= places[:, None]) & (seg_row[None, :] == seg_row[:, None]) & (valid_row[None, :] > 0)
    scores = jnp.where(allowed[None], scores, NEG_FILL)
    probs = reduced_width(jax.nn.softmax(scores, axis=-1))
    attended = jnp.einsum('hqk,khd->qhd', probs, values, precision=MAXIMUM_PRECISE)
    return attended.reshape(LENGTH, D)

def one_replica(params, pack):
    gain_attn, query_key_value_weight, w_out, gain_mix, w_control, w_in, w_back = params
    stream, seg_rows, valid_rows = pack
    activation_reduced = reduced_width(layer_norm(stream, gain_attn))
    query_key_value = reduced_backward(reduced_width(jnp.einsum('fia,ap->fip', activation_reduced, query_key_value_weight, precision=MAXIMUM_PRECISE)))
    queries = query_key_value[..., :D].reshape(GROUP, LENGTH, HEADS, HEAD)
    keys = query_key_value[..., D:2 * D].reshape(GROUP, LENGTH, HEADS, HEAD)
    values = query_key_value[..., 2 * D:].reshape(GROUP, LENGTH, HEADS, HEAD)
    attended = lax.map(jax.checkpoint(attend_sequence), (queries, keys, values, seg_rows, valid_rows))
    attended = reduced_backward(reduced_width(attended))
    attn_out = reduced_backward(jnp.einsum('gld,de->gle', attended, w_out, precision=MAXIMUM_PRECISE))
    resid = stream + attn_out
    u_low = reduced_width(layer_norm(resid, gain_mix))
    logits = reduced_backward(jnp.einsum('gld,de->gle', u_low, w_control, precision=MAXIMUM_PRECISE))
    masked = jnp.where(valid_rows[..., None] > 0, logits, NEG_FILL)
    weights_low = reduced_width(jax.nn.softmax(masked, axis=0))
    mixed = reduced_backward(reduced_width(jnp.einsum('gle,gld->eld', weights_low, u_low, precision=MAXIMUM_PRECISE)))
    pre_act = reduced_backward(jnp.einsum('eld,edf->elf', mixed, w_in, precision=MAXIMUM_PRECISE))
    act_low = reduced_width(jax.nn.gelu(pre_act))
    expert_out = reduced_backward(reduced_width(jnp.einsum('elf,efd->eld', act_low, w_back, precision=MAXIMUM_PRECISE)))
    mix_out = jnp.einsum('gle,eld->gld', weights_low, expert_out, precision=MAXIMUM_PRECISE)
    return (resid + mix_out, attn_out, mix_out)

def reference(tokens, gain_attn, query_key_value_weight, w_out, gain_mix, w_control, w_in, w_back, segments, valid, cotangent):
    stream = tokens.astype(jnp.float32)
    params = tuple((p.astype(jnp.float32) for p in (gain_attn, query_key_value_weight, w_out, gain_mix, w_control, w_in, w_back)))

    def forward(stream, *params):
        outs, attn_out, mix_out = lax.map(jax.checkpoint(partial(one_replica, params)), (stream, segments, valid))
        return (outs, (attn_out, mix_out))
    out_full, pullback, (attn_out, mix_out) = jax.vjp(forward, stream, *params, has_aux=True)
    grads = pullback(cotangent.astype(jnp.float32))
    valid_mask = (valid > 0).astype(jnp.float32)[..., None]
    count = jnp.sum(valid_mask) * D
    stats = jnp.stack([jnp.sqrt(jnp.sum(valid_mask * field * field) / count) for field in (out_full, attn_out, mix_out)])
    return (out_full.astype(jnp.bfloat16), grads[0].astype(jnp.bfloat16), grads[1], grads[2], grads[3], grads[4], grads[5], grads[6], grads[7], stats)
```

```python
import functools
import jax
import jax.numpy as jnp
from jax import lax
from jax.experimental import pallas as pl
from jax.experimental.pallas import tpu as pltpu
from jax.sharding import PartitionSpec as P

HEADS = 8
NEG_FILL = -1e30
MESH = pl.DeviceIdType.MESH
BF = jnp.bfloat16
F32 = jnp.float32
ANY = pl.BlockSpec(memory_space=pl.ANY)
VM = pl.BlockSpec(memory_space=pltpu.VMEM)
VMEM_LIMIT = 60 * 1024 * 1024


def dot(a, b, dims=((1,), (0,))):
    return lax.dot_general(a, b, (dims, ((), ())), preferred_element_type=F32)


def normalized(x):
    center = x - jnp.mean(x, -1, keepdims=True)
    spread = jnp.mean(center * center, -1, keepdims=True)
    rstd = lax.rsqrt(spread + 1e-05)
    return center * rstd, rstd


def ring(n_expert, n_context):
    e = lax.axis_index("expert")
    c = lax.axis_index("context")
    n = n_expert * n_context
    me = e * n_context + c

    def peer(k):
        j = lax.rem(me + k, n)
        pe = lax.div(j, n_context)
        pc = lax.rem(j, n_context)
        return j, pe, pc

    return e, c, me, n, peer


def enter(peer, n):
    barrier = pltpu.get_barrier_semaphore()
    for k in range(1, n):
        _, pe, pc = peer(k)
        pl.semaphore_signal(
            barrier, inc=1, device_id={"expert": pe, "context": pc}, device_id_type=MESH
        )
    pl.semaphore_wait(barrier, n - 1)


def mask_bias(bias, kmark, qmark, s, q0, qn):
    kk = q0 + qn
    place_k = lax.broadcasted_iota(jnp.int32, (kk, qn), 0)
    place_q = lax.broadcasted_iota(jnp.int32, (kk, qn), 1) + q0
    same = kmark[s, pl.ds(0, kk), :] == qmark[s, :, pl.ds(q0, qn)]
    bias[pl.ds(0, kk), :] = jnp.where(same & (place_k <= place_q), 0.0, NEG_FILL)


def forward_kernel(
    tokens, cot, kmark, qmark, gain, wqkv, wout,
    resid_m, cot_m, tok_a, qkv_o, att_o, lse_o, sq_o,
    tok, qkv, att, res, bias,
    tok_s, tok_r, cot_s, cot_r, res_s, res_r, own_s, save_s,
    *, n_expert, n_context,
):
    e, c, me, n, peer = ring(n_expert, n_context)
    seqs, length, width = qkv_o.shape[0], qkv_o.shape[1], tokens.shape[-1]
    half = length // n_context
    slab = half // n_expert
    qn = 256
    enter(peer, n)
    outgoing = []
    for s in range(seqs):
        for k in range(1, n_context):
            pc = lax.rem(c + k, n_context)
            cp = pltpu.make_async_remote_copy(
                src_ref=tokens.at[pc, s], dst_ref=tok.at[s, c],
                send_sem=tok_s.at[s, k], recv_sem=tok_r.at[s, k],
                device_id={"context": pc}, device_id_type=MESH,
            )
            cp.start()
            outgoing.append(cp)
    own = []
    for s in range(seqs):
        cp = pltpu.make_async_copy(tokens.at[c, s], tok.at[s, c], own_s.at[s])
        cp.start()
        own.append(cp)

    def project(s, h):
        x = tok[s, h].astype(F32)
        y, _ = normalized(x)
        a = (y * gain[...]).astype(BF)
        qkv[s, pl.ds(pl.multiple_of(h * half, half), half), :] = dot(a, wqkv[...]).astype(BF)

    for s in range(seqs):
        own[s].wait()
        project(s, c)
    for cp in outgoing:
        cp.wait()
    crossing = []
    for k in range(1, n):
        j, pe, pc = peer(k)
        cp = pltpu.make_async_remote_copy(
            src_ref=cot.at[pc, :, pl.ds(pl.multiple_of(pe * slab, slab), slab), :],
            dst_ref=cot_m.at[pl.ds(e * seqs, seqs), c],
            send_sem=cot_s.at[k], recv_sem=cot_r.at[k],
            device_id={"expert": pe, "context": pc}, device_id_type=MESH,
        )
        cp.start()
        crossing.append(cp)
    local = pltpu.make_async_copy(
        cot.at[c, :, pl.ds(pl.multiple_of(e * slab, slab), slab), :],
        cot_m.at[pl.ds(e * seqs, seqs), c], own_s.at[seqs],
    )
    local.start()
    for k in range(1, n_context):
        for s in range(seqs):
            project(s, lax.rem(c + k, n_context))
    saves = [
        pltpu.make_async_copy(qkv, qkv_o, save_s.at[0]),
        pltpu.make_async_copy(tok, tok_a, save_s.at[1]),
    ]
    for cp in saves:
        cp.start()
    lane = lax.broadcasted_iota(jnp.int32, (qn, 128), 1)
    moving = []
    total = jnp.zeros((1, width), F32)
    for s in range(seqs):
        for qb in range(length // qn):
            kk = (qb + 1) * qn
            rows = pl.ds(qb * qn, qn)
            mask_bias(bias, kmark, qmark, s, qb * qn, qn)

            def pair(hp, _):
                at = pl.multiple_of(hp * 128, 128)
                q2 = qkv[s, rows, pl.ds(at, 128)] * BF(0.125)
                k2 = qkv[s, pl.ds(0, kk), pl.ds(width + at, 128)]
                v2 = qkv[s, pl.ds(0, kk), pl.ds(2 * width + at, 128)]
                outs = []
                for h in range(2):
                    mine = (lane >= 64) if h else (lane < 64)
                    qm = jnp.where(mine, q2, jnp.zeros_like(q2))
                    st = dot(k2, qm, ((1,), (1,))) + bias[pl.ds(0, kk), :]
                    top = jnp.max(st, 0, keepdims=True)
                    p = jnp.exp(st - top)
                    tot = jnp.sum(p, 0, keepdims=True)
                    lse_o[s, pl.ds(2 * hp + h, 1), rows] = top + jnp.log(tot)
                    low = (p * (1.0 / tot)).astype(BF)
                    outs.append(dot(low, v2, ((0,), (0,))))
                att[s, rows, pl.ds(at, 128)] = jnp.where(lane < 64, outs[0], outs[1]).astype(BF)
                return 0

            lax.fori_loop(0, width // 128, pair, 0)
            h = qb * qn // half
            attn_out = dot(att[s, rows, :], wout[...])
            within = qb * qn - h * half
            x = tok[s, h, pl.ds(within, qn), :].astype(F32)
            res[s, h, pl.ds(within, qn), :] = (x + attn_out).astype(BF)
            ok = kmark[s, rows, :] >= 0
            total += jnp.sum(jnp.where(ok, attn_out * attn_out, 0.0), 0, keepdims=True)
            if (qb + 1) * qn == (h + 1) * half:
                for k in range(1, n_expert):
                    pe = lax.rem(e + k, n_expert)
                    cp = pltpu.make_async_remote_copy(
                        src_ref=res.at[s, h, pl.ds(pl.multiple_of(pe * slab, slab), slab), :],
                        dst_ref=resid_m.at[e * seqs + s, h],
                        send_sem=res_s.at[s, h, k], recv_sem=res_r.at[s, h, k],
                        device_id={"expert": pe}, device_id_type=MESH,
                    )
                    cp.start()
                    moving.append(cp)
                cp = pltpu.make_async_copy(
                    res.at[s, h, pl.ds(pl.multiple_of(e * slab, slab), slab), :],
                    resid_m.at[e * seqs + s, h], res_s.at[s, h, 0],
                )
                cp.start()
                moving.append(cp)
    sq_o[...] = total
    keep = pltpu.make_async_copy(att, att_o, save_s.at[2])
    keep.start()
    for cp in saves + moving + crossing + [local, keep]:
        cp.wait()


def forward(tokens, cot, kmark, qmark, gain, wqkv, wout, n_expert, n_context):
    reps, seqs, half, width = tokens.shape
    length = half * n_context
    slab = half // n_expert
    group = seqs * n_expert
    n = n_expert * n_context
    sem = pltpu.SemaphoreType.DMA
    return pl.pallas_call(
        functools.partial(forward_kernel, n_expert=n_expert, n_context=n_context),
        out_shape=(
            jax.ShapeDtypeStruct((group, n_context, slab, width), BF),
            jax.ShapeDtypeStruct((group, n_context, slab, width), BF),
            jax.ShapeDtypeStruct((seqs, n_context, half, width), BF),
            jax.ShapeDtypeStruct((seqs, length, 3 * width), BF),
            jax.ShapeDtypeStruct((seqs, length, width), BF),
            jax.ShapeDtypeStruct((seqs, HEADS, length), F32),
            jax.ShapeDtypeStruct((1, width), F32),
        ),
        in_specs=[ANY, ANY, VM, VM, VM, VM, VM],
        out_specs=(ANY, ANY, ANY, ANY, ANY, VM, VM),
        scratch_shapes=[
            pltpu.VMEM((seqs, n_context, half, width), BF),
            pltpu.VMEM((seqs, length, 3 * width), BF),
            pltpu.VMEM((seqs, length, width), BF),
            pltpu.VMEM((seqs, n_context, half, width), BF),
            pltpu.VMEM((length, 256), F32),
            sem((seqs, n_context)), sem((seqs, n_context)),
            sem((n,)), sem((n,)),
            sem((seqs, n_context, n_expert)), sem((seqs, n_context, n_expert)),
            sem((seqs + 1,)), sem((3,)),
        ],
        compiler_params=pltpu.CompilerParams(
            collective_id=0, has_side_effects=True, vmem_limit_bytes=VMEM_LIMIT
        ),
        name="attend_forward",
    )(tokens, cot, kmark, qmark, gain, wqkv, wout)


def mix_phase(resid_low, cot, valid_m, gain_mix, w_control, w_in1, w_back1, n_expert, n_context):
    group, halves, slab, width = resid_low.shape
    n = n_expert * n_context
    rows = halves * slab
    resid = resid_low.reshape(group, rows, width).astype(F32)
    cot = cot.reshape(group, rows, width)
    here = valid_m.reshape(group, rows) > 0
    normed, norm_back = jax.vjp(lambda r, g: normalized(r)[0] * g, resid, gain_mix)
    u = normed.astype(BF)
    logits = jnp.einsum("spd,de->spe", u, w_control, preferred_element_type=F32)
    masked = jnp.where(here[..., None], logits, NEG_FILL)
    weights = jax.nn.softmax(masked, 0)
    low = weights.astype(BF)

    def to_owner(x):
        return lax.all_to_all(x, ("expert", "context"), 0, 0)

    mixed = to_owner(jnp.einsum("spe,spd->epd", low, u, preferred_element_type=F32).astype(BF))
    dexp = to_owner(jnp.einsum("spe,spd->epd", low, cot, preferred_element_type=F32).astype(BF))
    x = mixed.reshape(n * rows, width)
    de = dexp.reshape(n * rows, width)
    pre = dot(x, w_in1)
    act, gelu_back = jax.vjp(jax.nn.gelu, pre)
    act = act.astype(BF)
    eo = dot(act, w_back1).astype(BF)
    grad_back = dot(act, de, ((0,), (0,)))
    d_pre = gelu_back(dot(de, w_back1, ((1,), (1,))))[0].astype(BF)
    grad_in = dot(x, d_pre, ((0,), (0,)))
    dm = dot(d_pre, w_in1, ((1,), (1,))).astype(BF)
    eo = to_owner(eo.reshape(n, rows, width))
    dm = to_owner(dm.reshape(n, rows, width))
    mix_out = jnp.einsum("spe,epd->spd", low, eo, preferred_element_type=F32)
    out_full = resid + mix_out
    d_w = jnp.einsum("spd,epd->spe", cot, eo, preferred_element_type=F32) + jnp.einsum(
        "spd,epd->spe", u, dm, preferred_element_type=F32
    )
    d_logits = (weights * (d_w - jnp.sum(weights * d_w, 0))).astype(BF)
    grad_control = jnp.einsum("spd,spe->de", u, d_logits, preferred_element_type=F32)
    d_u = jnp.einsum("spe,de->spd", d_logits, w_control, preferred_element_type=F32) + jnp.einsum(
        "spe,epd->spd", low, dm, preferred_element_type=F32
    )
    d_norm, grad_gain_mix = norm_back(d_u)
    d_attn = (cot.astype(F32) + d_norm).astype(BF)
    okf = here.astype(F32)[..., None]
    sums = jnp.stack([jnp.sum(okf * out_full * out_full), jnp.sum(okf * mix_out * mix_out), jnp.sum(okf)])
    shape = (group, halves, slab, width)
    return d_attn.reshape(shape), out_full.astype(BF).reshape(shape), grad_in, grad_back, grad_control, grad_gain_mix, sums


def back_phase(d_attn, tok_a, qkv, att, lse, kmark, qmark, gain, wqkv, wout):
    seqs, length, width = d_attn.shape
    x = tok_a.astype(F32)
    normed, norm_back = jax.vjp(lambda r, g: normalized(r)[0] * g, x, gain)
    a = normed.astype(BF)
    grad_out = jnp.einsum("sld,sle->de", att, d_attn, preferred_element_type=F32)
    d_att = jnp.einsum("sle,de->sld", d_attn, wout, preferred_element_type=F32).astype(BF)

    def one(pack):
        qkv, d_att, lse, km, qm = pack
        q, k, v = (t.reshape(length, HEADS, -1) for t in jnp.split(qkv, 3, -1))
        do = d_att.reshape(length, HEADS, -1)
        i = jnp.arange(length)
        ok = (i[:, None] >= i[None, :]) & (km.T == qm.T)
        s = jnp.where(ok[None], jnp.einsum("qhd,khd->hqk", q, k, preferred_element_type=F32) * 0.125, NEG_FILL)
        p = jnp.exp(s - lse[..., None])
        dp = jnp.einsum("qhd,khd->hqk", do, v, preferred_element_type=F32)
        ds = (p * (dp - jnp.sum(p * dp, -1, keepdims=True))).astype(BF)
        dq = jnp.einsum("hqk,khd->qhd", ds, k, preferred_element_type=F32) * 0.125
        dk = jnp.einsum("hqk,qhd->khd", ds, q, preferred_element_type=F32) * 0.125
        dv = jnp.einsum("hqk,qhd->khd", p.astype(BF), do, preferred_element_type=F32)
        return jnp.concatenate([t.reshape(length, width) for t in (dq, dk, dv)], -1).astype(BF)

    d_qkv = lax.map(one, (qkv, d_att, lse, kmark, qmark))
    grad_qkv = jnp.einsum("sld,slc->dc", a, d_qkv, preferred_element_type=F32)
    d_a = jnp.einsum("slc,dc->sld", d_qkv, wqkv, preferred_element_type=F32)
    d_norm, grad_gain = norm_back(d_a)
    return (d_attn.astype(F32) + d_norm).astype(BF), grad_qkv, grad_out, grad_gain


def per_device(n_expert, n_context, tokens, gain_attn, wqkv, w_out, gain_mix, w_control, w_in, w_back, segments, valid, cotangent):
    reps, seqs, half, width = tokens.shape
    length = half * n_context
    slab = half // n_expert
    group = seqs * n_expert
    e, c = lax.axis_index("expert"), lax.axis_index("context")

    def pick(x, i, axis=0):
        return lax.dynamic_index_in_dim(x, i, axis, keepdims=False)

    seg_a, valid_a = pick(segments, c), pick(valid, c)
    kmark = jnp.where(valid_a > 0, seg_a, -1)[:, :, None]
    qmark = seg_a[:, None, :]
    valid_all = pick(lax.all_gather(valid, "expert"), c, 1).reshape(group, n_context, n_expert, slab)
    valid_m = pick(valid_all, e, 2)
    resid_m, cot_m, tok_a, qkv, att, lse, sq = forward(
        tokens, cotangent, kmark, qmark, gain_attn[None], wqkv, w_out, n_expert, n_context
    )
    d_attn_m, out_m, grad_in, grad_back, grad_control, grad_gain_mix, sums = mix_phase(
        resid_m, cot_m, valid_m, gain_mix, w_control, pick(w_in, c), pick(w_back, c), n_expert, n_context
    )
    d_attn = lax.all_to_all(d_attn_m, "expert", 0, 2, tiled=True).reshape(seqs, length, width)

    def home(x):
        x = x.reshape(n_expert, seqs, n_context, slab, width).transpose(0, 2, 1, 3, 4)
        x = x.reshape(n_expert * n_context, seqs, slab, width)
        x = lax.all_to_all(x, ("expert", "context"), 0, 0).reshape(n_expert, n_context, seqs, slab, width)
        return x.transpose(1, 2, 0, 3, 4).reshape(reps, seqs, half, width)

    output = home(out_m)
    d_tok, grad_qkv, grad_out, grad_gain = back_phase(
        d_attn, tok_a.reshape(seqs, length, width), qkv, att, lse, kmark, qmark, gain_attn, wqkv, w_out
    )
    d_tok = d_tok.reshape(seqs, n_context, half, width).transpose(1, 0, 2, 3)
    d_tokens = lax.all_to_all(d_tok, "context", 0, 0)

    def whole(g):
        g = lax.psum(g.astype(BF), "dp")
        return lax.all_gather(g, "context").astype(F32)

    squares = jnp.stack([sums[0], jnp.sum(sq), sums[1], sums[2]])
    grad_gain, grad_qkv, grad_out, grad_gain_mix, grad_control, squares = lax.psum(
        (grad_gain, grad_qkv, grad_out, grad_gain_mix, grad_control, squares), ("expert", "context", "dp")
    )
    stats = jnp.sqrt(squares[:3] / (squares[3] * width))
    return (
        output, d_tokens, grad_gain, grad_qkv, grad_out, grad_gain_mix, grad_control,
        whole(grad_in), whole(grad_back), stats,
    )


def solution(mesh):
    shards = P("dp", "expert", "context", None)
    rows = P("dp", "expert", None)
    experts = P("expert", None, None)
    return jax.shard_map(
        functools.partial(per_device, mesh.shape["expert"], mesh.shape["context"]),
        mesh=mesh,
        in_specs=(shards, P(), P(), P(), P(), P(), experts, experts, rows, rows, shards),
        out_specs=(shards, shards, P(), P(), P(), P(), P(), experts, experts, P()),
        check_vma=False,
    )
```

```python
import functools
import jax
import jax.numpy as jnp
from jax import lax
from jax.experimental import pallas as pl
from jax.experimental.pallas import tpu as pltpu
from jax.sharding import PartitionSpec as P

HEADS = 8
NEG_FILL = -1e30
MESH = pl.DeviceIdType.MESH
BF = jnp.bfloat16
F32 = jnp.float32
ANY = pl.BlockSpec(memory_space=pl.ANY)
VM = pl.BlockSpec(memory_space=pltpu.VMEM)
VMEM_LIMIT = 60 * 1024 * 1024


def dot(a, b, dims=((1,), (0,))):
    return lax.dot_general(a, b, (dims, ((), ())), preferred_element_type=F32)


def normalized(x):
    center = x - jnp.mean(x, -1, keepdims=True)
    spread = jnp.mean(center * center, -1, keepdims=True)
    rstd = lax.rsqrt(spread + 1e-05)
    return center * rstd, rstd


def ring(n_expert, n_context):
    e = lax.axis_index("expert")
    c = lax.axis_index("context")
    n = n_expert * n_context
    me = e * n_context + c

    def peer(k):
        j = lax.rem(me + k, n)
        pe = lax.div(j, n_context)
        pc = lax.rem(j, n_context)
        return j, pe, pc

    return e, c, me, n, peer


def enter(peer, n):
    barrier = pltpu.get_barrier_semaphore()
    for k in range(1, n):
        _, pe, pc = peer(k)
        pl.semaphore_signal(
            barrier, inc=1, device_id={"expert": pe, "context": pc}, device_id_type=MESH
        )
    pl.semaphore_wait(barrier, n - 1)


def mask_bias(bias, kmark, qmark, s, q0, qn):
    kk = q0 + qn
    place_k = lax.broadcasted_iota(jnp.int32, (kk, qn), 0)
    place_q = lax.broadcasted_iota(jnp.int32, (kk, qn), 1) + q0
    same = kmark[s, pl.ds(0, kk), :] == qmark[s, :, pl.ds(q0, qn)]
    bias[pl.ds(0, kk), :] = jnp.where(same & (place_k <= place_q), 0.0, NEG_FILL)


def forward_kernel(
    tokens, cot, kmark, qmark, gain, wqkv, wout,
    resid_m, cot_m, tok_a, qkv_o, att_o, lse_o, sq_o,
    tok, qkv, att, res, bias,
    tok_s, tok_r, cot_s, cot_r, res_s, res_r, own_s, save_s,
    *, n_expert, n_context,
):
    e, c, me, n, peer = ring(n_expert, n_context)
    seqs, length, width = qkv_o.shape[0], qkv_o.shape[1], tokens.shape[-1]
    half = length // n_context
    slab = half // n_expert
    qn = 256
    enter(peer, n)
    outgoing = []
    for s in range(seqs):
        for k in range(1, n_context):
            pc = lax.rem(c + k, n_context)
            cp = pltpu.make_async_remote_copy(
                src_ref=tokens.at[pc, s], dst_ref=tok.at[s, c],
                send_sem=tok_s.at[s, k], recv_sem=tok_r.at[s, k],
                device_id={"context": pc}, device_id_type=MESH,
            )
            cp.start()
            outgoing.append(cp)
    own = []
    for s in range(seqs):
        cp = pltpu.make_async_copy(tokens.at[c, s], tok.at[s, c], own_s.at[s])
        cp.start()
        own.append(cp)

    def project(s, h):
        x = tok[s, h].astype(F32)
        y, _ = normalized(x)
        a = (y * gain[...]).astype(BF)
        qkv[s, pl.ds(pl.multiple_of(h * half, half), half), :] = dot(a, wqkv[...]).astype(BF)

    for s in range(seqs):
        own[s].wait()
        project(s, c)
    for cp in outgoing:
        cp.wait()
    crossing = []
    for k in range(1, n):
        j, pe, pc = peer(k)
        cp = pltpu.make_async_remote_copy(
            src_ref=cot.at[pc, :, pl.ds(pl.multiple_of(pe * slab, slab), slab), :],
            dst_ref=cot_m.at[pl.ds(e * seqs, seqs), c],
            send_sem=cot_s.at[k], recv_sem=cot_r.at[k],
            device_id={"expert": pe, "context": pc}, device_id_type=MESH,
        )
        cp.start()
        crossing.append(cp)
    local = pltpu.make_async_copy(
        cot.at[c, :, pl.ds(pl.multiple_of(e * slab, slab), slab), :],
        cot_m.at[pl.ds(e * seqs, seqs), c], own_s.at[seqs],
    )
    local.start()
    for k in range(1, n_context):
        for s in range(seqs):
            project(s, lax.rem(c + k, n_context))
    saves = [
        pltpu.make_async_copy(qkv, qkv_o, save_s.at[0]),
        pltpu.make_async_copy(tok, tok_a, save_s.at[1]),
    ]
    for cp in saves:
        cp.start()
    lane = lax.broadcasted_iota(jnp.int32, (qn, 128), 1)
    moving = []
    total = jnp.zeros((1, width), F32)
    for s in range(seqs):
        for qb in range(length // qn):
            kk = (qb + 1) * qn
            rows = pl.ds(qb * qn, qn)
            mask_bias(bias, kmark, qmark, s, qb * qn, qn)

            def pair(hp, _):
                at = pl.multiple_of(hp * 128, 128)
                q2 = qkv[s, rows, pl.ds(at, 128)] * BF(0.125)
                k2 = qkv[s, pl.ds(0, kk), pl.ds(width + at, 128)]
                v2 = qkv[s, pl.ds(0, kk), pl.ds(2 * width + at, 128)]
                outs = []
                for h in range(2):
                    mine = (lane >= 64) if h else (lane < 64)
                    qm = jnp.where(mine, q2, jnp.zeros_like(q2))
                    st = dot(k2, qm, ((1,), (1,))) + bias[pl.ds(0, kk), :]
                    top = jnp.max(st, 0, keepdims=True)
                    p = jnp.exp(st - top)
                    tot = jnp.sum(p, 0, keepdims=True)
                    lse_o[s, pl.ds(2 * hp + h, 1), rows] = top + jnp.log(tot)
                    low = (p * (1.0 / tot)).astype(BF)
                    outs.append(dot(low, v2, ((0,), (0,))))
                att[s, rows, pl.ds(at, 128)] = jnp.where(lane < 64, outs[0], outs[1]).astype(BF)
                return 0

            lax.fori_loop(0, width // 128, pair, 0)
            h = qb * qn // half
            attn_out = dot(att[s, rows, :], wout[...])
            within = qb * qn - h * half
            x = tok[s, h, pl.ds(within, qn), :].astype(F32)
            res[s, h, pl.ds(within, qn), :] = (x + attn_out).astype(BF)
            ok = kmark[s, rows, :] >= 0
            total += jnp.sum(jnp.where(ok, attn_out * attn_out, 0.0), 0, keepdims=True)
            if (qb + 1) * qn == (h + 1) * half:
                for k in range(1, n_expert):
                    pe = lax.rem(e + k, n_expert)
                    cp = pltpu.make_async_remote_copy(
                        src_ref=res.at[s, h, pl.ds(pl.multiple_of(pe * slab, slab), slab), :],
                        dst_ref=resid_m.at[e * seqs + s, h],
                        send_sem=res_s.at[s, h, k], recv_sem=res_r.at[s, h, k],
                        device_id={"expert": pe}, device_id_type=MESH,
                    )
                    cp.start()
                    moving.append(cp)
                cp = pltpu.make_async_copy(
                    res.at[s, h, pl.ds(pl.multiple_of(e * slab, slab), slab), :],
                    resid_m.at[e * seqs + s, h], res_s.at[s, h, 0],
                )
                cp.start()
                moving.append(cp)
    sq_o[...] = total
    keep = pltpu.make_async_copy(att, att_o, save_s.at[2])
    keep.start()
    for cp in saves + moving + crossing + [local, keep]:
        cp.wait()


def forward(tokens, cot, kmark, qmark, gain, wqkv, wout, n_expert, n_context):
    reps, seqs, half, width = tokens.shape
    length = half * n_context
    slab = half // n_expert
    group = seqs * n_expert
    n = n_expert * n_context
    sem = pltpu.SemaphoreType.DMA
    return pl.pallas_call(
        functools.partial(forward_kernel, n_expert=n_expert, n_context=n_context),
        out_shape=(
            jax.ShapeDtypeStruct((group, n_context, slab, width), BF),
            jax.ShapeDtypeStruct((group, n_context, slab, width), BF),
            jax.ShapeDtypeStruct((seqs, n_context, half, width), BF),
            jax.ShapeDtypeStruct((seqs, length, 3 * width), BF),
            jax.ShapeDtypeStruct((seqs, length, width), BF),
            jax.ShapeDtypeStruct((seqs, HEADS, length), F32),
            jax.ShapeDtypeStruct((1, width), F32),
        ),
        in_specs=[ANY, ANY, VM, VM, VM, VM, VM],
        out_specs=(ANY, ANY, ANY, ANY, ANY, VM, VM),
        scratch_shapes=[
            pltpu.VMEM((seqs, n_context, half, width), BF),
            pltpu.VMEM((seqs, length, 3 * width), BF),
            pltpu.VMEM((seqs, length, width), BF),
            pltpu.VMEM((seqs, n_context, half, width), BF),
            pltpu.VMEM((length, 256), F32),
            sem((seqs, n_context)), sem((seqs, n_context)),
            sem((n,)), sem((n,)),
            sem((seqs, n_context, n_expert)), sem((seqs, n_context, n_expert)),
            sem((seqs + 1,)), sem((3,)),
        ],
        compiler_params=pltpu.CompilerParams(
            collective_id=0, has_side_effects=True, vmem_limit_bytes=VMEM_LIMIT
        ),
        name="attend_forward",
    )(tokens, cot, kmark, qmark, gain, wqkv, wout)


def mix_kernel(
    resid_m, cot_m, ok_m, gain, wc, w_in, w_back,
    d_attn, out_m, gi_o, gb_o, gc_o, gm_o, sq_o,
    res, cot, u, wts, big, mixed, dexp, xs, des, eos, dms, eor, dmr, win, wback, gi, gbt, dat, out, glow,
    go_s, go_r, back_s, back_r, at_s, at_r, in_s, save_s,
    *, n_expert, n_context,
):
    e, c, me, n, peer = ring(n_expert, n_context)
    group, halves, slab, width = res.shape
    seqs = group // n_expert
    ff = win.shape[1]
    experts = n
    span = max(16, 256 // group)
    steps = slab // span
    chunk = 512 // slab
    loads = [
        pltpu.make_async_copy(resid_m, res, in_s.at[0]),
        pltpu.make_async_copy(cot_m, cot, in_s.at[1]),
        pltpu.make_async_copy(w_in.at[c], win, in_s.at[2]),
        pltpu.make_async_copy(w_back.at[c], wback, in_s.at[3]),
    ]
    for cp in loads:
        cp.start()
    enter(peer, n)
    rows, cols = group * span, experts * span
    spread = (
        lax.broadcasted_iota(jnp.int32, (experts, cols), 1) // span
        == lax.broadcasted_iota(jnp.int32, (experts, cols), 0)
    ).astype(BF)
    gather = (
        lax.broadcasted_iota(jnp.int32, (cols, experts), 0) // span
        == lax.broadcasted_iota(jnp.int32, (cols, experts), 1)
    ).astype(BF)
    diag = lax.rem(lax.broadcasted_iota(jnp.int32, (rows, cols), 0), span) == lax.rem(
        lax.broadcasted_iota(jnp.int32, (rows, cols), 1), span
    )
    loads[0].wait()
    loads[1].wait()
    sent = []
    for h in range(halves):

        def first(g, _):
            at = pl.ds(pl.multiple_of(g * span, span), span)
            r = res[:, h, at, :].reshape(rows, width).astype(F32)
            normed, _ = normalized(r)
            ug = (normed * gain[...]).astype(BF)
            u[:, h, at, :] = ug.reshape(group, span, width)
            ok = ok_m[:, h, at, :].reshape(rows, 1)
            logits = jnp.where(ok > 0, dot(ug, wc[...]), NEG_FILL).reshape(group, span, experts)
            ex = jnp.exp(logits - jnp.max(logits, 0, keepdims=True))
            w = (ex / jnp.sum(ex, 0, keepdims=True)).reshape(rows, experts)
            wts[h * steps + g] = w
            wide = jnp.where(diag, dot(w.astype(BF), spread), 0.0).astype(BF)
            big[h * steps + g] = wide
            cg = cot[:, h, at, :].reshape(rows, width)
            mixed[h, :, at, :] = dot(wide, ug, ((0,), (0,))).astype(BF).reshape(experts, span, width)
            dexp[h, :, at, :] = dot(wide, cg, ((0,), (0,))).astype(BF).reshape(experts, span, width)
            return 0

        lax.fori_loop(0, steps, first, 0)
        for i, (src, dst) in enumerate(((mixed, xs), (dexp, des))):
            dst[h, 0] = src[h, me]
            for k in range(1, n):
                j, pe, pc = peer(k)
                cp = pltpu.make_async_remote_copy(
                    src_ref=src.at[h, j], dst_ref=dst.at[h, k],
                    send_sem=go_s.at[i, h, k], recv_sem=go_r.at[i, h, k],
                    device_id={"expert": pe, "context": pc}, device_id_type=MESH,
                )
                cp.start()
                sent.append((i, h, k, cp))
    loads[2].wait()
    loads[3].wait()
    tile = 512
    gi[...] = jnp.zeros_like(gi)
    gbt[...] = jnp.zeros_like(gbt)
    returned = []
    for h in range(halves):
        for kg in range(n // chunk):
            slots = range(kg * chunk, (kg + 1) * chunk)
            for i, hh, k, cp in sent:
                if hh == h and k in slots:
                    cp.wait_recv()
            x = xs[h, pl.ds(kg * chunk, chunk)].reshape(chunk * slab, width)
            de = des[h, pl.ds(kg * chunk, chunk)].reshape(chunk * slab, width)
            xt, det = x.T, de.T

            def expert_tile(f, carry):
                eo, dm = carry
                at = pl.ds(pl.multiple_of(f * tile, tile), tile)
                pre = dot(x, win[:, at])
                sq = pre * pre
                t = jnp.tanh(0.7978845608028654 * pre * (1.0 + 0.044715 * sq))
                act = (0.5 * pre * (1.0 + t)).astype(BF)
                slope = 0.5 * (1.0 + t) + 0.5 * pre * (1.0 - t * t) * (
                    0.7978845608028654 * (1.0 + 3 * 0.044715 * sq)
                )
                d_pre = (slope * dot(de, wback[at, :], ((1,), (1,)))).astype(BF)
                gbt[:, at] += dot(det, act)
                gi[:, at] += dot(xt, d_pre)
                return eo + dot(act, wback[at, :]), dm + dot(d_pre, win[:, at], ((1,), (1,)))

            zero = jnp.zeros((chunk * slab, width), F32)
            eo, dm = lax.fori_loop(0, ff // tile, expert_tile, (zero, zero))
            eos[h, pl.ds(kg * chunk, chunk)] = eo.astype(BF).reshape(chunk, slab, width)
            dms[h, pl.ds(kg * chunk, chunk)] = dm.astype(BF).reshape(chunk, slab, width)
            for i, (src, dst) in enumerate(((eos, eor), (dms, dmr))):
                for k in slots:
                    if k == 0:
                        dst[h, me] = src[h, 0]
                        continue
                    j, pe, pc = peer(n - k)
                    cp = pltpu.make_async_remote_copy(
                        src_ref=src.at[h, k], dst_ref=dst.at[h, me],
                        send_sem=back_s.at[i, h, k], recv_sem=back_r.at[i, h, k],
                        device_id={"expert": pe, "context": pc}, device_id_type=MESH,
                    )
                    cp.start()
                    returned.append((i, h, k, cp))
    glow[0] = gi[...].astype(BF)
    keep = [pltpu.make_async_copy(glow.at[0], gi_o, save_s.at[0])]
    keep[0].start()
    for f in range(ff // tile):
        glow[1, :, pl.ds(f * tile, tile)] = gbt[:, pl.ds(f * tile, tile)].astype(BF)
    keep.append(pltpu.make_async_copy(glow.at[1], gb_o, save_s.at[1]))
    keep[1].start()
    gc_o[...] = jnp.zeros_like(gc_o)
    gm_o[...] = jnp.zeros_like(gm_o)
    sq_o[...] = jnp.zeros_like(sq_o)
    moving = []
    for h in range(halves):
        for i, hh, k, cp in returned:
            if hh == h:
                cp.wait_recv()

        def second(g, _):
            at = pl.ds(pl.multiple_of(g * span, span), span)
            r = res[:, h, at, :].reshape(rows, width).astype(F32)
            normed, rstd = normalized(r)
            ug = u[:, h, at, :].reshape(rows, width)
            cg = cot[:, h, at, :].reshape(rows, width)
            ok = ok_m[:, h, at, :].reshape(rows, 1) > 0
            eg = eor[h, :, at, :].reshape(cols, width)
            dg = dmr[h, :, at, :].reshape(cols, width)
            wide = big[h * steps + g]
            w = wts[h * steps + g]
            mix = dot(wide, eg)
            full = r + mix
            out[:, h, at, :] = full.astype(BF).reshape(group, span, width)
            sq_o[pl.ds(0, 1), :] += jnp.sum(jnp.where(ok, full * full, 0.0), 0, keepdims=True)
            sq_o[pl.ds(1, 1), :] += jnp.sum(jnp.where(ok, mix * mix, 0.0), 0, keepdims=True)
            dw = jnp.where(diag, dot(cg, eg, ((1,), (1,))) + dot(ug, dg, ((1,), (1,))), 0.0)
            high = dw.astype(BF)
            rest = (dw - high.astype(F32)).astype(BF)
            dw = dot(high, gather) + dot(rest, gather)
            inner = jnp.sum((w * dw).reshape(group, span, experts), 0, keepdims=True)
            d_log = (
                (w.reshape(group, span, experts) * (dw.reshape(group, span, experts) - inner))
                .reshape(rows, experts)
                .astype(BF)
            )
            gc_o[...] += dot(ug, d_log, ((0,), (0,)))
            d_u = dot(d_log, wc[...], ((1,), (1,))) + dot(wide, dg)
            gm_o[...] += jnp.sum(d_u * normed, 0, keepdims=True)
            q = d_u * gain[...]
            d_res = cg.astype(F32) + rstd * (
                q - jnp.mean(q, -1, keepdims=True) - normed * jnp.mean(q * normed, -1, keepdims=True)
            )
            dat[:, h, at, :] = d_res.astype(BF).reshape(group, span, width)
            return 0

        lax.fori_loop(0, steps, second, 0)
        mine = pl.ds(pl.multiple_of(e * slab, slab), slab)
        for k in range(1, n_expert):
            pe = lax.rem(e + k, n_expert)
            cp = pltpu.make_async_remote_copy(
                src_ref=dat.at[pl.ds(pe * seqs, seqs), h], dst_ref=d_attn.at[:, h, mine, :],
                send_sem=at_s.at[h, k], recv_sem=at_r.at[h, k],
                device_id={"expert": pe}, device_id_type=MESH,
            )
            cp.start()
            moving.append(cp)
        cp = pltpu.make_async_copy(
            dat.at[pl.ds(e * seqs, seqs), h], d_attn.at[:, h, mine, :], at_s.at[h, 0]
        )
        cp.start()
        moving.append(cp)
    cp = pltpu.make_async_copy(out, out_m, save_s.at[2])
    cp.start()
    for _, _, _, sending in sent + returned:
        sending.wait_send()
    for cp in moving + keep + [cp]:
        cp.wait()


def mix(resid_m, cot_m, ok_m, gain, wc, w_in, w_back, n_expert, n_context):
    group, halves, slab, width = resid_m.shape
    seqs = group // n_expert
    n = n_expert * n_context
    ff = w_in.shape[-1]
    span = max(16, 256 // group)
    steps = slab // span
    sem = pltpu.SemaphoreType.DMA
    block = pltpu.VMEM((group, halves, slab, width), BF)
    turned = pltpu.VMEM((halves, n, slab, width), BF)
    return pl.pallas_call(
        functools.partial(mix_kernel, n_expert=n_expert, n_context=n_context),
        out_shape=(
            jax.ShapeDtypeStruct((seqs, halves, slab * n_expert, width), BF),
            jax.ShapeDtypeStruct((group, halves, slab, width), BF),
            jax.ShapeDtypeStruct((width, ff), BF),
            jax.ShapeDtypeStruct((width, ff), BF),
            jax.ShapeDtypeStruct((width, n), F32),
            jax.ShapeDtypeStruct((1, width), F32),
            jax.ShapeDtypeStruct((2, width), F32),
        ),
        in_specs=[ANY, ANY, VM, VM, VM, ANY, ANY],
        out_specs=(ANY, ANY, ANY, ANY, VM, VM, VM),
        scratch_shapes=[
            block, block, block,
            pltpu.VMEM((halves * steps, group * span, n), F32),
            pltpu.VMEM((halves * steps, group * span, n * span), BF),
            turned, turned, turned, turned, turned, turned, turned, turned,
            pltpu.VMEM((width, ff), BF), pltpu.VMEM((ff, width), BF),
            pltpu.VMEM((width, ff), F32), pltpu.VMEM((width, ff), F32),
            block, block, pltpu.VMEM((2, width, ff), BF),
            sem((2, halves, n)), sem((2, halves, n)),
            sem((2, halves, n)), sem((2, halves, n)),
            sem((halves, n_expert)), sem((halves, n_expert)),
            sem((4,)), sem((3,)),
        ],
        compiler_params=pltpu.CompilerParams(
            collective_id=1, has_side_effects=True, vmem_limit_bytes=VMEM_LIMIT
        ),
        name="mix_and_experts",
    )(resid_m, cot_m, ok_m, gain, wc, w_in, w_back)


def backward_kernel(
    d_attn, tok_a, qkv_a, att_a, lse, kmark, qmark, gain, wqkv, wout, out_m,
    dtok_o, out_o, gq_o, go_o, gg_o,
    da, tok, qkv, att, datt, dkv, dqkv, dtok, bias,
    out_s, out_r, tok_s, tok_r, in_s, own_s,
    *, n_expert, n_context,
):
    e, c, me, n, peer = ring(n_expert, n_context)
    seqs, length, width = da.shape
    half = length // n_context
    slab = half // n_expert
    qn = 256
    loads = [
        pltpu.make_async_copy(src, dst, in_s.at[i])
        for i, (src, dst) in enumerate(((d_attn, da), (att_a, att), (qkv_a, qkv), (tok_a, tok)))
    ]
    for cp in loads:
        cp.start()
    enter(peer, n)
    crossing = []
    mine = pl.ds(pl.multiple_of(e * slab, slab), slab)
    for k in range(1, n):
        j, pe, pc = peer(k)
        cp = pltpu.make_async_remote_copy(
            src_ref=out_m.at[pl.ds(pe * seqs, seqs), pc], dst_ref=out_o.at[c, :, mine, :],
            send_sem=out_s.at[k], recv_sem=out_r.at[k],
            device_id={"expert": pe, "context": pc}, device_id_type=MESH,
        )
        cp.start()
        crossing.append(cp)
    cp = pltpu.make_async_copy(
        out_m.at[pl.ds(e * seqs, seqs), c], out_o.at[c, :, mine, :], own_s.at[0, 0]
    )
    cp.start()
    crossing.append(cp)
    lane = lax.broadcasted_iota(jnp.int32, (qn, 128), 1)
    gg_o[...] = jnp.zeros_like(gg_o)
    for i in range(4):
        loads[i].wait()
    for s in range(seqs):
        datt[...] = dot(da[s], wout[...], ((1,), (1,))).astype(BF)
        go = dot(att[s], da[s], ((0,), (0,)))
        go_o[...] = go if s == 0 else go_o[...] + go
        dkv[...] = jnp.zeros_like(dkv)
        for qb in range(length // qn):
            kk = (qb + 1) * qn
            rows = pl.ds(qb * qn, qn)
            mask_bias(bias, kmark, qmark, s, qb * qn, qn)

            def pair(hp, _):
                at = pl.multiple_of(hp * 128, 128)
                q2 = qkv[s, rows, pl.ds(at, 128)] * BF(0.125)
                k2 = qkv[s, pl.ds(0, kk), pl.ds(width + at, 128)]
                v2 = qkv[s, pl.ds(0, kk), pl.ds(2 * width + at, 128)]
                do2 = datt[rows, pl.ds(at, 128)]
                dqs, dss, lows, qms, doms = [], [], [], [], []
                for h in range(2):
                    mine = (lane >= 64) if h else (lane < 64)
                    qm = jnp.where(mine, q2, jnp.zeros_like(q2))
                    dom = jnp.where(mine, do2, jnp.zeros_like(do2))
                    st = dot(k2, qm, ((1,), (1,))) + bias[pl.ds(0, kk), :]
                    p = jnp.exp(st - lse[s, pl.ds(2 * hp + h, 1), rows])
                    dp = dot(v2, dom, ((1,), (1,)))
                    delta = jnp.sum(p * dp, 0, keepdims=True)
                    ds = (p * (dp - delta)).astype(BF)
                    dqs.append(dot(ds, k2, ((0,), (0,))))
                    dss.append(ds)
                    lows.append(p.astype(BF))
                    qms.append(qm)
                    doms.append(dom)
                dqkv[rows, pl.ds(at, 128)] = (jnp.where(lane < 64, dqs[0], dqs[1]) * 0.125).astype(BF)
                dkv[pl.ds(0, kk), pl.ds(at, 128)] += dot(dss[0], qms[0]) + dot(dss[1], qms[1])
                dkv[pl.ds(0, kk), pl.ds(width + at, 128)] += dot(lows[0], doms[0]) + dot(
                    lows[1], doms[1]
                )
                return 0

            lax.fori_loop(0, width // 128, pair, 0)
        dqkv[:, pl.ds(width, 2 * width)] = dkv[...].astype(BF)
        for h in range(n_context):
            rows = pl.ds(h * half, half)
            normed, rstd = normalized(tok[s, h].astype(F32))
            a = (normed * gain[...]).astype(BF)
            gq = dot(a, dqkv[rows, :], ((0,), (0,)))
            gq_o[...] = gq if s == 0 and h == 0 else gq_o[...] + gq
            d_a = dot(dqkv[rows, :], wqkv[...], ((1,), (1,)))
            gg_o[...] += jnp.sum(d_a * normed, 0, keepdims=True)
            q = d_a * gain[...]
            dt = da[s, rows, :].astype(F32) + rstd * (
                q - jnp.mean(q, -1, keepdims=True) - normed * jnp.mean(q * normed, -1, keepdims=True)
            )
            dtok[s, h] = dt.astype(BF)
        for k in range(1, n_context):
            pc = lax.rem(c + k, n_context)
            cp = pltpu.make_async_remote_copy(
                src_ref=dtok.at[s, pc], dst_ref=dtok_o.at[c, s],
                send_sem=tok_s.at[s, k], recv_sem=tok_r.at[s, k],
                device_id={"context": pc}, device_id_type=MESH,
            )
            cp.start()
            crossing.append(cp)
        cp = pltpu.make_async_copy(dtok.at[s, c], dtok_o.at[c, s], own_s.at[1, s])
        cp.start()
        crossing.append(cp)
    for cp in crossing:
        cp.wait()


def backward(d_attn, tok_a, qkv, att, lse, kmark, qmark, gain, wqkv, wout, out_m, n_expert, n_context):
    seqs, length, width = d_attn.shape
    half = length // n_context
    n = n_expert * n_context
    sem = pltpu.SemaphoreType.DMA
    return pl.pallas_call(
        functools.partial(backward_kernel, n_expert=n_expert, n_context=n_context),
        out_shape=(
            jax.ShapeDtypeStruct((n_context, seqs, half, width), BF),
            jax.ShapeDtypeStruct((n_context, seqs, half, width), BF),
            jax.ShapeDtypeStruct((width, 3 * width), F32),
            jax.ShapeDtypeStruct((width, width), F32),
            jax.ShapeDtypeStruct((1, width), F32),
        ),
        in_specs=[ANY, ANY, ANY, ANY, VM, VM, VM, VM, VM, VM, ANY],
        out_specs=(ANY, ANY, VM, VM, VM),
        scratch_shapes=[
            pltpu.VMEM((seqs, length, width), BF),
            pltpu.VMEM((seqs, n_context, half, width), BF),
            pltpu.VMEM((seqs, length, 3 * width), BF),
            pltpu.VMEM((seqs, length, width), BF),
            pltpu.VMEM((length, width), BF),
            pltpu.VMEM((length, 2 * width), F32),
            pltpu.VMEM((length, 3 * width), BF),
            pltpu.VMEM((seqs, n_context, half, width), BF),
            pltpu.VMEM((length, 256), F32),
            sem((n,)), sem((n,)),
            sem((seqs, n_context)), sem((seqs, n_context)),
            sem((4,)), sem((2, max(seqs, 1))),
        ],
        compiler_params=pltpu.CompilerParams(
            collective_id=2, has_side_effects=True, vmem_limit_bytes=VMEM_LIMIT
        ),
        name="attend_backward",
    )(d_attn, tok_a, qkv, att, lse, kmark, qmark, gain, wqkv, wout, out_m)


def per_device(n_expert, n_context, tokens, gain_attn, wqkv, w_out, gain_mix, w_control, w_in, w_back, segments, valid, cotangent):
    reps, seqs, half, width = tokens.shape
    length = half * n_context
    slab = half // n_expert
    group = seqs * n_expert
    e, c = lax.axis_index("expert"), lax.axis_index("context")

    def pick(x, i, axis=0):
        return lax.dynamic_index_in_dim(x, i, axis, keepdims=False)

    seg_a, valid_a = pick(segments, c), pick(valid, c)
    kmark = jnp.where(valid_a > 0, seg_a, -1)[:, :, None]
    qmark = seg_a[:, None, :]
    valid_all = pick(lax.all_gather(valid, "expert"), c, 1).reshape(group, n_context, n_expert, slab)
    valid_m = pick(valid_all, e, 2)
    resid_m, cot_m, tok_a, qkv, att, lse, sq = forward(
        tokens, cotangent, kmark, qmark, gain_attn[None], wqkv, w_out, n_expert, n_context
    )
    d_attn, out_m, grad_in, grad_back_t, grad_control, grad_gain_mix, sq_mix = mix(
        resid_m, cot_m, valid_m[..., None], gain_mix[None], w_control, w_in, w_back, n_expert, n_context
    )
    d_tokens, output, grad_qkv, grad_out, grad_gain = backward(
        d_attn.reshape(seqs, length, width), tok_a, qkv, att, lse, kmark, qmark, gain_attn[None],
        wqkv, w_out, out_m, n_expert, n_context,
    )

    def whole(g):
        return lax.all_gather(lax.psum(g, "dp"), "context").astype(F32)

    squares = jnp.stack(
        [jnp.sum(sq_mix[0]), jnp.sum(sq), jnp.sum(sq_mix[1]), jnp.sum((valid_m > 0).astype(F32))]
    )
    grad_gain, grad_qkv, grad_out, grad_gain_mix, grad_control, squares = lax.psum(
        (grad_gain[0], grad_qkv, grad_out, grad_gain_mix[0], grad_control, squares),
        ("expert", "context", "dp"),
    )
    stats = jnp.sqrt(squares[:3] / (squares[3] * width))
    return (
        output, d_tokens, grad_gain, grad_qkv, grad_out, grad_gain_mix, grad_control,
        whole(grad_in), whole(grad_back_t).transpose(0, 2, 1), stats,
    )


def solution(mesh):
    shards = P("dp", "expert", "context", None)
    rows = P("dp", "expert", None)
    experts = P("expert", None, None)
    return jax.shard_map(
        functools.partial(per_device, mesh.shape["expert"], mesh.shape["context"]),
        mesh=mesh,
        in_specs=(shards, P(), P(), P(), P(), P(), experts, experts, rows, rows, shards),
        out_specs=(shards, shards, P(), P(), P(), P(), P(), experts, experts, P()),
        check_vma=False,
    )
```

```python
import functools
import jax
import jax.numpy as jnp
from jax import lax
from jax.experimental import pallas as pl
from jax.experimental.pallas import tpu as pltpu
from jax.sharding import PartitionSpec as P

HEADS = 8
NEG_FILL = -1e30
MESH = pl.DeviceIdType.MESH
BF = jnp.bfloat16
F32 = jnp.float32
ANY = pl.BlockSpec(memory_space=pl.ANY)
VM = pl.BlockSpec(memory_space=pltpu.VMEM)
VMEM_LIMIT = 60 * 1024 * 1024
DELAY = 2


def dot(a, b, dims=((1,), (0,))):
    return lax.dot_general(a, b, (dims, ((), ())), preferred_element_type=F32)


def normalized(x):
    center = x - jnp.mean(x, -1, keepdims=True)
    spread = jnp.mean(center * center, -1, keepdims=True)
    rstd = lax.rsqrt(spread + 1e-05)
    return center * rstd, rstd


def ring(n_expert, n_context):
    e = lax.axis_index("expert")
    c = lax.axis_index("context")
    n = n_expert * n_context
    me = e * n_context + c

    def peer(k):
        j = lax.rem(me + k, n)
        pe = lax.div(j, n_context)
        pc = lax.rem(j, n_context)
        return j, pe, pc

    return e, c, me, n, peer


def enter(peer, n, reduce=None):
    barrier = pltpu.get_barrier_semaphore()
    for k in range(1, n):
        _, pe, pc = peer(k)
        pl.semaphore_signal(
            barrier, inc=1, device_id={"expert": pe, "context": pc}, device_id_type=MESH
        )
    extra = 0 if reduce is None else reduce.greet()
    pl.semaphore_wait(barrier, n - 1 + extra)


class Reduce:
    def __init__(self, own, rin, lin, ring_r, ring_l, sems, sums, n_dp, n_context):
        self.own, self.ins, self.rings, self.sums = own, (rin, lin), (ring_r, ring_l), sums
        self.send, self.recv, self.swap_s, self.swap_r, self.keep = sems
        self.count, self.slots = own.shape[0], ring_r.shape[0]
        self.n_dp, self.n_context = n_dp, n_context
        self.z, self.c = lax.axis_index("dp"), lax.axis_index("context")

    def greet(self):
        barrier = pltpu.get_barrier_semaphore()
        z, last = self.z, self.n_dp - 1
        for here, to in ((z > 0, z - 1), (z < last, z + 1)):

            @pl.when(here)
            def _():
                pl.semaphore_signal(barrier, inc=1, device_id={"dp": to}, device_id_type=MESH)

        return jnp.minimum(z, 1) + jnp.minimum(last - z, 1)

    def hop(self, way, i):
        to = self.z + (1 if way == 0 else -1)
        slot = lax.rem(i, self.slots)
        return pltpu.make_async_remote_copy(
            src_ref=self.rings[way].at[slot], dst_ref=self.ins[way].at[i],
            send_sem=self.send.at[way, slot], recv_sem=self.recv.at[way, i],
            device_id={"dp": to}, device_id_type=MESH,
        )

    def swaps(self, i):
        out = []
        for k in range(1, self.n_context):
            pc = lax.rem(self.c + k, self.n_context)
            out.append(
                pltpu.make_async_remote_copy(
                    src_ref=self.own.at[i], dst_ref=self.sums.at[self.c, i],
                    send_sem=self.swap_s.at[k, i], recv_sem=self.swap_r.at[k, i],
                    device_id={"context": pc}, device_id_type=MESH,
                )
            )
        out.append(pltpu.make_async_copy(self.own.at[i], self.sums.at[self.c, i], self.keep.at[i]))
        return out

    def tick(self, t):
        last = self.n_dp - 1
        for way in range(2):
            behind = self.z if way == 0 else last - self.z
            i = t - DELAY * behind
            has_in, has_out = behind > 0, behind < last

            @pl.when((i >= 0) & (i < self.count))
            def _():
                @pl.when(has_in)
                def _():
                    self.hop(way, i).wait_recv()

                @pl.when(has_out)
                def _():
                    @pl.when(i >= self.slots)
                    def _():
                        self.hop(way, i - self.slots).wait_send()

                    slot = lax.rem(i, self.slots)

                    @pl.when(has_in)
                    def _():
                        self.rings[way][slot] = (
                            self.ins[way][i].astype(F32) + self.own[i].astype(F32)
                        ).astype(BF)

                    @pl.when(jnp.logical_not(has_in))
                    def _():
                        self.rings[way][slot] = self.own[i]

                    self.hop(way, i).start()

        m = t - DELAY * jnp.maximum(self.z, last - self.z)

        @pl.when((m >= 0) & (m < self.count))
        def _():
            first, final = self.z == 0, self.z == last

            @pl.when(first)
            def _():
                self.own[m] = (self.own[m].astype(F32) + self.ins[1][m].astype(F32)).astype(BF)

            @pl.when(final)
            def _():
                self.own[m] = (self.own[m].astype(F32) + self.ins[0][m].astype(F32)).astype(BF)

            @pl.when(jnp.logical_not(first | final))
            def _():
                self.own[m] = (
                    self.own[m].astype(F32) + self.ins[0][m].astype(F32) + self.ins[1][m].astype(F32)
                ).astype(BF)

            for cp in self.swaps(m):
                cp.start()

    def finish(self, t):
        lax.fori_loop(t, self.count + DELAY * (self.n_dp - 1), lambda i, _: (self.tick(i), 0)[1], 0)
        last = self.n_dp - 1
        for way in range(2):

            @pl.when((self.z if way == 0 else last - self.z) < last)
            def _():
                for i in range(max(0, self.count - self.slots), self.count):
                    self.hop(way, i).wait_send()

        def drain(i, _):
            for cp in self.swaps(i):
                cp.wait()
            return 0

        lax.fori_loop(0, self.count, drain, 0)


def reduce_scratch(count, n_context, slots=4):
    sem = pltpu.SemaphoreType.DMA
    block = pltpu.VMEM((count, 128, 512), BF)
    ring_block = pltpu.VMEM((slots, 128, 512), BF)
    return [
        block, block, ring_block, ring_block,
        sem((2, slots)), sem((2, count)), sem((n_context, count)), sem((n_context, count)), sem((count,)),
    ]


def mask_bias(bias, kmark, qmark, s, q0, qn):
    kk = q0 + qn
    place_k = lax.broadcasted_iota(jnp.int32, (kk, qn), 0)
    place_q = lax.broadcasted_iota(jnp.int32, (kk, qn), 1) + q0
    same = kmark[s, pl.ds(0, kk), :] == qmark[s, :, pl.ds(q0, qn)]
    bias[pl.ds(0, kk), :] = jnp.where(same & (place_k <= place_q), 0.0, NEG_FILL)


def forward_kernel(
    tokens, cot, kmark, qmark, gain, wqkv, wout,
    resid_m, cot_m, tok_a, qkv_o, att_o, lse_o, sq_o,
    tok, qkv, vt, att, att_t, res, bias,
    tok_s, tok_r, cot_s, cot_r, res_s, res_r, own_s, save_s,
    *, n_expert, n_context,
):
    e, c, me, n, peer = ring(n_expert, n_context)
    seqs, length, width = qkv_o.shape[0], qkv_o.shape[1], tokens.shape[-1]
    half = length // n_context
    slab = half // n_expert
    qn = 256
    enter(peer, n)
    outgoing = []
    for s in range(seqs):
        for k in range(1, n_context):
            pc = lax.rem(c + k, n_context)
            cp = pltpu.make_async_remote_copy(
                src_ref=tokens.at[pc, s], dst_ref=tok.at[s, c],
                send_sem=tok_s.at[s, k], recv_sem=tok_r.at[s, k],
                device_id={"context": pc}, device_id_type=MESH,
            )
            cp.start()
            outgoing.append(cp)
    own = []
    for s in range(seqs):
        cp = pltpu.make_async_copy(tokens.at[c, s], tok.at[s, c], own_s.at[s])
        cp.start()
        own.append(cp)

    def project(s, h):
        x = tok[s, h].astype(F32)
        y, _ = normalized(x)
        a = (y * gain[...]).astype(BF)
        at = pl.ds(pl.multiple_of(h * half, half), half)
        qkv[s, at, :] = dot(a, wqkv[...]).astype(BF)
        vt[s, :, at] = dot(wqkv[:, pl.ds(2 * width, width)], a, ((0,), (1,))).astype(BF)

    for s in range(seqs):
        own[s].wait()
        project(s, c)
    for cp in outgoing:
        cp.wait()
    crossing = []
    for k in range(1, n):
        j, pe, pc = peer(k)
        cp = pltpu.make_async_remote_copy(
            src_ref=cot.at[pc, :, pl.ds(pl.multiple_of(pe * slab, slab), slab), :],
            dst_ref=cot_m.at[pl.ds(e * seqs, seqs), c],
            send_sem=cot_s.at[k], recv_sem=cot_r.at[k],
            device_id={"expert": pe, "context": pc}, device_id_type=MESH,
        )
        cp.start()
        crossing.append(cp)
    local = pltpu.make_async_copy(
        cot.at[c, :, pl.ds(pl.multiple_of(e * slab, slab), slab), :],
        cot_m.at[pl.ds(e * seqs, seqs), c], own_s.at[seqs],
    )
    local.start()
    for k in range(1, n_context):
        for s in range(seqs):
            project(s, lax.rem(c + k, n_context))
    saves = [
        pltpu.make_async_copy(qkv, qkv_o, save_s.at[0]),
        pltpu.make_async_copy(tok, tok_a, save_s.at[1]),
    ]
    for cp in saves:
        cp.start()
    lane = lax.broadcasted_iota(jnp.int32, (qn, 128), 1)
    moving = []
    total = jnp.zeros((1, width), F32)
    for s in range(seqs):
        for qb in range(length // qn):
            kk = (qb + 1) * qn
            rows = pl.ds(qb * qn, qn)
            mask_bias(bias, kmark, qmark, s, qb * qn, qn)

            for at in range(0, width, 128):
                q2 = qkv[s, rows, pl.ds(at, 128)] * BF(0.125)
                k2 = qkv[s, pl.ds(0, kk), pl.ds(width + at, 128)]
                outs = []
                for h in range(2):
                    mine = (lane >= 64) if h else (lane < 64)
                    qm = jnp.where(mine, q2, jnp.zeros_like(q2))
                    st = dot(k2, qm, ((1,), (1,))) + bias[pl.ds(0, kk), :]
                    top = jnp.max(st, 0, keepdims=True)
                    p = jnp.exp(st - top)
                    tot = jnp.sum(p, 0, keepdims=True)
                    lse_o[s, pl.ds(at // 64 + h, 1), rows] = top + jnp.log(tot)
                    vh = vt[s, pl.ds(at + 64 * h, 64), pl.ds(0, kk)]
                    outs.append(dot(vh, p.astype(BF)) * (1.0 / tot))
                both = jnp.concatenate(outs, 0)
                att_t[s, pl.ds(at, 128), rows] = both.astype(BF)
                att[s, rows, pl.ds(at, 128)] = both.T.astype(BF)
            h = qb * qn // half
            attn_out = dot(att[s, rows, :], wout[...])
            within = qb * qn - h * half
            x = tok[s, h, pl.ds(within, qn), :].astype(F32)
            res[s, h, pl.ds(within, qn), :] = (x + attn_out).astype(BF)
            ok = kmark[s, rows, :] >= 0
            total += jnp.sum(jnp.where(ok, attn_out * attn_out, 0.0), 0, keepdims=True)
            if (qb + 1) * qn == (h + 1) * half:
                for k in range(1, n_expert):
                    pe = lax.rem(e + k, n_expert)
                    cp = pltpu.make_async_remote_copy(
                        src_ref=res.at[s, h, pl.ds(pl.multiple_of(pe * slab, slab), slab), :],
                        dst_ref=resid_m.at[e * seqs + s, h],
                        send_sem=res_s.at[s, h, k], recv_sem=res_r.at[s, h, k],
                        device_id={"expert": pe}, device_id_type=MESH,
                    )
                    cp.start()
                    moving.append(cp)
                cp = pltpu.make_async_copy(
                    res.at[s, h, pl.ds(pl.multiple_of(e * slab, slab), slab), :],
                    resid_m.at[e * seqs + s, h], res_s.at[s, h, 0],
                )
                cp.start()
                moving.append(cp)
    sq_o[...] = total
    keep = pltpu.make_async_copy(att_t, att_o, save_s.at[2])
    keep.start()
    for cp in saves + moving + crossing + [local, keep]:
        cp.wait()


def forward(tokens, cot, kmark, qmark, gain, wqkv, wout, n_expert, n_context):
    reps, seqs, half, width = tokens.shape
    length = half * n_context
    slab = half // n_expert
    group = seqs * n_expert
    n = n_expert * n_context
    sem = pltpu.SemaphoreType.DMA
    return pl.pallas_call(
        functools.partial(forward_kernel, n_expert=n_expert, n_context=n_context),
        out_shape=(
            jax.ShapeDtypeStruct((group, n_context, slab, width), BF),
            jax.ShapeDtypeStruct((group, n_context, slab, width), BF),
            jax.ShapeDtypeStruct((seqs, n_context, half, width), BF),
            jax.ShapeDtypeStruct((seqs, length, 3 * width), BF),
            jax.ShapeDtypeStruct((seqs, width, length), BF),
            jax.ShapeDtypeStruct((seqs, HEADS, length), F32),
            jax.ShapeDtypeStruct((1, width), F32),
        ),
        in_specs=[ANY, ANY, VM, VM, VM, VM, VM],
        out_specs=(ANY, ANY, ANY, ANY, ANY, VM, VM),
        scratch_shapes=[
            pltpu.VMEM((seqs, n_context, half, width), BF),
            pltpu.VMEM((seqs, length, 3 * width), BF),
            pltpu.VMEM((seqs, width, length), BF),
            pltpu.VMEM((seqs, length, width), BF),
            pltpu.VMEM((seqs, width, length), BF),
            pltpu.VMEM((seqs, n_context, half, width), BF),
            pltpu.VMEM((length, 256), F32),
            sem((seqs, n_context)), sem((seqs, n_context)),
            sem((n,)), sem((n,)),
            sem((seqs, n_context, n_expert)), sem((seqs, n_context, n_expert)),
            sem((seqs + 1,)), sem((3,)),
        ],
        compiler_params=pltpu.CompilerParams(
            collective_id=0, has_side_effects=True, vmem_limit_bytes=VMEM_LIMIT
        ),
        name="attend_forward",
    )(tokens, cot, kmark, qmark, gain, wqkv, wout)


def mix_kernel(
    resid_m, cot_m, ok_m, gain, wc, w_in, w_back,
    d_attn, out_m, part_o, sums, gc_o, gm_o, sq_o,
    res, cot, u, wts, mixed, dexp, xs, des, eos, dms, eor, dmr, win, wback, acts, d_pres, glow,
    go_s, go_r, back_s, back_r, at_s, at_r, in_s, save_s, *rest,
    n_expert, n_context, n_dp, early,
):
    e, c, me, n, peer = ring(n_expert, n_context)
    group, halves, slab, width = res.shape
    seqs = group // n_expert
    ff = win.shape[1]
    experts = n
    span = max(16, 256 // group)
    steps = slab // span
    chunk = 512 // slab
    reduce = Reduce(
        glow.at[pl.ds(0, early)], *rest[:4], rest[4:], sums, n_dp, n_context
    )
    loads = [
        pltpu.make_async_copy(resid_m, res, in_s.at[0]),
        pltpu.make_async_copy(cot_m, cot, in_s.at[1]),
        pltpu.make_async_copy(w_in.at[c], win, in_s.at[2]),
        pltpu.make_async_copy(w_back.at[c], wback, in_s.at[3]),
    ]
    for cp in loads:
        cp.start()
    enter(peer, n, reduce)
    rows, cols = group * span, experts * span
    spread = (
        lax.broadcasted_iota(jnp.int32, (experts, cols), 1) // span
        == lax.broadcasted_iota(jnp.int32, (experts, cols), 0)
    ).astype(BF)
    gather = (
        lax.broadcasted_iota(jnp.int32, (cols, experts), 0) // span
        == lax.broadcasted_iota(jnp.int32, (cols, experts), 1)
    ).astype(BF)
    diag = lax.rem(lax.broadcasted_iota(jnp.int32, (rows, cols), 0), span) == lax.rem(
        lax.broadcasted_iota(jnp.int32, (rows, cols), 1), span
    )
    loads[0].wait()
    loads[1].wait()
    sent = []
    for h in range(halves):

        def first(g, _):
            at = pl.ds(pl.multiple_of(g * span, span), span)
            r = res[:, h, at, :].reshape(rows, width).astype(F32)
            normed, _ = normalized(r)
            ug = (normed * gain[...]).astype(BF)
            u[:, h, at, :] = ug.reshape(group, span, width)
            ok = ok_m[:, h, at, :].reshape(rows, 1)
            logits = jnp.where(ok > 0, dot(ug, wc[...]), NEG_FILL).reshape(group, span, experts)
            ex = jnp.exp(logits - jnp.max(logits, 0, keepdims=True))
            w = (ex / jnp.sum(ex, 0, keepdims=True)).reshape(rows, experts)
            wts[h * steps + g] = w
            wide = jnp.where(diag, dot(w.astype(BF), spread), 0.0).astype(BF)
            cg = cot[:, h, at, :].reshape(rows, width)
            mixed[h, :, at, :] = dot(wide, ug, ((0,), (0,))).astype(BF).reshape(experts, span, width)
            dexp[h, :, at, :] = dot(wide, cg, ((0,), (0,))).astype(BF).reshape(experts, span, width)
            return 0

        lax.fori_loop(0, steps, first, 0)
        for i, (src, dst) in enumerate(((mixed, xs), (dexp, des))):
            dst[h, 0] = src[h, me]
            for k in range(1, n):
                j, pe, pc = peer(k)
                cp = pltpu.make_async_remote_copy(
                    src_ref=src.at[h, j], dst_ref=dst.at[h, k],
                    send_sem=go_s.at[i, h, k], recv_sem=go_r.at[i, h, k],
                    device_id={"expert": pe, "context": pc}, device_id_type=MESH,
                )
                cp.start()
                sent.append((i, h, k, cp))
    loads[2].wait()
    loads[3].wait()
    tile = 512
    returned = []
    for h in range(halves):
        for kg in range(n // chunk):
            slots = range(kg * chunk, (kg + 1) * chunk)
            for i, hh, k, cp in sent:
                if hh == h and k in slots:
                    cp.wait_recv()
            x = xs[h, pl.ds(kg * chunk, chunk)].reshape(chunk * slab, width)
            de = des[h, pl.ds(kg * chunk, chunk)].reshape(chunk * slab, width)
            base = (h * (n // chunk) + kg) * chunk * slab

            def expert_tile(f, carry):
                eo, dm = carry
                at = pl.ds(pl.multiple_of(f * tile, tile), tile)
                pre = dot(x, win[:, at])
                sq = pre * pre
                t = jnp.tanh(0.7978845608028654 * pre * (1.0 + 0.044715 * sq))
                act = (0.5 * pre * (1.0 + t)).astype(BF)
                slope = 0.5 * (1.0 + t) + 0.5 * pre * (1.0 - t * t) * (
                    0.7978845608028654 * (1.0 + 3 * 0.044715 * sq)
                )
                d_pre = (slope * dot(de, wback[at, :], ((1,), (1,)))).astype(BF)
                acts[pl.ds(base, chunk * slab), at] = act
                d_pres[pl.ds(base, chunk * slab), at] = d_pre
                return eo + dot(act, wback[at, :]), dm + dot(d_pre, win[:, at], ((1,), (1,)))

            zero = jnp.zeros((chunk * slab, width), F32)
            eo, dm = lax.fori_loop(0, ff // tile, expert_tile, (zero, zero))
            eos[h, pl.ds(kg * chunk, chunk)] = eo.astype(BF).reshape(chunk, slab, width)
            dms[h, pl.ds(kg * chunk, chunk)] = dm.astype(BF).reshape(chunk, slab, width)
            for i, (src, dst) in enumerate(((eos, eor), (dms, dmr))):
                for k in slots:
                    if k == 0:
                        dst[h, me] = src[h, 0]
                        continue
                    j, pe, pc = peer(n - k)
                    cp = pltpu.make_async_remote_copy(
                        src_ref=src.at[h, k], dst_ref=dst.at[h, me],
                        send_sem=back_s.at[i, h, k], recv_sem=back_r.at[i, h, k],
                        device_id={"expert": pe, "context": pc}, device_id_type=MESH,
                    )
                    cp.start()
                    returned.append((i, h, k, cp))
    per = width // 128
    tokens = halves * n * slab

    def grad_in_tile(f, _):
        at = pl.ds(pl.multiple_of(f * tile, tile), tile)
        g = dot(xs[...].reshape(tokens, width), d_pres[:, at], ((0,), (0,)))
        glow[pl.ds(f * per, per)] = g.astype(BF).reshape(per, 128, tile)
        return 0

    def grad_back_tile(f, _):
        at = pl.ds(pl.multiple_of(f * tile, tile), tile)
        g = dot(acts[:, at], des[...].reshape(tokens, width), ((0,), (0,)))
        glow[pl.ds((ff // tile + f) * per, per)] = g.astype(BF).reshape(per, 128, width)
        for i in range(per):
            reduce.tick(f * per + i)
        return 0

    lax.fori_loop(0, ff // tile, grad_in_tile, 0)
    lax.fori_loop(0, ff // tile, grad_back_tile, 0)
    blocks = glow.shape[0]
    out, dat = mixed, dexp
    for _, _, _, sending in sent:
        sending.wait_send()
    keep = [
        pltpu.make_async_copy(glow.at[pl.ds(early, blocks - early)], part_o, save_s.at[0])
    ]
    keep[0].start()
    gc_o[...] = jnp.zeros_like(gc_o)
    gm_o[...] = jnp.zeros_like(gm_o)
    sq_o[...] = jnp.zeros_like(sq_o)
    moving = []
    for h in range(halves):
        for i, hh, k, cp in returned:
            if hh == h:
                cp.wait_recv()

        def second(g, _):
            at = pl.ds(pl.multiple_of(g * span, span), span)
            r = res[:, h, at, :].reshape(rows, width).astype(F32)
            normed, rstd = normalized(r)
            ug = u[:, h, at, :].reshape(rows, width)
            cg = cot[:, h, at, :].reshape(rows, width)
            ok = ok_m[:, h, at, :].reshape(rows, 1) > 0
            eg = eor[h, :, at, :].reshape(cols, width)
            dg = dmr[h, :, at, :].reshape(cols, width)
            w = wts[h * steps + g]
            wide = jnp.where(diag, dot(w.astype(BF), spread), 0.0).astype(BF)
            mix = dot(wide, eg)
            full = r + mix
            out[h, :, at, :] = full.astype(BF).reshape(group, span, width)
            sq_o[pl.ds(0, 1), :] += jnp.sum(jnp.where(ok, full * full, 0.0), 0, keepdims=True)
            sq_o[pl.ds(1, 1), :] += jnp.sum(jnp.where(ok, mix * mix, 0.0), 0, keepdims=True)
            dw = jnp.where(diag, dot(cg, eg, ((1,), (1,))) + dot(ug, dg, ((1,), (1,))), 0.0)
            high = dw.astype(BF)
            rest = (dw - high.astype(F32)).astype(BF)
            dw = dot(high, gather) + dot(rest, gather)
            inner = jnp.sum((w * dw).reshape(group, span, experts), 0, keepdims=True)
            d_log = (
                (w.reshape(group, span, experts) * (dw.reshape(group, span, experts) - inner))
                .reshape(rows, experts)
                .astype(BF)
            )
            gc_o[...] += dot(ug, d_log, ((0,), (0,)))
            d_u = dot(d_log, wc[...], ((1,), (1,))) + dot(wide, dg)
            gm_o[...] += jnp.sum(d_u * normed, 0, keepdims=True)
            q = d_u * gain[...]
            d_res = cg.astype(F32) + rstd * (
                q - jnp.mean(q, -1, keepdims=True) - normed * jnp.mean(q * normed, -1, keepdims=True)
            )
            dat[h, :, at, :] = d_res.astype(BF).reshape(group, span, width)
            reduce.tick(ff // 128 + h * steps + g)
            return 0

        lax.fori_loop(0, steps, second, 0)
        mine = pl.ds(pl.multiple_of(e * slab, slab), slab)
        for k in range(1, n_expert):
            pe = lax.rem(e + k, n_expert)
            cp = pltpu.make_async_remote_copy(
                src_ref=dat.at[h, pl.ds(pe * seqs, seqs)], dst_ref=d_attn.at[:, h, mine, :],
                send_sem=at_s.at[h, k], recv_sem=at_r.at[h, k],
                device_id={"expert": pe}, device_id_type=MESH,
            )
            cp.start()
            moving.append(cp)
        cp = pltpu.make_async_copy(
            dat.at[h, pl.ds(e * seqs, seqs)], d_attn.at[:, h, mine, :], at_s.at[h, 0]
        )
        cp.start()
        moving.append(cp)
    cp = pltpu.make_async_copy(out, out_m, save_s.at[2])
    cp.start()
    for _, _, _, sending in returned:
        sending.wait_send()
    reduce.finish(ff // 128 + halves * steps)
    for cp in moving + keep + [cp]:
        cp.wait()


def mix(resid_m, cot_m, ok_m, gain, wc, w_in, w_back, n_expert, n_context, n_dp, early):
    group, halves, slab, width = resid_m.shape
    seqs = group // n_expert
    n = n_expert * n_context
    ff = w_in.shape[-1]
    span = max(16, 256 // group)
    steps = slab // span
    blocks = 2 * width * ff // (128 * 512)
    sem = pltpu.SemaphoreType.DMA
    block = pltpu.VMEM((group, halves, slab, width), BF)
    turned = pltpu.VMEM((halves, n, slab, width), BF)
    return pl.pallas_call(
        functools.partial(
            mix_kernel, n_expert=n_expert, n_context=n_context, n_dp=n_dp, early=early
        ),
        out_shape=(
            jax.ShapeDtypeStruct((seqs, halves, slab * n_expert, width), BF),
            jax.ShapeDtypeStruct((halves, group, slab, width), BF),
            jax.ShapeDtypeStruct((blocks - early, 128, 512), BF),
            jax.ShapeDtypeStruct((n_context, early, 128, 512), BF),
            jax.ShapeDtypeStruct((width, n), F32),
            jax.ShapeDtypeStruct((1, width), F32),
            jax.ShapeDtypeStruct((2, width), F32),
        ),
        in_specs=[ANY, ANY, VM, VM, VM, ANY, ANY],
        out_specs=(ANY, ANY, ANY, ANY, VM, VM, VM),
        scratch_shapes=[
            block, block, block,
            pltpu.VMEM((halves * steps, group * span, n), F32),
            turned, turned, turned, turned, turned, turned, turned, turned,
            pltpu.VMEM((width, ff), BF), pltpu.VMEM((ff, width), BF),
            pltpu.VMEM((halves * n * slab, ff), BF), pltpu.VMEM((halves * n * slab, ff), BF),
            pltpu.VMEM((blocks, 128, 512), BF),
            sem((2, halves, n)), sem((2, halves, n)),
            sem((2, halves, n)), sem((2, halves, n)),
            sem((halves, n_expert)), sem((halves, n_expert)),
            sem((4,)), sem((3,)),
            *reduce_scratch(early, n_context),
        ],
        compiler_params=pltpu.CompilerParams(
            collective_id=1, has_side_effects=True, vmem_limit_bytes=63 * 1024 * 1024
        ),
        name="mix_and_experts",
    )(resid_m, cot_m, ok_m, gain, wc, w_in, w_back)


def backward_kernel(
    d_attn, tok_a, qkv_a, att_a, lse, kmark, qmark, gain, wqkv, wout, out_m, part,
    dtok_o, out_o, sums, gq_o, go_o, gg_o,
    da, tok, qkv, att, datt, delta, dkv, dqkv, dtok, bias, own,
    out_s, out_r, tok_s, tok_r, in_s, own_s, *rest,
    n_expert, n_context, n_dp,
):
    e, c, me, n, peer = ring(n_expert, n_context)
    seqs, length, width = da.shape
    half = length // n_context
    slab = half // n_expert
    qn = 256
    loads = [
        pltpu.make_async_copy(src, dst, in_s.at[i])
        for i, (src, dst) in enumerate(
            ((d_attn, da), (att_a, att), (qkv_a, qkv), (tok_a, tok), (part, own))
        )
    ]
    reduce = Reduce(own, *rest[:4], rest[4:], sums, n_dp, n_context)
    for cp in loads:
        cp.start()
    enter(peer, n, reduce)
    crossing = []
    mine = pl.ds(pl.multiple_of(e * slab, slab), slab)
    for k in range(1, n):
        j, pe, pc = peer(k)
        cp = pltpu.make_async_remote_copy(
            src_ref=out_m.at[pc, pl.ds(pe * seqs, seqs)], dst_ref=out_o.at[c, :, mine, :],
            send_sem=out_s.at[k], recv_sem=out_r.at[k],
            device_id={"expert": pe, "context": pc}, device_id_type=MESH,
        )
        cp.start()
        crossing.append(cp)
    cp = pltpu.make_async_copy(
        out_m.at[c, pl.ds(e * seqs, seqs)], out_o.at[c, :, mine, :], own_s.at[0, 0]
    )
    cp.start()
    crossing.append(cp)
    lane = lax.broadcasted_iota(jnp.int32, (qn, 128), 1)
    gg_o[...] = jnp.zeros_like(gg_o)
    for cp in loads:
        cp.wait()
    pairs = width // 128
    for s in range(seqs):
        datt[...] = dot(da[s], wout[...], ((1,), (1,))).astype(BF)
        turned = dot(wout[...], da[s], ((1,), (1,))).astype(BF).astype(F32) * att[s].astype(F32)
        delta[...] = jnp.sum(turned.reshape(HEADS, width // HEADS, length), 1)
        go = dot(att[s], da[s])
        go_o[...] = go if s == 0 else go_o[...] + go
        dkv[...] = jnp.zeros_like(dkv)
        for qb in range(length // qn):
            kk = (qb + 1) * qn
            rows = pl.ds(qb * qn, qn)
            mask_bias(bias, kmark, qmark, s, qb * qn, qn)

            def pair(hp, _):
                at = pl.multiple_of(hp * 128, 128)
                q2 = qkv[s, rows, pl.ds(at, 128)] * BF(0.125)
                k2 = qkv[s, pl.ds(0, kk), pl.ds(width + at, 128)]
                v2 = qkv[s, pl.ds(0, kk), pl.ds(2 * width + at, 128)]
                do2 = datt[rows, pl.ds(at, 128)]
                kt = k2.T
                dqs, dss, lows, qms, doms = [], [], [], [], []
                for h in range(2):
                    mine = (lane >= 64) if h else (lane < 64)
                    qm = jnp.where(mine, q2, jnp.zeros_like(q2))
                    dom = jnp.where(mine, do2, jnp.zeros_like(do2))
                    st = dot(k2, qm, ((1,), (1,))) + bias[pl.ds(0, kk), :]
                    p = jnp.exp(st - lse[s, pl.ds(2 * hp + h, 1), rows])
                    dp = dot(v2, dom, ((1,), (1,)))
                    ds = (p * (dp - delta[pl.ds(2 * hp + h, 1), rows])).astype(BF)
                    dqs.append(dot(kt[h * 64 : h * 64 + 64], ds))
                    dss.append(ds)
                    lows.append(p.astype(BF))
                    qms.append(qm)
                    doms.append(dom)
                dqkv[rows, pl.ds(at, 128)] = (
                    (jnp.concatenate(dqs, 0) * 0.125).T.astype(BF)
                )
                dkv[pl.ds(0, kk), pl.ds(at, 128)] += dot(dss[0], qms[0]) + dot(dss[1], qms[1])
                dkv[pl.ds(0, kk), pl.ds(width + at, 128)] += dot(lows[0], doms[0]) + dot(
                    lows[1], doms[1]
                )
                reduce.tick((s * (length // qn) + qb) * pairs + hp)
                return 0

            lax.fori_loop(0, pairs, pair, 0)
        dqkv[:, pl.ds(width, 2 * width)] = dkv[...].astype(BF)
        for h in range(n_context):
            rows = pl.ds(h * half, half)
            normed, rstd = normalized(tok[s, h].astype(F32))
            a = (normed * gain[...]).astype(BF)
            gq = dot(a, dqkv[rows, :], ((0,), (0,)))
            gq_o[...] = gq if s == 0 and h == 0 else gq_o[...] + gq
            d_a = dot(dqkv[rows, :], wqkv[...], ((1,), (1,)))
            gg_o[...] += jnp.sum(d_a * normed, 0, keepdims=True)
            q = d_a * gain[...]
            dt = da[s, rows, :].astype(F32) + rstd * (
                q - jnp.mean(q, -1, keepdims=True) - normed * jnp.mean(q * normed, -1, keepdims=True)
            )
            dtok[s, h] = dt.astype(BF)
        for k in range(1, n_context):
            pc = lax.rem(c + k, n_context)
            cp = pltpu.make_async_remote_copy(
                src_ref=dtok.at[s, pc], dst_ref=dtok_o.at[c, s],
                send_sem=tok_s.at[s, k], recv_sem=tok_r.at[s, k],
                device_id={"context": pc}, device_id_type=MESH,
            )
            cp.start()
            crossing.append(cp)
        cp = pltpu.make_async_copy(dtok.at[s, c], dtok_o.at[c, s], own_s.at[1, s])
        cp.start()
        crossing.append(cp)
    reduce.finish(seqs * (length // qn) * pairs)
    for cp in crossing:
        cp.wait()


def backward(
    d_attn, tok_a, qkv, att, lse, kmark, qmark, gain, wqkv, wout, out_m, part, n_expert, n_context, n_dp
):
    seqs, length, width = d_attn.shape
    half = length // n_context
    n = n_expert * n_context
    sem = pltpu.SemaphoreType.DMA
    return pl.pallas_call(
        functools.partial(
            backward_kernel, n_expert=n_expert, n_context=n_context, n_dp=n_dp
        ),
        out_shape=(
            jax.ShapeDtypeStruct((n_context, seqs, half, width), BF),
            jax.ShapeDtypeStruct((n_context, seqs, half, width), BF),
            jax.ShapeDtypeStruct((n_context, *part.shape), BF),
            jax.ShapeDtypeStruct((width, 3 * width), F32),
            jax.ShapeDtypeStruct((width, width), F32),
            jax.ShapeDtypeStruct((1, width), F32),
        ),
        in_specs=[ANY, ANY, ANY, ANY, VM, VM, VM, VM, VM, VM, ANY, ANY],
        out_specs=(ANY, ANY, ANY, VM, VM, VM),
        scratch_shapes=[
            pltpu.VMEM((seqs, length, width), BF),
            pltpu.VMEM((seqs, n_context, half, width), BF),
            pltpu.VMEM((seqs, length, 3 * width), BF),
            pltpu.VMEM((seqs, width, length), BF),
            pltpu.VMEM((length, width), BF),
            pltpu.VMEM((HEADS, length), F32),
            pltpu.VMEM((length, 2 * width), F32),
            pltpu.VMEM((length, 3 * width), BF),
            pltpu.VMEM((seqs, n_context, half, width), BF),
            pltpu.VMEM((length, 256), F32),
            pltpu.VMEM(part.shape, BF),
            sem((n,)), sem((n,)),
            sem((seqs, n_context)), sem((seqs, n_context)),
            sem((5,)), sem((2, seqs)),
            *reduce_scratch(part.shape[0], n_context),
        ],
        compiler_params=pltpu.CompilerParams(
            collective_id=2, has_side_effects=True, vmem_limit_bytes=VMEM_LIMIT
        ),
        name="attend_backward",
    )(d_attn, tok_a, qkv, att, lse, kmark, qmark, gain, wqkv, wout, out_m, part)


def share_kernel(
    gq, go, misc, gq_o, go_o, misc_o,
    pack, other, chip, corners, along, whole,
    core_s, core_r, chip_s, chip_r, dp_s, dp_r, dp2_s, dp2_r, out_s, out_r, fin_s, fin_r,
    *, n_expert, n_context, n_dp,
):
    e, c, z = (lax.axis_index(a) for a in ("expert", "context", "dp"))
    core = lax.rem(e, 2)
    chips = n_expert // 2 * n_context
    me = lax.div(e, 2) * n_context + c
    width = go.shape[1]
    total = pack.shape[0]
    part = total // 2
    piece = part // chips
    lanes = width // n_dp
    twin = {"expert": e + 1 - 2 * core}

    def chip_at(k):
        j = lax.rem(me + k, chips)
        return j, {"expert": lax.div(j, n_context) * 2 + core, "context": lax.rem(j, n_context)}

    barrier = pltpu.get_barrier_semaphore()
    where = [twin] + [chip_at(k)[1] for k in range(1, chips)]
    where += [{"dp": lax.rem(z + k, n_dp)} for k in range(1, n_dp)]
    for to in where:
        pl.semaphore_signal(barrier, inc=1, device_id=to, device_id_type=MESH)
    for b in range(3):
        pack[pl.ds(b * width, width), :] = gq[:, pl.ds(b * width, width)].astype(BF)
    pack[pl.ds(3 * width, width), :] = go[...].astype(BF)
    rest = total - 4 * width
    tail = misc[...]
    if rest > tail.shape[0]:
        tail = jnp.concatenate((tail, jnp.zeros((rest - tail.shape[0], width), F32)))
    pack[pl.ds(4 * width, rest), :] = tail.astype(BF)
    pl.semaphore_wait(barrier, len(where))

    def remote(src, dst, ss, rs, to):
        cp = pltpu.make_async_remote_copy(
            src_ref=src, dst_ref=dst, send_sem=ss, recv_sem=rs, device_id=to, device_id_type=MESH
        )
        cp.start()
        return cp

    def rows(i, n):
        return pl.ds(pl.multiple_of(i * n, 16), n)

    sent = []
    for k in range(chips):
        j = lax.rem(me + k + 1, chips)
        at = pl.ds(pl.multiple_of((1 - core) * part + j * piece, 16), piece)
        sent.append(remote(pack.at[at], other.at[rows(j, piece)], core_s.at[k], core_r.at[k], twin))
    first = list(sent)
    for k in range(chips):
        j = lax.rem(me + k + 1, chips)
        first[k].wait_recv()
        at = pl.ds(pl.multiple_of(core * part + j * piece, 16), piece)
        chip[rows(j, piece), :] = (
            pack[at, :].astype(F32) + other[rows(j, piece), :].astype(F32)
        ).astype(BF)
        if k < chips - 1:
            _, to = chip_at(k + 1)
            sent.append(
                remote(chip.at[rows(j, piece)], corners.at[k], chip_s.at[k], chip_r.at[k], to)
            )
    acc = chip[rows(me, piece), :].astype(F32)
    for k in range(chips - 1):
        sent[chips + k].wait_recv()
        acc += corners[k].astype(F32)
    chip[rows(me, piece), :] = acc.astype(BF)
    mine = pl.ds(pl.multiple_of(z * lanes, lanes), lanes)
    steps = []
    for k in range(1, n_dp):
        to = lax.rem(z + k, n_dp)
        theirs = pl.ds(pl.multiple_of(to * lanes, lanes), lanes)
        steps.append(
            remote(
                chip.at[rows(me, piece), theirs], along.at[k - 1], dp_s.at[k - 1], dp_r.at[k - 1],
                {"dp": to},
            )
        )
    acc = chip[rows(me, piece), mine].astype(F32)
    for k in range(1, n_dp):
        steps[k - 1].wait_recv()
        acc += along[k - 1].astype(F32)
    home = pl.ds(pl.multiple_of(core * part + me * piece, 16), piece)
    whole[home, mine] = acc.astype(BF)
    back = []
    for k in range(1, n_dp):
        to = lax.rem(z + k, n_dp)
        back.append(
            remote(
                whole.at[home, mine], whole.at[home, mine], dp2_s.at[k - 1], dp2_r.at[k - 1],
                {"dp": to},
            )
        )
    for cp in back:
        cp.wait_recv()
    spread = [remote(whole.at[home], whole.at[home], fin_s.at[0], fin_r.at[0], twin)]
    outs = []
    for k in range(1, chips):
        _, to = chip_at(k)
        outs.append(remote(whole.at[home], whole.at[home], out_s.at[k - 1], out_r.at[k - 1], to))
    for k in range(1, chips):
        outs[k - 1].wait_recv()
        j = lax.rem(me + chips - k, chips)
        got = whole.at[pl.ds(pl.multiple_of(core * part + j * piece, 16), piece)]
        spread.append(remote(got, got, fin_s.at[k], fin_r.at[k], twin))
    for cp in spread:
        cp.wait_recv()
    for b in range(3):
        gq_o[:, pl.ds(b * width, width)] = whole[pl.ds(b * width, width), :].astype(F32)
    go_o[...] = whole[pl.ds(3 * width, width), :].astype(F32)
    misc_o[...] = whole[pl.ds(4 * width, misc_o.shape[0]), :].astype(F32)
    for cp in sent + steps + back + outs + spread:
        cp.wait_send()


def share(gq, go, misc, n_expert, n_context, n_dp):
    width = go.shape[1]
    chips = n_expert // 2 * n_context
    unit = 2 * chips * 16
    total = -(-(4 * width + misc.shape[0]) // unit) * unit
    part = total // 2
    piece = part // chips
    sem = pltpu.SemaphoreType.DMA
    return pl.pallas_call(
        functools.partial(share_kernel, n_expert=n_expert, n_context=n_context, n_dp=n_dp),
        out_shape=(
            jax.ShapeDtypeStruct(gq.shape, F32),
            jax.ShapeDtypeStruct(go.shape, F32),
            jax.ShapeDtypeStruct(misc.shape, F32),
        ),
        in_specs=[VM, VM, VM],
        out_specs=(VM, VM, VM),
        scratch_shapes=[
            pltpu.VMEM((total, width), BF),
            pltpu.VMEM((part, width), BF),
            pltpu.VMEM((part, width), BF),
            pltpu.VMEM((max(1, chips - 1), piece, width), BF),
            pltpu.VMEM((max(1, n_dp - 1), piece, width // n_dp), BF),
            pltpu.VMEM((total, width), BF),
            sem((chips,)), sem((chips,)), sem((chips,)), sem((chips,)),
            sem((n_dp,)), sem((n_dp,)), sem((n_dp,)), sem((n_dp,)),
            sem((chips,)), sem((chips,)), sem((chips,)), sem((chips,)),
        ],
        compiler_params=pltpu.CompilerParams(
            collective_id=3, has_side_effects=True, vmem_limit_bytes=VMEM_LIMIT
        ),
        name="share_gradients",
    )(gq, go, misc)


def per_device(n_expert, n_context, n_dp, tokens, gain_attn, wqkv, w_out, gain_mix, w_control, w_in, w_back, segments, valid, cotangent):
    reps, seqs, half, width = tokens.shape
    length = half * n_context
    slab = half // n_expert
    group = seqs * n_expert
    e, c = lax.axis_index("expert"), lax.axis_index("context")

    def pick(x, i, axis=0):
        return lax.dynamic_index_in_dim(x, i, axis, keepdims=False)

    seg_a, valid_a = pick(segments, c), pick(valid, c)
    kmark = jnp.where(valid_a > 0, seg_a, -1)[:, :, None]
    qmark = seg_a[:, None, :]
    valid_all = pick(lax.all_gather(valid, "expert"), c, 1).reshape(group, n_context, n_expert, slab)
    valid_m = pick(valid_all, e, 2)
    resid_m, cot_m, tok_a, qkv, att, lse, sq = forward(
        tokens, cotangent, kmark, qmark, gain_attn[None], wqkv, w_out, n_expert, n_context
    )
    d_attn, out_m, part, sums_early, grad_control, grad_gain_mix, sq_mix = mix(
        resid_m, cot_m, valid_m[..., None], gain_mix[None], w_control, w_in, w_back,
        n_expert, n_context, n_dp, width * w_in.shape[-1] // (128 * 512),
    )
    d_tokens, output, sums_late, grad_qkv, grad_out, grad_gain = backward(
        d_attn.reshape(seqs, length, width), tok_a, qkv, att, lse, kmark, qmark, gain_attn[None],
        wqkv, w_out, out_m, part, n_expert, n_context, n_dp,
    )

    ff = w_in.shape[-1]
    grad_in = (
        sums_early.reshape(n_context, ff // 512, width, 512).transpose(0, 2, 1, 3)
        .reshape(n_context, width, ff).astype(F32)
    )
    grad_back = sums_late.reshape(n_context, ff, width).astype(F32)
    squares = jnp.stack(
        [jnp.sum(sq_mix[0]), jnp.sum(sq), jnp.sum(sq_mix[1]), jnp.sum((valid_m > 0).astype(F32))]
    )
    n_all = grad_control.shape[1]
    misc = jnp.concatenate(
        (
            grad_control.T, grad_gain, grad_gain_mix, jnp.pad(squares, (0, width - 4))[None],
            jnp.zeros((-(n_all + 3) % 16, width), F32),
        )
    )
    grad_qkv, grad_out, misc = share(grad_qkv, grad_out, misc, n_expert, n_context, n_dp)
    grad_control = misc[:n_all].T
    grad_gain, grad_gain_mix, squares = (misc[n_all + i] for i in range(3))
    stats = jnp.sqrt(squares[:3] / (squares[3] * width))
    return (
        output, d_tokens, grad_gain, grad_qkv, grad_out, grad_gain_mix, grad_control,
        grad_in, grad_back, stats,
    )


def solution(mesh):
    shards = P("dp", "expert", "context", None)
    rows = P("dp", "expert", None)
    experts = P("expert", None, None)
    return jax.shard_map(
        functools.partial(
            per_device, mesh.shape["expert"], mesh.shape["context"], mesh.shape["dp"]
        ),
        mesh=mesh,
        in_specs=(shards, P(), P(), P(), P(), P(), experts, experts, rows, rows, shards),
        out_specs=(shards, shards, P(), P(), P(), P(), P(), experts, experts, P()),
        check_vma=False,
    )
```

```python
import functools
import jax
import jax.numpy as jnp
from jax import lax
from jax.experimental import pallas as pl
from jax.experimental.pallas import tpu as pltpu
from jax.sharding import PartitionSpec as P

HEADS = 8
NEG_FILL = -1e30
MESH = pl.DeviceIdType.MESH
BF = jnp.bfloat16
F32 = jnp.float32
ANY = pl.BlockSpec(memory_space=pl.ANY)
VM = pl.BlockSpec(memory_space=pltpu.VMEM)
VMEM_LIMIT = 60 * 1024 * 1024


def dot(a, b, dims=((1,), (0,))):
    return lax.dot_general(a, b, (dims, ((), ())), preferred_element_type=F32)


def normalized(x):
    center = x - jnp.mean(x, -1, keepdims=True)
    spread = jnp.mean(center * center, -1, keepdims=True)
    rstd = lax.rsqrt(spread + 1e-05)
    return center * rstd, rstd


def ring(n_expert, n_context):
    e = lax.axis_index("expert")
    c = lax.axis_index("context")
    n = n_expert * n_context
    me = e * n_context + c

    def peer(k):
        j = lax.rem(me + k, n)
        pe = lax.div(j, n_context)
        pc = lax.rem(j, n_context)
        return j, pe, pc

    return e, c, me, n, peer


def enter(peer, n, reduce=None):
    barrier = pltpu.get_barrier_semaphore()
    for k in range(1, n):
        _, pe, pc = peer(k)
        pl.semaphore_signal(
            barrier, inc=1, device_id={"expert": pe, "context": pc}, device_id_type=MESH
        )
    extra = 0 if reduce is None else reduce.greet()
    pl.semaphore_wait(barrier, n - 1 + extra)


class Reduce:
    def __init__(self, own, rin, lin, ring_r, ring_l, sems, sums, base, lag, n_dp, n_context):
        self.lag = lag
        self.own, self.ins, self.rings, self.sums = own, (rin, lin), (ring_r, ring_l), sums
        self.send, self.recv, self.swap_s, self.swap_r, self.keep = sems
        self.count, self.slots = own.shape[0], ring_r.shape[0]
        self.n_dp, self.n_context, self.base = n_dp, n_context, base
        self.z, self.c = lax.axis_index("dp"), lax.axis_index("context")

    def greet(self):
        barrier = pltpu.get_barrier_semaphore()
        z, last = self.z, self.n_dp - 1
        for here, to in ((z > 0, z - 1), (z < last, z + 1)):

            @pl.when(here)
            def _():
                pl.semaphore_signal(barrier, inc=1, device_id={"dp": to}, device_id_type=MESH)

        return jnp.minimum(z, 1) + jnp.minimum(last - z, 1)

    def hop(self, way, i):
        to = self.z + (1 if way == 0 else -1)
        slot = lax.rem(i, self.slots)
        return pltpu.make_async_remote_copy(
            src_ref=self.rings[way].at[slot], dst_ref=self.ins[way].at[i],
            send_sem=self.send.at[way, slot], recv_sem=self.recv.at[way, i],
            device_id={"dp": to}, device_id_type=MESH,
        )

    def swaps(self, i):
        out = []
        for k in range(1, self.n_context):
            pc = lax.rem(self.c + k, self.n_context)
            out.append(
                pltpu.make_async_remote_copy(
                    src_ref=self.own.at[i], dst_ref=self.sums.at[self.c, self.base + i],
                    send_sem=self.swap_s.at[k, i], recv_sem=self.swap_r.at[k, i],
                    device_id={"context": pc}, device_id_type=MESH,
                )
            )
        out.append(
            pltpu.make_async_copy(
                self.own.at[i], self.sums.at[self.c, self.base + i], self.keep.at[i]
            )
        )
        return out

    def tick(self, t, swap=True):
        last = self.n_dp - 1
        for way in range(2):
            behind = self.z if way == 0 else last - self.z
            i = t - self.lag * behind
            has_in, has_out = behind > 0, behind < last

            @pl.when((i >= 0) & (i < self.count))
            def _():
                @pl.when(has_in)
                def _():
                    self.hop(way, i).wait_recv()

                @pl.when(has_out)
                def _():
                    @pl.when(i >= self.slots)
                    def _():
                        self.hop(way, i - self.slots).wait_send()

                    slot = lax.rem(i, self.slots)

                    @pl.when(has_in)
                    def _():
                        self.rings[way][slot] = (
                            self.ins[way][i].astype(F32) + self.own[i].astype(F32)
                        ).astype(BF)

                    @pl.when(jnp.logical_not(has_in))
                    def _():
                        self.rings[way][slot] = self.own[i]

                    self.hop(way, i).start()

        m = t - self.lag * jnp.maximum(self.z, last - self.z)

        @pl.when((m >= 0) & (m < self.count))
        def _():
            first, final = self.z == 0, self.z == last

            @pl.when(first)
            def _():
                self.own[m] = (self.own[m].astype(F32) + self.ins[1][m].astype(F32)).astype(BF)

            @pl.when(final)
            def _():
                self.own[m] = (self.own[m].astype(F32) + self.ins[0][m].astype(F32)).astype(BF)

            @pl.when(jnp.logical_not(first | final))
            def _():
                self.own[m] = (
                    self.own[m].astype(F32) + self.ins[0][m].astype(F32) + self.ins[1][m].astype(F32)
                ).astype(BF)

            if swap:
                for cp in self.swaps(m):
                    cp.start()

    def release(self, t):
        done = jnp.minimum(t - self.lag * jnp.maximum(self.z, self.n_dp - 1 - self.z), self.count)

        def one(m, _):
            @pl.when(m < done)
            def _():
                for cp in self.swaps(m):
                    cp.start()

            return 0

        lax.fori_loop(0, self.count, one, 0)

    def finish(self, t):
        lax.fori_loop(t, self.count + self.lag * (self.n_dp - 1), lambda i, _: (self.tick(i), 0)[1], 0)
        last = self.n_dp - 1
        for way in range(2):

            @pl.when((self.z if way == 0 else last - self.z) < last)
            def _():
                for i in range(max(0, self.count - self.slots), self.count):
                    self.hop(way, i).wait_send()

        def drain(i, _):
            for cp in self.swaps(i):
                cp.wait()
            return 0

        lax.fori_loop(0, self.count, drain, 0)


def reduce_scratch(count, n_context, slots=4):
    sem = pltpu.SemaphoreType.DMA
    block = pltpu.VMEM((count, 128, 512), BF)
    ring_block = pltpu.VMEM((slots, 128, 512), BF)
    return [
        block, block, ring_block, ring_block,
        sem((2, slots)), sem((2, count)), sem((n_context, count)), sem((n_context, count)), sem((count,)),
    ]


def mask_bias(bias, kmark, qmark, s, q0, qn):
    kk = q0 + qn
    place_k = lax.broadcasted_iota(jnp.int32, (kk, qn), 0)
    place_q = lax.broadcasted_iota(jnp.int32, (kk, qn), 1) + q0
    same = kmark[s, pl.ds(0, kk), :] == qmark[s, :, pl.ds(q0, qn)]
    bias[pl.ds(0, kk), :] = jnp.where(same & (place_k <= place_q), 0.0, NEG_FILL)


def forward_kernel(
    tokens, cot, kmark, qmark, live, gain, wqkv, wout,
    resid_m, cot_m, live_m, tok_a, qkv_o, att_o, lse_o, sq_o,
    tok, qkv, vt, att, att_t, res, bias,
    tok_s, tok_r, cot_s, cot_r, res_s, res_r, live_s, live_r, own_s, save_s,
    *, n_expert, n_context,
):
    e, c, me, n, peer = ring(n_expert, n_context)
    seqs, length, width = qkv_o.shape[0], qkv_o.shape[1], tokens.shape[-1]
    half = length // n_context
    slab = half // n_expert
    qn = 256
    enter(peer, n)
    def outgoing(s):
        out = []
        for k in range(1, n_context):
            pc = lax.rem(c + k, n_context)
            out.append(
                pltpu.make_async_remote_copy(
                    src_ref=tokens.at[pc, s], dst_ref=tok.at[s, c],
                    send_sem=tok_s.at[s, k], recv_sem=tok_r.at[s, k],
                    device_id={"context": pc}, device_id_type=MESH,
                )
            )
        return out

    for cp in outgoing(0):
        cp.start()
    own = []
    for s in range(seqs):
        cp = pltpu.make_async_copy(tokens.at[c, s], tok.at[s, c], own_s.at[s])
        cp.start()
        own.append(cp)

    def project(s, h):
        x = tok[s, h].astype(F32)
        y, _ = normalized(x)
        a = (y * gain[...]).astype(BF)
        at = pl.ds(pl.multiple_of(h * half, half), half)
        qkv[s, at, :] = dot(a, wqkv[...]).astype(BF)
        vt[s, :, at] = dot(wqkv[:, pl.ds(2 * width, width)], a, ((0,), (1,))).astype(BF)

    for s in range(seqs):
        own[s].wait()
        project(s, c)
    for cp in outgoing(0):
        cp.wait()
    for s in range(1, seqs):
        for cp in outgoing(s):
            cp.start()
    mine = pl.ds(e * seqs, seqs)
    local = [pltpu.make_async_copy(live, live_m.at[mine], own_s.at[seqs + 1])]
    crossing = []
    for k in range(1, n_expert):
        pe = lax.rem(e + k, n_expert)
        crossing.append(
            pltpu.make_async_remote_copy(
                src_ref=live, dst_ref=live_m.at[mine], send_sem=live_s.at[k], recv_sem=live_r.at[k],
                device_id={"expert": pe}, device_id_type=MESH,
            )
        )
    for k in range(1, n):
        j, pe, pc = peer(k)
        crossing.append(
            pltpu.make_async_remote_copy(
                src_ref=cot.at[pc, :, pl.ds(pl.multiple_of(pe * slab, slab), slab), :],
                dst_ref=cot_m.at[mine, c],
                send_sem=cot_s.at[k], recv_sem=cot_r.at[k],
                device_id={"expert": pe, "context": pc}, device_id_type=MESH,
            )
        )
    local.append(
        pltpu.make_async_copy(
            cot.at[c, :, pl.ds(pl.multiple_of(e * slab, slab), slab), :],
            cot_m.at[mine, c], own_s.at[seqs],
        )
    )
    for cp in local:
        cp.start()
    saves = [
        pltpu.make_async_copy(qkv, qkv_o, save_s.at[0]),
        pltpu.make_async_copy(tok, tok_a, save_s.at[1]),
    ]
    lane = lax.broadcasted_iota(jnp.int32, (qn, 128), 1)
    moving = []
    total = jnp.zeros((1, width), F32)
    for s in range(seqs):
        if 0 < s < seqs - 1:
            for cp in outgoing(s):
                cp.wait()
        for k in range(1, n_context):
            project(s, lax.rem(c + k, n_context))
        if s == seqs - 1:
            for cp in saves:
                cp.start()
        for qb in range(length // qn):
            if s == max(0, seqs - 2) and qb * 2 == length // qn:
                for later in range(s + 1, seqs):
                    for cp in outgoing(later):
                        cp.wait()
                for cp in crossing:
                    cp.start()
            kk = (qb + 1) * qn
            rows = pl.ds(qb * qn, qn)
            mask_bias(bias, kmark, qmark, s, qb * qn, qn)

            for at in range(0, width, 128):
                q2 = qkv[s, rows, pl.ds(at, 128)] * BF(0.125)
                k2 = qkv[s, pl.ds(0, kk), pl.ds(width + at, 128)]
                outs = []
                for h in range(2):
                    mine = (lane >= 64) if h else (lane < 64)
                    qm = jnp.where(mine, q2, jnp.zeros_like(q2))
                    st = dot(k2, qm, ((1,), (1,))) + bias[pl.ds(0, kk), :]
                    top = jnp.max(st, 0, keepdims=True)
                    p = jnp.exp(st - top)
                    tot = jnp.sum(p, 0, keepdims=True)
                    lse_o[s, pl.ds(at // 64 + h, 1), rows] = top + jnp.log(tot)
                    vh = vt[s, pl.ds(at + 64 * h, 64), pl.ds(0, kk)]
                    outs.append(dot(vh, p.astype(BF)) * (1.0 / tot))
                both = jnp.concatenate(outs, 0)
                att_t[s, pl.ds(at, 128), rows] = both.astype(BF)
                att[s, rows, pl.ds(at, 128)] = both.T.astype(BF)
            h = qb * qn // half
            attn_out = dot(att[s, rows, :], wout[...])
            within = qb * qn - h * half
            x = tok[s, h, pl.ds(within, qn), :].astype(F32)
            res[s, h, pl.ds(within, qn), :] = (x + attn_out).astype(BF)
            ok = kmark[s, rows, :] >= 0
            total += jnp.sum(jnp.where(ok, attn_out * attn_out, 0.0), 0, keepdims=True)
            if (qb + 1) * qn == (h + 1) * half:
                for k in range(1, n_expert):
                    pe = lax.rem(e + k, n_expert)
                    cp = pltpu.make_async_remote_copy(
                        src_ref=res.at[s, h, pl.ds(pl.multiple_of(pe * slab, slab), slab), :],
                        dst_ref=resid_m.at[e * seqs + s, h],
                        send_sem=res_s.at[s, h, k], recv_sem=res_r.at[s, h, k],
                        device_id={"expert": pe}, device_id_type=MESH,
                    )
                    cp.start()
                    moving.append(cp)
                cp = pltpu.make_async_copy(
                    res.at[s, h, pl.ds(pl.multiple_of(e * slab, slab), slab), :],
                    resid_m.at[e * seqs + s, h], res_s.at[s, h, 0],
                )
                cp.start()
                moving.append(cp)
    sq_o[...] = total
    keep = pltpu.make_async_copy(att_t, att_o, save_s.at[2])
    keep.start()
    for cp in saves + moving + crossing + local + [keep]:
        cp.wait()


def forward(tokens, cot, kmark, qmark, live, gain, wqkv, wout, n_expert, n_context):
    reps, seqs, half, width = tokens.shape
    length = half * n_context
    slab = half // n_expert
    group = seqs * n_expert
    n = n_expert * n_context
    sem = pltpu.SemaphoreType.DMA
    return pl.pallas_call(
        functools.partial(forward_kernel, n_expert=n_expert, n_context=n_context),
        out_shape=(
            jax.ShapeDtypeStruct((group, n_context, slab, width), BF),
            jax.ShapeDtypeStruct((group, n_context, slab, width), BF),
            jax.ShapeDtypeStruct((group, *live.shape[1:]), F32),
            jax.ShapeDtypeStruct((seqs, n_context, half, width), BF),
            jax.ShapeDtypeStruct((seqs, length, 3 * width), BF),
            jax.ShapeDtypeStruct((seqs, width, length), BF),
            jax.ShapeDtypeStruct((seqs, HEADS, length), F32),
            jax.ShapeDtypeStruct((1, width), F32),
        ),
        in_specs=[ANY, ANY, VM, VM, VM, VM, VM, VM],
        out_specs=(ANY, ANY, ANY, ANY, ANY, ANY, VM, VM),
        scratch_shapes=[
            pltpu.VMEM((seqs, n_context, half, width), BF),
            pltpu.VMEM((seqs, length, 3 * width), BF),
            pltpu.VMEM((seqs, width, length), BF),
            pltpu.VMEM((seqs, length, width), BF),
            pltpu.VMEM((seqs, width, length), BF),
            pltpu.VMEM((seqs, n_context, half, width), BF),
            pltpu.VMEM((length, 256), F32),
            sem((seqs, n_context)), sem((seqs, n_context)),
            sem((n,)), sem((n,)),
            sem((seqs, n_context, n_expert)), sem((seqs, n_context, n_expert)),
            sem((n_expert,)), sem((n_expert,)),
            sem((seqs + 2,)), sem((3,)),
        ],
        compiler_params=pltpu.CompilerParams(
            collective_id=0, has_side_effects=True, vmem_limit_bytes=VMEM_LIMIT
        ),
        name="attend_forward",
    )(tokens, cot, kmark, qmark, live, gain, wqkv, wout)


def mix_kernel(
    resid_m, cot_m, live_m, gain, wc, w_in, w_back,
    d_attn, out_m, part_o, sums, gc_o, gm_o, sq_o,
    res, cot, u, wts, mixed, dexp, xs, des, eos, dms, eor, dmr, win, wback, acts, d_pres, glow,
    go_s, go_r, back_s, back_r, at_s, at_r, in_s, save_s, *rest,
    n_expert, n_context, n_dp, early,
):
    e, c, me, n, peer = ring(n_expert, n_context)
    group, halves, slab, width = res.shape
    seqs = group // n_expert
    ff = win.shape[1]
    experts = n
    span = max(16, 256 // group)
    steps = slab // span
    chunk = 512 // slab
    reduce = Reduce(
        glow.at[pl.ds(0, early)], *rest[:4], rest[4:], sums, 0, 2, n_dp, n_context
    )
    loads = [
        pltpu.make_async_copy(resid_m, res, in_s.at[0]),
        pltpu.make_async_copy(cot_m, cot, in_s.at[1]),
        pltpu.make_async_copy(w_in.at[c], win, in_s.at[2]),
        pltpu.make_async_copy(w_back.at[c], wback, in_s.at[3]),
    ]
    for cp in loads:
        cp.start()
    enter(peer, n, reduce)
    rows, cols = group * span, experts * span
    spread = (
        lax.broadcasted_iota(jnp.int32, (experts, cols), 1) // span
        == lax.broadcasted_iota(jnp.int32, (experts, cols), 0)
    ).astype(BF)
    gather = (
        lax.broadcasted_iota(jnp.int32, (cols, experts), 0) // span
        == lax.broadcasted_iota(jnp.int32, (cols, experts), 1)
    ).astype(BF)
    diag = lax.rem(lax.broadcasted_iota(jnp.int32, (rows, cols), 0), span) == lax.rem(
        lax.broadcasted_iota(jnp.int32, (rows, cols), 1), span
    )

    def filled(h, g):
        place = lax.broadcasted_iota(jnp.int32, (group, span, 1), 1) + (
            (h * n_expert + e) * slab + g * span
        )
        ok = place.astype(F32) < live_m[:, pl.ds(0, 1), pl.ds(0, 1)]
        return jnp.where(ok, 1.0, 0.0).reshape(rows, 1) > 0

    loads[0].wait()
    loads[1].wait()
    sent = []
    for h in range(halves):

        def first(g, _):
            at = pl.ds(pl.multiple_of(g * span, span), span)
            r = res[:, h, at, :].reshape(rows, width).astype(F32)
            normed, _ = normalized(r)
            ug = (normed * gain[...]).astype(BF)
            u[:, h, at, :] = ug.reshape(group, span, width)
            logits = jnp.where(filled(h, g), dot(ug, wc[...]), NEG_FILL).reshape(group, span, experts)
            ex = jnp.exp(logits - jnp.max(logits, 0, keepdims=True))
            w = (ex / jnp.sum(ex, 0, keepdims=True)).reshape(rows, experts)
            wts[h * steps + g] = w
            wide = jnp.where(diag, dot(w.astype(BF), spread), 0.0).astype(BF)
            cg = cot[:, h, at, :].reshape(rows, width)
            mixed[h, :, at, :] = dot(wide, ug, ((0,), (0,))).astype(BF).reshape(experts, span, width)
            dexp[h, :, at, :] = dot(wide, cg, ((0,), (0,))).astype(BF).reshape(experts, span, width)
            return 0

        lax.fori_loop(0, steps, first, 0)
        for i, (src, dst) in enumerate(((mixed, xs), (dexp, des))):
            dst[h, 0] = src[h, me]
            for k in range(1, n):
                j, pe, pc = peer(k)
                cp = pltpu.make_async_remote_copy(
                    src_ref=src.at[h, j], dst_ref=dst.at[h, k],
                    send_sem=go_s.at[i, h, k], recv_sem=go_r.at[i, h, k],
                    device_id={"expert": pe, "context": pc}, device_id_type=MESH,
                )
                cp.start()
                sent.append((i, h, k, cp))
    loads[2].wait()
    loads[3].wait()
    tile = 512
    returned = []
    for h in range(halves):
        for kg in range(n // chunk):
            slots = range(kg * chunk, (kg + 1) * chunk)
            for i, hh, k, cp in sent:
                if hh == h and k in slots:
                    cp.wait_recv()
            x = xs[h, pl.ds(kg * chunk, chunk)].reshape(chunk * slab, width)
            de = des[h, pl.ds(kg * chunk, chunk)].reshape(chunk * slab, width)
            base = (h * (n // chunk) + kg) * chunk * slab

            def expert_tile(f, carry):
                eo, dm = carry
                at = pl.ds(pl.multiple_of(f * tile, tile), tile)
                pre = dot(x, win[:, at])
                sq = pre * pre
                t = jnp.tanh(0.7978845608028654 * pre * (1.0 + 0.044715 * sq))
                act = (0.5 * pre * (1.0 + t)).astype(BF)
                slope = 0.5 * (1.0 + t) + 0.5 * pre * (1.0 - t * t) * (
                    0.7978845608028654 * (1.0 + 3 * 0.044715 * sq)
                )
                d_pre = (slope * dot(de, wback[at, :], ((1,), (1,)))).astype(BF)
                acts[pl.ds(base, chunk * slab), at] = act
                d_pres[pl.ds(base, chunk * slab), at] = d_pre
                return eo + dot(act, wback[at, :]), dm + dot(d_pre, win[:, at], ((1,), (1,)))

            zero = jnp.zeros((chunk * slab, width), F32)
            eo, dm = lax.fori_loop(0, ff // tile, expert_tile, (zero, zero))
            eos[h, pl.ds(kg * chunk, chunk)] = eo.astype(BF).reshape(chunk, slab, width)
            dms[h, pl.ds(kg * chunk, chunk)] = dm.astype(BF).reshape(chunk, slab, width)
            for i, (src, dst) in enumerate(((eos, eor), (dms, dmr))):
                for k in slots:
                    if k == 0:
                        dst[h, me] = src[h, 0]
                        continue
                    j, pe, pc = peer(n - k)
                    cp = pltpu.make_async_remote_copy(
                        src_ref=src.at[h, k], dst_ref=dst.at[h, me],
                        send_sem=back_s.at[i, h, k], recv_sem=back_r.at[i, h, k],
                        device_id={"expert": pe, "context": pc}, device_id_type=MESH,
                    )
                    cp.start()
                    returned.append((i, h, k, cp))
    per = width // 128
    tokens = halves * n * slab

    def grad_tile(f, _):
        at = pl.ds(pl.multiple_of(f * tile, tile), tile)
        g = dot(xs[...].reshape(tokens, width), d_pres[:, at], ((0,), (0,)))
        glow[pl.ds(f * per, per)] = g.astype(BF).reshape(per, 128, tile)
        g = dot(acts[:, at], des[...].reshape(tokens, width), ((0,), (0,)))
        glow[pl.ds((ff // tile + f) * per, per)] = g.astype(BF).reshape(per, 128, width)
        reduce.tick(f, swap=False)
        return 0

    lax.fori_loop(0, ff // tile, grad_tile, 0)
    blocks = glow.shape[0]
    out, dat = mixed, dexp
    for _, _, _, sending in sent:
        sending.wait_send()
    keep = [
        pltpu.make_async_copy(glow.at[pl.ds(early, blocks - early)], part_o, save_s.at[0])
    ]
    keep[0].start()
    gc_o[...] = jnp.zeros_like(gc_o)
    gm_o[...] = jnp.zeros_like(gm_o)
    sq_o[...] = jnp.zeros_like(sq_o)
    moving = []
    for h in range(halves):
        for i, hh, k, cp in returned:
            if hh == h:
                cp.wait_recv()
        if h == halves - 1:
            reduce.release(ff // tile + h * steps)

        def second(g, _):
            at = pl.ds(pl.multiple_of(g * span, span), span)
            r = res[:, h, at, :].reshape(rows, width).astype(F32)
            normed, rstd = normalized(r)
            ug = u[:, h, at, :].reshape(rows, width)
            cg = cot[:, h, at, :].reshape(rows, width)
            ok = filled(h, g)
            eg = eor[h, :, at, :].reshape(cols, width)
            dg = dmr[h, :, at, :].reshape(cols, width)
            w = wts[h * steps + g]
            wide = jnp.where(diag, dot(w.astype(BF), spread), 0.0).astype(BF)
            mix = dot(wide, eg)
            full = r + mix
            out[h, :, at, :] = full.astype(BF).reshape(group, span, width)
            sq_o[pl.ds(0, 1), :] += jnp.sum(jnp.where(ok, full * full, 0.0), 0, keepdims=True)
            sq_o[pl.ds(1, 1), :] += jnp.sum(jnp.where(ok, mix * mix, 0.0), 0, keepdims=True)
            dw = jnp.where(diag, dot(cg, eg, ((1,), (1,))) + dot(ug, dg, ((1,), (1,))), 0.0)
            high = dw.astype(BF)
            rest = (dw - high.astype(F32)).astype(BF)
            dw = dot(high, gather) + dot(rest, gather)
            inner = jnp.sum((w * dw).reshape(group, span, experts), 0, keepdims=True)
            d_log = (
                (w.reshape(group, span, experts) * (dw.reshape(group, span, experts) - inner))
                .reshape(rows, experts)
                .astype(BF)
            )
            gc_o[...] += dot(ug, d_log, ((0,), (0,)))
            d_u = dot(d_log, wc[...], ((1,), (1,))) + dot(wide, dg)
            gm_o[...] += jnp.sum(d_u * normed, 0, keepdims=True)
            q = d_u * gain[...]
            d_res = cg.astype(F32) + rstd * (
                q - jnp.mean(q, -1, keepdims=True) - normed * jnp.mean(q * normed, -1, keepdims=True)
            )
            dat[h, :, at, :] = d_res.astype(BF).reshape(group, span, width)
            reduce.tick(ff // tile + h * steps + g, swap=h == halves - 1)
            return 0

        lax.fori_loop(0, steps, second, 0)
        mine = pl.ds(pl.multiple_of(e * slab, slab), slab)
        for k in range(1, n_expert):
            pe = lax.rem(e + k, n_expert)
            cp = pltpu.make_async_remote_copy(
                src_ref=dat.at[h, pl.ds(pe * seqs, seqs)], dst_ref=d_attn.at[:, h, mine, :],
                send_sem=at_s.at[h, k], recv_sem=at_r.at[h, k],
                device_id={"expert": pe}, device_id_type=MESH,
            )
            cp.start()
            moving.append(cp)
        cp = pltpu.make_async_copy(
            dat.at[h, pl.ds(e * seqs, seqs)], d_attn.at[:, h, mine, :], at_s.at[h, 0]
        )
        cp.start()
        moving.append(cp)
    cp = pltpu.make_async_copy(out, out_m, save_s.at[2])
    cp.start()
    for _, _, _, sending in returned:
        sending.wait_send()
    reduce.finish(ff // tile + halves * steps)
    for cp in moving + keep + [cp]:
        cp.wait()


def mix(resid_m, cot_m, live_m, gain, wc, w_in, w_back, n_expert, n_context, n_dp, early):
    group, halves, slab, width = resid_m.shape
    seqs = group // n_expert
    n = n_expert * n_context
    ff = w_in.shape[-1]
    span = max(16, 256 // group)
    steps = slab // span
    blocks = 2 * width * ff // (128 * 512)
    sem = pltpu.SemaphoreType.DMA
    block = pltpu.VMEM((group, halves, slab, width), BF)
    turned = pltpu.VMEM((halves, n, slab, width), BF)
    return pl.pallas_call(
        functools.partial(
            mix_kernel, n_expert=n_expert, n_context=n_context, n_dp=n_dp, early=early
        ),
        out_shape=(
            jax.ShapeDtypeStruct((seqs, halves, slab * n_expert, width), BF),
            jax.ShapeDtypeStruct((halves, group, slab, width), BF),
            jax.ShapeDtypeStruct((blocks - early, 128, 512), BF),
            jax.ShapeDtypeStruct((n_context, blocks, 128, 512), BF),
            jax.ShapeDtypeStruct((width, n), F32),
            jax.ShapeDtypeStruct((1, width), F32),
            jax.ShapeDtypeStruct((2, width), F32),
        ),
        in_specs=[ANY, ANY, VM, VM, VM, ANY, ANY],
        out_specs=(ANY, ANY, ANY, ANY, VM, VM, VM),
        scratch_shapes=[
            block, block, block,
            pltpu.VMEM((halves * steps, group * span, n), F32),
            turned, turned, turned, turned, turned, turned, turned, turned,
            pltpu.VMEM((width, ff), BF), pltpu.VMEM((ff, width), BF),
            pltpu.VMEM((halves * n * slab, ff), BF), pltpu.VMEM((halves * n * slab, ff), BF),
            pltpu.VMEM((blocks, 128, 512), BF),
            sem((2, halves, n)), sem((2, halves, n)),
            sem((2, halves, n)), sem((2, halves, n)),
            sem((halves, n_expert)), sem((halves, n_expert)),
            sem((4,)), sem((3,)),
            *reduce_scratch(early, n_context),
        ],
        compiler_params=pltpu.CompilerParams(
            collective_id=1, has_side_effects=True, vmem_limit_bytes=63 * 1024 * 1024
        ),
        name="mix_and_experts",
    )(resid_m, cot_m, live_m, gain, wc, w_in, w_back)


def backward_kernel(
    d_attn, tok_a, qkv_a, att_a, lse, kmark, qmark, gain, wqkv, wout, out_m, part, sums_in,
    dtok_o, last_o, out_o, sums, gq_o, go_o, gg_o,
    da, tok, qkv, att, datt, delta, dkv, dqkv, dtok, bias, own,
    out_s, out_r, tok_s, tok_r, in_s, own_s, *rest,
    n_expert, n_context, n_dp, base,
):
    e, c, me, n, peer = ring(n_expert, n_context)
    seqs, length, width = da.shape
    half = length // n_context
    slab = half // n_expert
    qn = 256
    loads = [
        pltpu.make_async_copy(src, dst, in_s.at[i])
        for i, (src, dst) in enumerate(
            ((d_attn, da), (att_a, att), (qkv_a, qkv), (tok_a, tok),
             (part.at[pl.ds(0, own.shape[0])], own))
        )
    ]
    reduce = Reduce(own, *rest[:4], rest[4:], sums, base, 2, n_dp, n_context)
    for cp in loads:
        cp.start()
    enter(peer, n, reduce)
    crossing = []
    mine = pl.ds(pl.multiple_of(e * slab, slab), slab)
    for k in range(1, n):
        j, pe, pc = peer(k)
        cp = pltpu.make_async_remote_copy(
            src_ref=out_m.at[pc, pl.ds(pe * seqs, seqs)], dst_ref=out_o.at[c, :, mine, :],
            send_sem=out_s.at[k], recv_sem=out_r.at[k],
            device_id={"expert": pe, "context": pc}, device_id_type=MESH,
        )
        cp.start()
        crossing.append(cp)
    cp = pltpu.make_async_copy(
        out_m.at[c, pl.ds(e * seqs, seqs)], out_o.at[c, :, mine, :], own_s.at[0, 0]
    )
    cp.start()
    crossing.append(cp)
    lane = lax.broadcasted_iota(jnp.int32, (qn, 128), 1)
    gg_o[...] = jnp.zeros_like(gg_o)
    for cp in loads:
        cp.wait()
    pairs = width // 128
    for s in range(seqs):
        datt[...] = dot(da[s], wout[...], ((1,), (1,))).astype(BF)
        turned = dot(wout[...], da[s], ((1,), (1,))).astype(BF).astype(F32) * att[s].astype(F32)
        delta[...] = jnp.sum(turned.reshape(HEADS, width // HEADS, length), 1)
        go = dot(att[s], da[s])
        go_o[...] = go if s == 0 else go_o[...] + go
        dkv[...] = jnp.zeros_like(dkv)
        for qb in range(length // qn):
            kk = (qb + 1) * qn
            rows = pl.ds(qb * qn, qn)
            mask_bias(bias, kmark, qmark, s, qb * qn, qn)

            def pair(hp, _):
                at = pl.multiple_of(hp * 128, 128)
                q2 = qkv[s, rows, pl.ds(at, 128)] * BF(0.125)
                k2 = qkv[s, pl.ds(0, kk), pl.ds(width + at, 128)]
                v2 = qkv[s, pl.ds(0, kk), pl.ds(2 * width + at, 128)]
                do2 = datt[rows, pl.ds(at, 128)]
                kt = k2.T
                dqs, dss, lows, qms, doms = [], [], [], [], []
                for h in range(2):
                    mine = (lane >= 64) if h else (lane < 64)
                    qm = jnp.where(mine, q2, jnp.zeros_like(q2))
                    dom = jnp.where(mine, do2, jnp.zeros_like(do2))
                    st = dot(k2, qm, ((1,), (1,))) + bias[pl.ds(0, kk), :]
                    p = jnp.exp(st - lse[s, pl.ds(2 * hp + h, 1), rows])
                    dp = dot(v2, dom, ((1,), (1,)))
                    ds = (p * (dp - delta[pl.ds(2 * hp + h, 1), rows])).astype(BF)
                    dqs.append(dot(kt[h * 64 : h * 64 + 64], ds))
                    dss.append(ds)
                    lows.append(p.astype(BF))
                    qms.append(qm)
                    doms.append(dom)
                dqkv[rows, pl.ds(at, 128)] = (
                    (jnp.concatenate(dqs, 0) * 0.125).T.astype(BF)
                )
                dkv[pl.ds(0, kk), pl.ds(at, 128)] += dot(dss[0], qms[0]) + dot(dss[1], qms[1])
                dkv[pl.ds(0, kk), pl.ds(width + at, 128)] += dot(lows[0], doms[0]) + dot(
                    lows[1], doms[1]
                )
                @pl.when(lax.rem(hp, 2) == 1)
                def _():
                    reduce.tick(((s * (length // qn) + qb) * pairs + hp) // 2)

                return 0

            lax.fori_loop(0, pairs, pair, 0)
        dqkv[:, pl.ds(width, 2 * width)] = dkv[...].astype(BF)
        for h in range(n_context):
            rows = pl.ds(h * half, half)
            normed, rstd = normalized(tok[s, h].astype(F32))
            a = (normed * gain[...]).astype(BF)
            gq = dot(a, dqkv[rows, :], ((0,), (0,)))
            gq_o[...] = gq if s == 0 and h == 0 else gq_o[...] + gq
            d_a = dot(dqkv[rows, :], wqkv[...], ((1,), (1,)))
            gg_o[...] += jnp.sum(d_a * normed, 0, keepdims=True)
            q = d_a * gain[...]
            dt = da[s, rows, :].astype(F32) + rstd * (
                q - jnp.mean(q, -1, keepdims=True) - normed * jnp.mean(q * normed, -1, keepdims=True)
            )
            dtok[s, h] = dt.astype(BF)
        if s == seqs - 1:
            cp = pltpu.make_async_copy(dtok.at[s], last_o, own_s.at[0, 1])
            cp.start()
            crossing.append(cp)
            continue
        for k in range(1, n_context):
            pc = lax.rem(c + k, n_context)
            cp = pltpu.make_async_remote_copy(
                src_ref=dtok.at[s, pc], dst_ref=dtok_o.at[c, s],
                send_sem=tok_s.at[s, k], recv_sem=tok_r.at[s, k],
                device_id={"context": pc}, device_id_type=MESH,
            )
            cp.start()
            crossing.append(cp)
        cp = pltpu.make_async_copy(dtok.at[s, c], dtok_o.at[c, s], own_s.at[1, s])
        cp.start()
        crossing.append(cp)
    reduce.finish(seqs * (length // qn) * pairs // 2)
    for cp in crossing:
        cp.wait()


def backward(
    d_attn, tok_a, qkv, att, lse, kmark, qmark, gain, wqkv, wout, out_m, part, sums,
    n_expert, n_context, n_dp, count,
):
    seqs, length, width = d_attn.shape
    half = length // n_context
    n = n_expert * n_context
    sem = pltpu.SemaphoreType.DMA
    return pl.pallas_call(
        functools.partial(
            backward_kernel, n_expert=n_expert, n_context=n_context, n_dp=n_dp,
            base=sums.shape[1] - part.shape[0],
        ),
        out_shape=(
            jax.ShapeDtypeStruct((n_context, seqs, half, width), BF),
            jax.ShapeDtypeStruct((n_context, half, width), BF),
            jax.ShapeDtypeStruct((n_context, seqs, half, width), BF),
            jax.ShapeDtypeStruct(sums.shape, BF),
            jax.ShapeDtypeStruct((width, 3 * width), F32),
            jax.ShapeDtypeStruct((width, width), F32),
            jax.ShapeDtypeStruct((1, width), F32),
        ),
        in_specs=[ANY, ANY, ANY, ANY, VM, VM, VM, VM, VM, VM, ANY, ANY, ANY],
        out_specs=(ANY, ANY, ANY, ANY, VM, VM, VM),
        input_output_aliases={12: 3},
        scratch_shapes=[
            pltpu.VMEM((seqs, length, width), BF),
            pltpu.VMEM((seqs, n_context, half, width), BF),
            pltpu.VMEM((seqs, length, 3 * width), BF),
            pltpu.VMEM((seqs, width, length), BF),
            pltpu.VMEM((length, width), BF),
            pltpu.VMEM((HEADS, length), F32),
            pltpu.VMEM((length, 2 * width), F32),
            pltpu.VMEM((length, 3 * width), BF),
            pltpu.VMEM((seqs, n_context, half, width), BF),
            pltpu.VMEM((length, 256), F32),
            pltpu.VMEM((count, *part.shape[1:]), BF),
            sem((n,)), sem((n,)),
            sem((seqs, n_context)), sem((seqs, n_context)),
            sem((5,)), sem((2, seqs)),
            *reduce_scratch(count, n_context),
        ],
        compiler_params=pltpu.CompilerParams(
            collective_id=2, has_side_effects=True, vmem_limit_bytes=VMEM_LIMIT
        ),
        name="attend_backward",
    )(d_attn, tok_a, qkv, att, lse, kmark, qmark, gain, wqkv, wout, out_m, part, sums)


def share_kernel(
    gq, go, misc, last, part_in, dtok_in, sums_in,
    gq_o, go_o, misc_o, dtok_o, sums,
    pack, other, chip, corners, along, whole, own,
    core_s, core_r, chip_s, chip_r, dp_s, dp_r, dp2_s, dp2_r, out_s, out_r, fin_s, fin_r, tok_s, tok_r, own_s, *rest,
    n_expert, n_context, n_dp,
):
    e, c, z = (lax.axis_index(a) for a in ("expert", "context", "dp"))
    core = lax.rem(e, 2)
    chips = n_expert // 2 * n_context
    me = lax.div(e, 2) * n_context + c
    width = go.shape[1]
    total = pack.shape[0]
    part = total // 2
    piece = part // chips
    lanes = width // n_dp
    twin = {"expert": e + 1 - 2 * core}

    def chip_at(k):
        j = lax.rem(me + k, chips)
        return j, {"expert": lax.div(j, n_context) * 2 + core, "context": lax.rem(j, n_context)}

    barrier = pltpu.get_barrier_semaphore()
    count = own.shape[0]
    load = pltpu.make_async_copy(
        part_in.at[pl.ds(part_in.shape[0] - count, count)], own, own_s.at[0]
    )
    load.start()
    reduce = Reduce(own, *rest[:4], rest[4:], sums, sums.shape[1] - count, 2, n_dp, n_context)
    ticks = [0]

    def tick(times):
        for _ in range(times):
            if ticks[0] < count + 2 * (n_dp - 1):
                reduce.tick(ticks[0])
                ticks[0] += 1

    seq = dtok_o.shape[1] - 1
    where = [twin] + [chip_at(k)[1] for k in range(1, chips)]
    where += [{"dp": lax.rem(z + k, n_dp)} for k in range(1, n_dp)]
    for to in where:
        pl.semaphore_signal(barrier, inc=1, device_id=to, device_id_type=MESH)
    for b in range(3):
        pack[pl.ds(b * width, width), :] = gq[:, pl.ds(b * width, width)].astype(BF)
    pack[pl.ds(3 * width, width), :] = go[...].astype(BF)
    more = total - 4 * width
    tail = misc[...]
    if more > tail.shape[0]:
        tail = jnp.concatenate((tail, jnp.zeros((more - tail.shape[0], width), F32)))
    pack[pl.ds(4 * width, more), :] = tail.astype(BF)
    pl.semaphore_wait(barrier, len(where))

    def remote(src, dst, ss, rs, to):
        cp = pltpu.make_async_remote_copy(
            src_ref=src, dst_ref=dst, send_sem=ss, recv_sem=rs, device_id=to, device_id_type=MESH
        )
        cp.start()
        return cp

    def rows(i, n):
        return pl.ds(pl.multiple_of(i * n, 16), n)

    bulk = [
        remote(
            last.at[lax.rem(c + k, n_context)], dtok_o.at[c, seq], tok_s.at[k], tok_r.at[k],
            {"context": lax.rem(c + k, n_context)},
        )
        for k in range(1, n_context)
    ]
    keep = pltpu.make_async_copy(last.at[c], dtok_o.at[c, seq], own_s.at[1])
    keep.start()
    sent = []
    for k in range(chips):
        j = lax.rem(me + k + 1, chips)
        at = pl.ds(pl.multiple_of((1 - core) * part + j * piece, 16), piece)
        sent.append(remote(pack.at[at], other.at[rows(j, piece)], core_s.at[k], core_r.at[k], twin))
    first = list(sent)
    for k in range(chips):
        j = lax.rem(me + k + 1, chips)
        first[k].wait_recv()
        at = pl.ds(pl.multiple_of(core * part + j * piece, 16), piece)
        chip[rows(j, piece), :] = (
            pack[at, :].astype(F32) + other[rows(j, piece), :].astype(F32)
        ).astype(BF)
        if k < chips - 1:
            _, to = chip_at(k + 1)
            sent.append(
                remote(chip.at[rows(j, piece)], corners.at[k], chip_s.at[k], chip_r.at[k], to)
            )
    load.wait()
    tick(4)
    acc = chip[rows(me, piece), :].astype(F32)
    for k in range(chips - 1):
        sent[chips + k].wait_recv()
        acc += corners[k].astype(F32)
    chip[rows(me, piece), :] = acc.astype(BF)
    mine = pl.ds(pl.multiple_of(z * lanes, lanes), lanes)
    steps = []
    for k in range(1, n_dp):
        to = lax.rem(z + k, n_dp)
        theirs = pl.ds(pl.multiple_of(to * lanes, lanes), lanes)
        steps.append(
            remote(
                chip.at[rows(me, piece), theirs], along.at[k - 1], dp_s.at[k - 1], dp_r.at[k - 1],
                {"dp": to},
            )
        )
    tick(2)
    acc = chip[rows(me, piece), mine].astype(F32)
    for k in range(1, n_dp):
        steps[k - 1].wait_recv()
        acc += along[k - 1].astype(F32)
    home = pl.ds(pl.multiple_of(core * part + me * piece, 16), piece)
    whole[home, mine] = acc.astype(BF)
    back = []
    for k in range(1, n_dp):
        to = lax.rem(z + k, n_dp)
        back.append(
            remote(
                whole.at[home, mine], whole.at[home, mine], dp2_s.at[k - 1], dp2_r.at[k - 1],
                {"dp": to},
            )
        )
    tick(2)
    for cp in back:
        cp.wait_recv()
    spread = [remote(whole.at[home], whole.at[home], fin_s.at[0], fin_r.at[0], twin)]
    outs = []
    for k in range(1, chips):
        _, to = chip_at(k)
        outs.append(remote(whole.at[home], whole.at[home], out_s.at[k - 1], out_r.at[k - 1], to))
    tick(3)
    for k in range(1, chips):
        outs[k - 1].wait_recv()
        tick(1)
        j = lax.rem(me + chips - k, chips)
        got = whole.at[pl.ds(pl.multiple_of(core * part + j * piece, 16), piece)]
        spread.append(remote(got, got, fin_s.at[k], fin_r.at[k], twin))
    for cp in spread:
        cp.wait_recv()
    for b in range(3):
        gq_o[:, pl.ds(b * width, width)] = whole[pl.ds(b * width, width), :].astype(F32)
    go_o[...] = whole[pl.ds(3 * width, width), :].astype(F32)
    misc_o[...] = whole[pl.ds(4 * width, misc_o.shape[0]), :].astype(F32)
    reduce.finish(ticks[0])
    for cp in sent + steps + back + outs + spread:
        cp.wait_send()
    for cp in bulk:
        cp.wait()
    keep.wait()


def share(gq, go, misc, last, part_in, dtok, sums, n_expert, n_context, n_dp, count):
    width = go.shape[1]
    chips = n_expert // 2 * n_context
    unit = 2 * chips * 16
    total = -(-(4 * width + misc.shape[0]) // unit) * unit
    part = total // 2
    piece = part // chips
    sem = pltpu.SemaphoreType.DMA
    return pl.pallas_call(
        functools.partial(share_kernel, n_expert=n_expert, n_context=n_context, n_dp=n_dp),
        out_shape=(
            jax.ShapeDtypeStruct(gq.shape, F32),
            jax.ShapeDtypeStruct(go.shape, F32),
            jax.ShapeDtypeStruct(misc.shape, F32),
            jax.ShapeDtypeStruct(dtok.shape, BF),
            jax.ShapeDtypeStruct(sums.shape, BF),
        ),
        in_specs=[VM, VM, VM, ANY, ANY, ANY, ANY],
        out_specs=(VM, VM, VM, ANY, ANY),
        input_output_aliases={5: 3, 6: 4},
        scratch_shapes=[
            pltpu.VMEM((total, width), BF),
            pltpu.VMEM((part, width), BF),
            pltpu.VMEM((part, width), BF),
            pltpu.VMEM((max(1, chips - 1), piece, width), BF),
            pltpu.VMEM((max(1, n_dp - 1), piece, width // n_dp), BF),
            pltpu.VMEM((total, width), BF),
            pltpu.VMEM((count, *sums.shape[2:]), BF),
            sem((chips,)), sem((chips,)), sem((chips,)), sem((chips,)),
            sem((n_dp,)), sem((n_dp,)), sem((n_dp,)), sem((n_dp,)),
            sem((chips,)), sem((chips,)), sem((chips,)), sem((chips,)),
            sem((n_context,)), sem((n_context,)), sem((2,)),
            *reduce_scratch(count, n_context),
        ],
        compiler_params=pltpu.CompilerParams(
            collective_id=3, has_side_effects=True, vmem_limit_bytes=VMEM_LIMIT
        ),
        name="share_gradients",
    )(gq, go, misc, last, part_in, dtok, sums)


def widen_kernel(src, gi, gb):
    f = pl.program_id(1)
    half = pl.num_programs(1) // 2

    @pl.when(f < half)
    def _():
        gi[0] = src[0].reshape(gi.shape[1:]).astype(F32)

    @pl.when(f >= half)
    def _():
        gb[0] = src[0].reshape(gb.shape[1:]).astype(F32)


def widen(sums, width, ff):
    n_context, blocks = sums.shape[:2]
    tiles = ff // 512
    per = blocks // (2 * tiles)
    return pl.pallas_call(
        widen_kernel,
        grid=(n_context, 2 * tiles),
        out_shape=(
            jax.ShapeDtypeStruct((n_context, width, ff), F32),
            jax.ShapeDtypeStruct((n_context, ff, width), F32),
        ),
        in_specs=[pl.BlockSpec((1, per, 128, 512), lambda c, f: (c, f, 0, 0))],
        out_specs=(
            pl.BlockSpec((1, width, 512), lambda c, f: (c, 0, jnp.minimum(f, tiles - 1))),
            pl.BlockSpec((1, 512, width), lambda c, f: (c, jnp.maximum(f - tiles, 0), 0)),
        ),
        name="widen_sums",
    )(sums)


def per_device(n_expert, n_context, n_dp, tokens, gain_attn, wqkv, w_out, gain_mix, w_control, w_in, w_back, segments, valid, cotangent):
    reps, seqs, half, width = tokens.shape
    length = half * n_context
    slab = half // n_expert
    group = seqs * n_expert
    e, c = lax.axis_index("expert"), lax.axis_index("context")

    def pick(x, i, axis=0):
        return lax.dynamic_index_in_dim(x, i, axis, keepdims=False)

    seg_a, valid_a = pick(segments, c), pick(valid, c)
    kmark = jnp.where(valid_a > 0, seg_a, -1)[:, :, None]
    qmark = seg_a[:, None, :]
    lengths = jnp.sum((valid_a > 0).astype(F32), 1)
    live = jnp.broadcast_to(lengths[:, None, None], (seqs, 8, 128))
    resid_m, cot_m, live_m, tok_a, qkv, att, lse, sq = forward(
        tokens, cotangent, kmark, qmark, live, gain_attn[None], wqkv, w_out, n_expert, n_context
    )
    blocks = 2 * width * w_in.shape[-1] // (128 * 512)
    first, final = blocks * 11 // 32, blocks * 10 // 32
    d_attn, out_m, part, sums, grad_control, grad_gain_mix, sq_mix = mix(
        resid_m, cot_m, live_m, gain_mix[None], w_control, w_in, w_back,
        n_expert, n_context, n_dp, first,
    )
    d_tokens, last, output, sums, grad_qkv, grad_out, grad_gain = backward(
        d_attn.reshape(seqs, length, width), tok_a, qkv, att, lse, kmark, qmark, gain_attn[None],
        wqkv, w_out, out_m, part, sums, n_expert, n_context, n_dp, blocks - first - final,
    )
    squares = jnp.stack([jnp.sum(sq_mix[0]), jnp.sum(sq), jnp.sum(sq_mix[1]), jnp.sum(lengths)])
    n_all = grad_control.shape[1]
    misc = jnp.concatenate(
        (
            grad_control.T, grad_gain, grad_gain_mix, jnp.pad(squares, (0, width - 4))[None],
            jnp.zeros((-(n_all + 3) % 16, width), F32),
        )
    )
    grad_qkv, grad_out, misc, d_tokens, sums = share(
        grad_qkv, grad_out, misc, last, part, d_tokens, sums, n_expert, n_context, n_dp, final
    )
    grad_control = misc[:n_all].T
    grad_gain, grad_gain_mix, squares = (misc[n_all + i] for i in range(3))
    grad_in, grad_back = widen(sums, width, w_in.shape[-1])
    stats = jnp.sqrt(squares[:3] / (squares[3] * width))
    return (
        output, d_tokens, grad_gain, grad_qkv, grad_out, grad_gain_mix, grad_control,
        grad_in, grad_back, stats,
    )


def solution(mesh):
    shards = P("dp", "expert", "context", None)
    rows = P("dp", "expert", None)
    experts = P("expert", None, None)
    return jax.shard_map(
        functools.partial(
            per_device, mesh.shape["expert"], mesh.shape["context"], mesh.shape["dp"]
        ),
        mesh=mesh,
        in_specs=(shards, P(), P(), P(), P(), P(), experts, experts, rows, rows, shards),
        out_specs=(shards, shards, P(), P(), P(), P(), P(), experts, experts, P()),
        check_vma=False,
    )
```

```python
import functools
import jax
import jax.numpy as jnp
from jax import lax
from jax.experimental import pallas as pl
from jax.experimental.pallas import tpu as pltpu
from jax.sharding import PartitionSpec as P

HEADS = 8
NEG_FILL = -1e30
MESH = pl.DeviceIdType.MESH
BF = jnp.bfloat16
F32 = jnp.float32
ANY = pl.BlockSpec(memory_space=pl.ANY)
VM = pl.BlockSpec(memory_space=pltpu.VMEM)
VMEM_LIMIT = 60 * 1024 * 1024


def dot(a, b, dims=((1,), (0,))):
    return lax.dot_general(a, b, (dims, ((), ())), preferred_element_type=F32)


def normalized(x):
    center = x - jnp.mean(x, -1, keepdims=True)
    spread = jnp.mean(center * center, -1, keepdims=True)
    rstd = lax.rsqrt(spread + 1e-05)
    return center * rstd, rstd


def ring(n_expert, n_context):
    e = lax.axis_index("expert")
    c = lax.axis_index("context")
    n = n_expert * n_context
    me = e * n_context + c

    def peer(k):
        j = lax.rem(me + k, n)
        pe = lax.div(j, n_context)
        pc = lax.rem(j, n_context)
        return j, pe, pc

    return e, c, me, n, peer


def enter(peer, n, reduce=None):
    barrier = pltpu.get_barrier_semaphore()
    for k in range(1, n):
        _, pe, pc = peer(k)
        pl.semaphore_signal(
            barrier, inc=1, device_id={"expert": pe, "context": pc}, device_id_type=MESH
        )
    extra = 0 if reduce is None else reduce.greet()
    pl.semaphore_wait(barrier, n - 1 + extra)


class Reduce:
    def __init__(self, own, rin, lin, ring_r, ring_l, sems, sums, base, lag, n_dp, n_context):
        self.lag = lag
        self.own, self.ins, self.rings, self.sums = own, (rin, lin), (ring_r, ring_l), sums
        self.send, self.recv, self.swap_s, self.swap_r, self.keep = sems
        self.count, self.slots = own.shape[0], ring_r.shape[0]
        self.n_dp, self.n_context, self.base = n_dp, n_context, base
        self.z, self.c = lax.axis_index("dp"), lax.axis_index("context")

    def greet(self):
        barrier = pltpu.get_barrier_semaphore()
        z, last = self.z, self.n_dp - 1
        for here, to in ((z > 0, z - 1), (z < last, z + 1)):

            @pl.when(here)
            def _():
                pl.semaphore_signal(barrier, inc=1, device_id={"dp": to}, device_id_type=MESH)

        return jnp.minimum(z, 1) + jnp.minimum(last - z, 1)

    def hop(self, way, i):
        to = self.z + (1 if way == 0 else -1)
        slot = lax.rem(i, self.slots)
        return pltpu.make_async_remote_copy(
            src_ref=self.rings[way].at[slot], dst_ref=self.ins[way].at[i],
            send_sem=self.send.at[way, slot], recv_sem=self.recv.at[way, i],
            device_id={"dp": to}, device_id_type=MESH,
        )

    def swaps(self, i):
        out = []
        for k in range(1, self.n_context):
            pc = lax.rem(self.c + k, self.n_context)
            out.append(
                pltpu.make_async_remote_copy(
                    src_ref=self.own.at[i], dst_ref=self.sums.at[self.c, self.base + i],
                    send_sem=self.swap_s.at[k, i], recv_sem=self.swap_r.at[k, i],
                    device_id={"context": pc}, device_id_type=MESH,
                )
            )
        out.append(
            pltpu.make_async_copy(
                self.own.at[i], self.sums.at[self.c, self.base + i], self.keep.at[i]
            )
        )
        return out

    def tick(self, t, swap=True):
        last = self.n_dp - 1
        for way in range(2):
            behind = self.z if way == 0 else last - self.z
            i = t - self.lag * behind
            has_in, has_out = behind > 0, behind < last

            @pl.when((i >= 0) & (i < self.count))
            def _():
                @pl.when(has_in)
                def _():
                    self.hop(way, i).wait_recv()

                @pl.when(has_out)
                def _():
                    @pl.when(i >= self.slots)
                    def _():
                        self.hop(way, i - self.slots).wait_send()

                    slot = lax.rem(i, self.slots)

                    @pl.when(has_in)
                    def _():
                        self.rings[way][slot] = (
                            self.ins[way][i].astype(F32) + self.own[i].astype(F32)
                        ).astype(BF)

                    @pl.when(jnp.logical_not(has_in))
                    def _():
                        self.rings[way][slot] = self.own[i]

                    self.hop(way, i).start()

        m = t - self.lag * jnp.maximum(self.z, last - self.z)

        @pl.when((m >= 0) & (m < self.count))
        def _():
            first, final = self.z == 0, self.z == last

            @pl.when(first)
            def _():
                self.own[m] = (self.own[m].astype(F32) + self.ins[1][m].astype(F32)).astype(BF)

            @pl.when(final)
            def _():
                self.own[m] = (self.own[m].astype(F32) + self.ins[0][m].astype(F32)).astype(BF)

            @pl.when(jnp.logical_not(first | final))
            def _():
                self.own[m] = (
                    self.own[m].astype(F32) + self.ins[0][m].astype(F32) + self.ins[1][m].astype(F32)
                ).astype(BF)

            if swap:
                for cp in self.swaps(m):
                    cp.start()

    def release(self, t):
        done = jnp.minimum(t - self.lag * jnp.maximum(self.z, self.n_dp - 1 - self.z), self.count)

        def one(m, _):
            @pl.when(m < done)
            def _():
                for cp in self.swaps(m):
                    cp.start()

            return 0

        lax.fori_loop(0, self.count, one, 0)

    def finish(self, t):
        lax.fori_loop(t, self.count + self.lag * (self.n_dp - 1), lambda i, _: (self.tick(i), 0)[1], 0)
        last = self.n_dp - 1
        for way in range(2):

            @pl.when((self.z if way == 0 else last - self.z) < last)
            def _():
                for i in range(max(0, self.count - self.slots), self.count):
                    self.hop(way, i).wait_send()

        def drain(i, _):
            for cp in self.swaps(i):
                cp.wait()
            return 0

        lax.fori_loop(0, self.count, drain, 0)


def reduce_scratch(count, n_context, slots=4):
    sem = pltpu.SemaphoreType.DMA
    block = pltpu.VMEM((count, 128, 512), BF)
    ring_block = pltpu.VMEM((slots, 128, 512), BF)
    return [
        block, block, ring_block, ring_block,
        sem((2, slots)), sem((2, count)), sem((n_context, count)), sem((n_context, count)), sem((count,)),
    ]


def mask_bias(bias, kmark, qmark, s, q0, qn):
    kk = q0 + qn
    place_k = lax.broadcasted_iota(jnp.int32, (kk, qn), 0)
    place_q = lax.broadcasted_iota(jnp.int32, (kk, qn), 1) + q0
    same = kmark[s, pl.ds(0, kk), :] == qmark[s, :, pl.ds(q0, qn)]
    bias[pl.ds(0, kk), :] = jnp.where(same & (place_k <= place_q), 0.0, NEG_FILL)


def forward_kernel(
    tokens, cot, kmark, qmark, live, gain, wqkv, wout,
    resid_m, cot_m, live_m, tok_a, qkv_o, att_o, lse_o, sq_o,
    tok, qkv, vt, att, att_t, res, bias,
    tok_s, tok_r, cot_s, cot_r, res_s, res_r, live_s, live_r, own_s, save_s,
    *, n_expert, n_context,
):
    e, c, me, n, peer = ring(n_expert, n_context)
    seqs, length, width = qkv_o.shape[0], qkv_o.shape[1], tokens.shape[-1]
    half = length // n_context
    slab = half // n_expert
    qn = 256
    enter(peer, n)
    def outgoing(s):
        out = []
        for k in range(1, n_context):
            pc = lax.rem(c + k, n_context)
            out.append(
                pltpu.make_async_remote_copy(
                    src_ref=tokens.at[pc, s], dst_ref=tok.at[s, c],
                    send_sem=tok_s.at[s, k], recv_sem=tok_r.at[s, k],
                    device_id={"context": pc}, device_id_type=MESH,
                )
            )
        return out

    for cp in outgoing(0):
        cp.start()
    own = []
    for s in range(seqs):
        cp = pltpu.make_async_copy(tokens.at[c, s], tok.at[s, c], own_s.at[s])
        cp.start()
        own.append(cp)

    def project(s, h):
        x = tok[s, h].astype(F32)
        y, _ = normalized(x)
        a = (y * gain[...]).astype(BF)
        at = pl.ds(pl.multiple_of(h * half, half), half)
        qkv[s, at, :] = dot(a, wqkv[...]).astype(BF)
        vt[s, :, at] = dot(wqkv[:, pl.ds(2 * width, width)], a, ((0,), (1,))).astype(BF)

    for s in range(seqs):
        own[s].wait()
        project(s, c)
    for cp in outgoing(0):
        cp.wait()
    for s in range(1, seqs):
        for cp in outgoing(s):
            cp.start()
    mine = pl.ds(e * seqs, seqs)
    local = [pltpu.make_async_copy(live, live_m.at[mine], own_s.at[seqs + 1])]
    crossing = []
    for k in range(1, n_expert):
        pe = lax.rem(e + k, n_expert)
        crossing.append(
            pltpu.make_async_remote_copy(
                src_ref=live, dst_ref=live_m.at[mine], send_sem=live_s.at[k], recv_sem=live_r.at[k],
                device_id={"expert": pe}, device_id_type=MESH,
            )
        )
    for k in range(1, n):
        j, pe, pc = peer(k)
        crossing.append(
            pltpu.make_async_remote_copy(
                src_ref=cot.at[pc, :, pl.ds(pl.multiple_of(pe * slab, slab), slab), :],
                dst_ref=cot_m.at[mine, c],
                send_sem=cot_s.at[k], recv_sem=cot_r.at[k],
                device_id={"expert": pe, "context": pc}, device_id_type=MESH,
            )
        )
    local.append(
        pltpu.make_async_copy(
            cot.at[c, :, pl.ds(pl.multiple_of(e * slab, slab), slab), :],
            cot_m.at[mine, c], own_s.at[seqs],
        )
    )
    for cp in local:
        cp.start()
    saves = [
        pltpu.make_async_copy(qkv, qkv_o, save_s.at[0]),
        pltpu.make_async_copy(tok, tok_a, save_s.at[1]),
    ]
    lane = lax.broadcasted_iota(jnp.int32, (qn, 128), 1)
    moving = []
    total = jnp.zeros((1, width), F32)
    for s in range(seqs):
        if 0 < s < seqs - 1:
            for cp in outgoing(s):
                cp.wait()
        for k in range(1, n_context):
            project(s, lax.rem(c + k, n_context))
        if s == seqs - 1:
            for cp in saves:
                cp.start()
        for qb in range(length // qn):
            if s == max(0, seqs - 2) and qb * 2 == length // qn:
                for later in range(s + 1, seqs):
                    for cp in outgoing(later):
                        cp.wait()
                for cp in crossing:
                    cp.start()
            kk = (qb + 1) * qn
            rows = pl.ds(qb * qn, qn)
            mask_bias(bias, kmark, qmark, s, qb * qn, qn)

            for at in range(0, width, 128):
                q2 = qkv[s, rows, pl.ds(at, 128)] * BF(0.125)
                k2 = qkv[s, pl.ds(0, kk), pl.ds(width + at, 128)]
                outs = []
                for h in range(2):
                    mine = (lane >= 64) if h else (lane < 64)
                    qm = jnp.where(mine, q2, jnp.zeros_like(q2))
                    st = dot(k2, qm, ((1,), (1,))) + bias[pl.ds(0, kk), :]
                    top = jnp.max(st, 0, keepdims=True)
                    p = jnp.exp(st - top)
                    tot = jnp.sum(p, 0, keepdims=True)
                    lse_o[s, pl.ds(at // 64 + h, 1), rows] = top + jnp.log(tot)
                    vh = vt[s, pl.ds(at + 64 * h, 64), pl.ds(0, kk)]
                    outs.append(dot(vh, p.astype(BF)) * (1.0 / tot))
                both = jnp.concatenate(outs, 0)
                att_t[s, pl.ds(at, 128), rows] = both.astype(BF)
                att[s, rows, pl.ds(at, 128)] = both.T.astype(BF)
            h = qb * qn // half
            attn_out = dot(att[s, rows, :], wout[...])
            within = qb * qn - h * half
            x = tok[s, h, pl.ds(within, qn), :].astype(F32)
            res[s, h, pl.ds(within, qn), :] = (x + attn_out).astype(BF)
            ok = kmark[s, rows, :] >= 0
            total += jnp.sum(jnp.where(ok, attn_out * attn_out, 0.0), 0, keepdims=True)
            if (qb + 1) * qn == (h + 1) * half:
                for k in range(1, n_expert):
                    pe = lax.rem(e + k, n_expert)
                    cp = pltpu.make_async_remote_copy(
                        src_ref=res.at[s, h, pl.ds(pl.multiple_of(pe * slab, slab), slab), :],
                        dst_ref=resid_m.at[e * seqs + s, h],
                        send_sem=res_s.at[s, h, k], recv_sem=res_r.at[s, h, k],
                        device_id={"expert": pe}, device_id_type=MESH,
                    )
                    cp.start()
                    moving.append(cp)
                cp = pltpu.make_async_copy(
                    res.at[s, h, pl.ds(pl.multiple_of(e * slab, slab), slab), :],
                    resid_m.at[e * seqs + s, h], res_s.at[s, h, 0],
                )
                cp.start()
                moving.append(cp)
    sq_o[...] = total
    keep = pltpu.make_async_copy(att_t, att_o, save_s.at[2])
    keep.start()
    for cp in saves + moving + crossing + local + [keep]:
        cp.wait()


def forward(tokens, cot, kmark, qmark, live, gain, wqkv, wout, n_expert, n_context):
    reps, seqs, half, width = tokens.shape
    length = half * n_context
    slab = half // n_expert
    group = seqs * n_expert
    n = n_expert * n_context
    sem = pltpu.SemaphoreType.DMA
    return pl.pallas_call(
        functools.partial(forward_kernel, n_expert=n_expert, n_context=n_context),
        out_shape=(
            jax.ShapeDtypeStruct((group, n_context, slab, width), BF),
            jax.ShapeDtypeStruct((group, n_context, slab, width), BF),
            jax.ShapeDtypeStruct((group, *live.shape[1:]), F32),
            jax.ShapeDtypeStruct((seqs, n_context, half, width), BF),
            jax.ShapeDtypeStruct((seqs, length, 3 * width), BF),
            jax.ShapeDtypeStruct((seqs, width, length), BF),
            jax.ShapeDtypeStruct((seqs, HEADS, length), F32),
            jax.ShapeDtypeStruct((1, width), F32),
        ),
        in_specs=[ANY, ANY, VM, VM, VM, VM, VM, VM],
        out_specs=(ANY, ANY, ANY, ANY, ANY, ANY, VM, VM),
        scratch_shapes=[
            pltpu.VMEM((seqs, n_context, half, width), BF),
            pltpu.VMEM((seqs, length, 3 * width), BF),
            pltpu.VMEM((seqs, width, length), BF),
            pltpu.VMEM((seqs, length, width), BF),
            pltpu.VMEM((seqs, width, length), BF),
            pltpu.VMEM((seqs, n_context, half, width), BF),
            pltpu.VMEM((length, 256), F32),
            sem((seqs, n_context)), sem((seqs, n_context)),
            sem((n,)), sem((n,)),
            sem((seqs, n_context, n_expert)), sem((seqs, n_context, n_expert)),
            sem((n_expert,)), sem((n_expert,)),
            sem((seqs + 2,)), sem((3,)),
        ],
        compiler_params=pltpu.CompilerParams(
            collective_id=0, has_side_effects=True, vmem_limit_bytes=VMEM_LIMIT
        ),
        name="attend_forward",
    )(tokens, cot, kmark, qmark, live, gain, wqkv, wout)


def mix_kernel(
    resid_m, cot_m, live_m, gain, wc, w_in, w_back,
    d_attn, out_m, part_o, sums, gc_o, gm_o, sq_o,
    res, cot, u, wts, mixed, dexp, xs, des, eos, dms, eor, dmr, win, wback, acts, d_pres, glow,
    go_s, go_r, back_s, back_r, at_s, at_r, in_s, save_s, *rest,
    n_expert, n_context, n_dp, early,
):
    e, c, me, n, peer = ring(n_expert, n_context)
    group, halves, slab, width = res.shape
    seqs = group // n_expert
    ff = win.shape[1]
    experts = n
    span = max(16, 256 // group)
    parts, sub = xs.shape[0], xs.shape[2]
    per_half = parts // halves
    steps = sub // span
    reduce = Reduce(
        glow.at[pl.ds(0, early)], *rest[:4], rest[4:], sums, 0, 2, n_dp, n_context
    )
    loads = [
        pltpu.make_async_copy(resid_m, res, in_s.at[0]),
        pltpu.make_async_copy(cot_m, cot, in_s.at[1]),
        pltpu.make_async_copy(w_in.at[c], win, in_s.at[2]),
        pltpu.make_async_copy(w_back.at[c], wback, in_s.at[3]),
    ]
    for cp in loads:
        cp.start()
    enter(peer, n, reduce)
    rows, cols = group * span, experts * span
    spread = (
        lax.broadcasted_iota(jnp.int32, (experts, cols), 1) // span
        == lax.broadcasted_iota(jnp.int32, (experts, cols), 0)
    ).astype(BF)
    gather = (
        lax.broadcasted_iota(jnp.int32, (cols, experts), 0) // span
        == lax.broadcasted_iota(jnp.int32, (cols, experts), 1)
    ).astype(BF)
    diag = lax.rem(lax.broadcasted_iota(jnp.int32, (rows, cols), 0), span) == lax.rem(
        lax.broadcasted_iota(jnp.int32, (rows, cols), 1), span
    )

    def within(b, g):
        return pl.ds(pl.multiple_of(b % per_half * sub + g * span, span), span)

    def filled(b, g):
        place = lax.broadcasted_iota(jnp.int32, (group, span, 1), 1) + (
            (b // per_half * n_expert + e) * slab + b % per_half * sub + g * span
        )
        ok = place.astype(F32) < live_m[:, pl.ds(0, 1), pl.ds(0, 1)]
        return jnp.where(ok, 1.0, 0.0).reshape(rows, 1) > 0

    loads[0].wait()
    loads[1].wait()
    sent = []
    for b in range(parts):
        h = b // per_half

        def first(g, _):
            at, here = pl.ds(pl.multiple_of(g * span, span), span), within(b, g)
            r = res[:, h, here, :].reshape(rows, width).astype(F32)
            normed, _ = normalized(r)
            ug = (normed * gain[...]).astype(BF)
            u[:, h, here, :] = ug.reshape(group, span, width)
            logits = jnp.where(filled(b, g), dot(ug, wc[...]), NEG_FILL).reshape(group, span, experts)
            ex = jnp.exp(logits - jnp.max(logits, 0, keepdims=True))
            w = (ex / jnp.sum(ex, 0, keepdims=True)).reshape(rows, experts)
            wts[b * steps + g] = w
            wide = jnp.where(diag, dot(w.astype(BF), spread), 0.0).astype(BF)
            cg = cot[:, h, here, :].reshape(rows, width)
            mixed[b, :, at, :] = dot(wide, ug, ((0,), (0,))).astype(BF).reshape(experts, span, width)
            dexp[b, :, at, :] = dot(wide, cg, ((0,), (0,))).astype(BF).reshape(experts, span, width)
            return 0

        lax.fori_loop(0, steps, first, 0)
        for i, (src, dst) in enumerate(((mixed, xs), (dexp, des))):
            dst[b, 0] = src[b, me]
            for k in range(1, n):
                j, pe, pc = peer(k)
                cp = pltpu.make_async_remote_copy(
                    src_ref=src.at[b, j], dst_ref=dst.at[b, k],
                    send_sem=go_s.at[i, b, k], recv_sem=go_r.at[i, b, k],
                    device_id={"expert": pe, "context": pc}, device_id_type=MESH,
                )
                cp.start()
                sent.append((b, cp))
    loads[2].wait()
    loads[3].wait()
    tile = 512
    returned = []
    rows_in = n * sub
    for b in range(parts):
        for bb, cp in sent:
            if bb == b:
                cp.wait_recv()
        x = xs[b].reshape(rows_in, width)
        de = des[b].reshape(rows_in, width)

        def expert_tile(f, carry):
            eo, dm = carry
            at = pl.ds(pl.multiple_of(f * tile, tile), tile)
            pre = dot(x, win[:, at])
            sq = pre * pre
            t = jnp.tanh(0.7978845608028654 * pre * (1.0 + 0.044715 * sq))
            act = (0.5 * pre * (1.0 + t)).astype(BF)
            slope = 0.5 * (1.0 + t) + 0.5 * pre * (1.0 - t * t) * (
                0.7978845608028654 * (1.0 + 3 * 0.044715 * sq)
            )
            d_pre = (slope * dot(de, wback[at, :], ((1,), (1,)))).astype(BF)
            acts[pl.ds(b * rows_in, rows_in), at] = act
            d_pres[pl.ds(b * rows_in, rows_in), at] = d_pre
            return eo + dot(act, wback[at, :]), dm + dot(d_pre, win[:, at], ((1,), (1,)))

        zero = jnp.zeros((rows_in, width), F32)
        eo, dm = lax.fori_loop(0, ff // tile, expert_tile, (zero, zero))
        eos[b] = eo.astype(BF).reshape(n, sub, width)
        dms[b] = dm.astype(BF).reshape(n, sub, width)
        for i, (src, dst) in enumerate(((eos, eor), (dms, dmr))):
            dst[b, me] = src[b, 0]
            for k in range(1, n):
                j, pe, pc = peer(n - k)
                cp = pltpu.make_async_remote_copy(
                    src_ref=src.at[b, k], dst_ref=dst.at[b, me],
                    send_sem=back_s.at[i, b, k], recv_sem=back_r.at[i, b, k],
                    device_id={"expert": pe, "context": pc}, device_id_type=MESH,
                )
                cp.start()
                returned.append((b, cp))
    per = width // 128
    tokens = parts * rows_in

    def grad_tile(f, _):
        at = pl.ds(pl.multiple_of(f * tile, tile), tile)
        g = dot(xs[...].reshape(tokens, width), d_pres[:, at], ((0,), (0,)))
        glow[pl.ds(f * per, per)] = g.astype(BF).reshape(per, 128, tile)
        g = dot(acts[:, at], des[...].reshape(tokens, width), ((0,), (0,)))
        glow[pl.ds((ff // tile + f) * per, per)] = g.astype(BF).reshape(per, 128, width)
        reduce.tick(f, swap=False)
        return 0

    lax.fori_loop(0, ff // tile, grad_tile, 0)
    blocks = glow.shape[0]
    out, dat = mixed, dexp
    for _, sending in sent:
        sending.wait_send()
    keep = [
        pltpu.make_async_copy(glow.at[pl.ds(early, blocks - early)], part_o, save_s.at[0])
    ]
    keep[0].start()
    gc_o[...] = jnp.zeros_like(gc_o)
    gm_o[...] = jnp.zeros_like(gm_o)
    sq_o[...] = jnp.zeros_like(sq_o)
    moving = []
    for b in range(parts):
        h = b // per_half
        for bb, cp in returned:
            if bb == b:
                cp.wait_recv()
        if b == parts - 1:
            reduce.release(ff // tile + b * steps)

        def second(g, _):
            at, here = pl.ds(pl.multiple_of(g * span, span), span), within(b, g)
            r = res[:, h, here, :].reshape(rows, width).astype(F32)
            normed, rstd = normalized(r)
            ug = u[:, h, here, :].reshape(rows, width)
            cg = cot[:, h, here, :].reshape(rows, width)
            ok = filled(b, g)
            eg = eor[b, :, at, :].reshape(cols, width)
            dg = dmr[b, :, at, :].reshape(cols, width)
            w = wts[b * steps + g]
            wide = jnp.where(diag, dot(w.astype(BF), spread), 0.0).astype(BF)
            mix = dot(wide, eg)
            full = r + mix
            out[b, :, at, :] = full.astype(BF).reshape(group, span, width)
            sq_o[pl.ds(0, 1), :] += jnp.sum(jnp.where(ok, full * full, 0.0), 0, keepdims=True)
            sq_o[pl.ds(1, 1), :] += jnp.sum(jnp.where(ok, mix * mix, 0.0), 0, keepdims=True)
            dw = jnp.where(diag, dot(cg, eg, ((1,), (1,))) + dot(ug, dg, ((1,), (1,))), 0.0)
            high = dw.astype(BF)
            rest = (dw - high.astype(F32)).astype(BF)
            dw = dot(high, gather) + dot(rest, gather)
            inner = jnp.sum((w * dw).reshape(group, span, experts), 0, keepdims=True)
            d_log = (
                (w.reshape(group, span, experts) * (dw.reshape(group, span, experts) - inner))
                .reshape(rows, experts)
                .astype(BF)
            )
            gc_o[...] += dot(d_log, ug, ((0,), (0,)))
            d_u = dot(d_log, wc[...], ((1,), (1,))) + dot(wide, dg)
            gm_o[...] += jnp.sum(d_u * normed, 0, keepdims=True)
            q = d_u * gain[...]
            d_res = cg.astype(F32) + rstd * (
                q - jnp.mean(q, -1, keepdims=True) - normed * jnp.mean(q * normed, -1, keepdims=True)
            )
            dat[b, :, at, :] = d_res.astype(BF).reshape(group, span, width)
            reduce.tick(ff // tile + b * steps + g, swap=b == parts - 1)
            return 0

        lax.fori_loop(0, steps, second, 0)
        mine = pl.ds(pl.multiple_of(e * slab + b % per_half * sub, sub), sub)
        for k in range(1, n_expert):
            pe = lax.rem(e + k, n_expert)
            cp = pltpu.make_async_remote_copy(
                src_ref=dat.at[b, pl.ds(pe * seqs, seqs)], dst_ref=d_attn.at[:, h, mine, :],
                send_sem=at_s.at[b, k], recv_sem=at_r.at[b, k],
                device_id={"expert": pe}, device_id_type=MESH,
            )
            cp.start()
            moving.append(cp)
        cp = pltpu.make_async_copy(
            dat.at[b, pl.ds(e * seqs, seqs)], d_attn.at[:, h, mine, :], at_s.at[b, 0]
        )
        cp.start()
        moving.append(cp)
    cp = pltpu.make_async_copy(out, out_m, save_s.at[2])
    cp.start()
    for _, sending in returned:
        sending.wait_send()
    reduce.finish(ff // tile + parts * steps)
    for cp in moving + keep + [cp]:
        cp.wait()


def mix(resid_m, cot_m, live_m, gain, wc, w_in, w_back, n_expert, n_context, n_dp, early):
    group, halves, slab, width = resid_m.shape
    seqs = group // n_expert
    n = n_expert * n_context
    ff = w_in.shape[-1]
    span = max(16, 256 // group)
    parts, sub = halves * 2, slab // 2
    steps = sub // span
    blocks = 2 * width * ff // (128 * 512)
    sem = pltpu.SemaphoreType.DMA
    block = pltpu.VMEM((group, halves, slab, width), BF)
    turned = pltpu.VMEM((parts, n, sub, width), BF)
    return pl.pallas_call(
        functools.partial(
            mix_kernel, n_expert=n_expert, n_context=n_context, n_dp=n_dp, early=early
        ),
        out_shape=(
            jax.ShapeDtypeStruct((seqs, halves, slab * n_expert, width), BF),
            jax.ShapeDtypeStruct((parts, group, sub, width), BF),
            jax.ShapeDtypeStruct((blocks - early, 128, 512), BF),
            jax.ShapeDtypeStruct((n_context, blocks, 128, 512), BF),
            jax.ShapeDtypeStruct((n, width), F32),
            jax.ShapeDtypeStruct((1, width), F32),
            jax.ShapeDtypeStruct((2, width), F32),
        ),
        in_specs=[ANY, ANY, VM, VM, VM, ANY, ANY],
        out_specs=(ANY, ANY, ANY, ANY, VM, VM, VM),
        scratch_shapes=[
            block, block, block,
            pltpu.VMEM((parts * steps, group * span, n), F32),
            turned, turned, turned, turned, turned, turned, turned, turned,
            pltpu.VMEM((width, ff), BF), pltpu.VMEM((ff, width), BF),
            pltpu.VMEM((halves * n * slab, ff), BF), pltpu.VMEM((halves * n * slab, ff), BF),
            pltpu.VMEM((blocks, 128, 512), BF),
            sem((2, parts, n)), sem((2, parts, n)),
            sem((2, parts, n)), sem((2, parts, n)),
            sem((parts, n_expert)), sem((parts, n_expert)),
            sem((4,)), sem((3,)),
            *reduce_scratch(early, n_context),
        ],
        compiler_params=pltpu.CompilerParams(
            collective_id=1, has_side_effects=True, vmem_limit_bytes=63 * 1024 * 1024
        ),
        name="mix_and_experts",
    )(resid_m, cot_m, live_m, gain, wc, w_in, w_back)


def backward_kernel(
    d_attn, tok_a, qkv_a, att_a, lse, kmark, qmark, gain, wqkv, wout, out_m, part, sums_in,
    dtok_o, last_o, out_o, sums, gq_o, go_o, gg_o,
    da, tok, qkv, att, datt, delta, dkv, dqkv, dtok, bias, own,
    out_s, out_r, tok_s, tok_r, in_s, own_s, *rest,
    n_expert, n_context, n_dp, base,
):
    e, c, me, n, peer = ring(n_expert, n_context)
    seqs, length, width = da.shape
    half = length // n_context
    slab = half // n_expert
    qn = 256
    loads = [
        pltpu.make_async_copy(src, dst, in_s.at[i])
        for i, (src, dst) in enumerate(
            ((d_attn, da), (att_a, att), (qkv_a, qkv), (tok_a, tok),
             (part.at[pl.ds(0, own.shape[0])], own))
        )
    ]
    reduce = Reduce(own, *rest[:4], rest[4:], sums, base, 2, n_dp, n_context)
    for cp in loads:
        cp.start()
    enter(peer, n, reduce)
    crossing = []
    per_half = out_m.shape[0] // n_context
    sub = slab // per_half
    for b in range(per_half):
        mine = pl.ds(pl.multiple_of(e * slab + b * sub, sub), sub)
        for k in range(1, n):
            j, pe, pc = peer(k)
            cp = pltpu.make_async_remote_copy(
                src_ref=out_m.at[pc * per_half + b, pl.ds(pe * seqs, seqs)],
                dst_ref=out_o.at[c, :, mine, :],
                send_sem=out_s.at[b, k], recv_sem=out_r.at[b, k],
                device_id={"expert": pe, "context": pc}, device_id_type=MESH,
            )
            cp.start()
            crossing.append(cp)
        cp = pltpu.make_async_copy(
            out_m.at[c * per_half + b, pl.ds(e * seqs, seqs)], out_o.at[c, :, mine, :], own_s.at[2, b]
        )
        cp.start()
        crossing.append(cp)
    lane = lax.broadcasted_iota(jnp.int32, (qn, 128), 1)
    gg_o[...] = jnp.zeros_like(gg_o)
    for cp in loads:
        cp.wait()
    pairs = width // 128
    for s in range(seqs):
        datt[...] = dot(da[s], wout[...], ((1,), (1,))).astype(BF)
        turned = dot(wout[...], da[s], ((1,), (1,))).astype(BF).astype(F32) * att[s].astype(F32)
        delta[...] = jnp.sum(turned.reshape(HEADS, width // HEADS, length), 1)
        go = dot(att[s], da[s])
        go_o[...] = go if s == 0 else go_o[...] + go
        dkv[...] = jnp.zeros_like(dkv)
        for qb in range(length // qn):
            kk = (qb + 1) * qn
            rows = pl.ds(qb * qn, qn)
            mask_bias(bias, kmark, qmark, s, qb * qn, qn)

            def pair(hp, _):
                at = pl.multiple_of(hp * 128, 128)
                q2 = qkv[s, rows, pl.ds(at, 128)] * BF(0.125)
                k2 = qkv[s, pl.ds(0, kk), pl.ds(width + at, 128)]
                v2 = qkv[s, pl.ds(0, kk), pl.ds(2 * width + at, 128)]
                do2 = datt[rows, pl.ds(at, 128)]
                kt = k2.T
                dqs, dss, lows, qms, doms = [], [], [], [], []
                for h in range(2):
                    mine = (lane >= 64) if h else (lane < 64)
                    qm = jnp.where(mine, q2, jnp.zeros_like(q2))
                    dom = jnp.where(mine, do2, jnp.zeros_like(do2))
                    st = dot(k2, qm, ((1,), (1,))) + bias[pl.ds(0, kk), :]
                    p = jnp.exp(st - lse[s, pl.ds(2 * hp + h, 1), rows])
                    dp = dot(v2, dom, ((1,), (1,)))
                    ds = (p * (dp - delta[pl.ds(2 * hp + h, 1), rows])).astype(BF)
                    dqs.append(dot(kt[h * 64 : h * 64 + 64], ds))
                    dss.append(ds)
                    lows.append(p.astype(BF))
                    qms.append(qm)
                    doms.append(dom)
                dqkv[rows, pl.ds(at, 128)] = (
                    (jnp.concatenate(dqs, 0) * 0.125).T.astype(BF)
                )
                dkv[pl.ds(0, kk), pl.ds(at, 128)] += dot(dss[0], qms[0]) + dot(dss[1], qms[1])
                dkv[pl.ds(0, kk), pl.ds(width + at, 128)] += dot(lows[0], doms[0]) + dot(
                    lows[1], doms[1]
                )
                @pl.when(lax.rem(hp, 2) == 1)
                def _():
                    reduce.tick(((s * (length // qn) + qb) * pairs + hp) // 2)

                return 0

            lax.fori_loop(0, pairs, pair, 0)
        dqkv[:, pl.ds(width, 2 * width)] = dkv[...].astype(BF)
        for h in range(n_context):
            rows = pl.ds(h * half, half)
            normed, rstd = normalized(tok[s, h].astype(F32))
            a = (normed * gain[...]).astype(BF)
            gq = dot(a, dqkv[rows, :], ((0,), (0,)))
            gq_o[...] = gq if s == 0 and h == 0 else gq_o[...] + gq
            d_a = dot(dqkv[rows, :], wqkv[...], ((1,), (1,)))
            gg_o[...] += jnp.sum(d_a * normed, 0, keepdims=True)
            q = d_a * gain[...]
            dt = da[s, rows, :].astype(F32) + rstd * (
                q - jnp.mean(q, -1, keepdims=True) - normed * jnp.mean(q * normed, -1, keepdims=True)
            )
            dtok[s, h] = dt.astype(BF)
        if s == seqs - 1:
            cp = pltpu.make_async_copy(dtok.at[s], last_o, own_s.at[0, 1])
            cp.start()
            crossing.append(cp)
            continue
        for k in range(1, n_context):
            pc = lax.rem(c + k, n_context)
            cp = pltpu.make_async_remote_copy(
                src_ref=dtok.at[s, pc], dst_ref=dtok_o.at[c, s],
                send_sem=tok_s.at[s, k], recv_sem=tok_r.at[s, k],
                device_id={"context": pc}, device_id_type=MESH,
            )
            cp.start()
            crossing.append(cp)
        cp = pltpu.make_async_copy(dtok.at[s, c], dtok_o.at[c, s], own_s.at[1, s])
        cp.start()
        crossing.append(cp)
    reduce.finish(seqs * (length // qn) * pairs // 2)
    for cp in crossing:
        cp.wait()


def backward(
    d_attn, tok_a, qkv, att, lse, kmark, qmark, gain, wqkv, wout, out_m, part, sums,
    n_expert, n_context, n_dp, count,
):
    seqs, length, width = d_attn.shape
    half = length // n_context
    n = n_expert * n_context
    sem = pltpu.SemaphoreType.DMA
    return pl.pallas_call(
        functools.partial(
            backward_kernel, n_expert=n_expert, n_context=n_context, n_dp=n_dp,
            base=sums.shape[1] - part.shape[0],
        ),
        out_shape=(
            jax.ShapeDtypeStruct((n_context, seqs, half, width), BF),
            jax.ShapeDtypeStruct((n_context, half, width), BF),
            jax.ShapeDtypeStruct((n_context, seqs, half, width), BF),
            jax.ShapeDtypeStruct(sums.shape, BF),
            jax.ShapeDtypeStruct((width, 3 * width), F32),
            jax.ShapeDtypeStruct((width, width), F32),
            jax.ShapeDtypeStruct((1, width), F32),
        ),
        in_specs=[ANY, ANY, ANY, ANY, VM, VM, VM, VM, VM, VM, ANY, ANY, ANY],
        out_specs=(ANY, ANY, ANY, ANY, VM, VM, VM),
        input_output_aliases={12: 3},
        scratch_shapes=[
            pltpu.VMEM((seqs, length, width), BF),
            pltpu.VMEM((seqs, n_context, half, width), BF),
            pltpu.VMEM((seqs, length, 3 * width), BF),
            pltpu.VMEM((seqs, width, length), BF),
            pltpu.VMEM((length, width), BF),
            pltpu.VMEM((HEADS, length), F32),
            pltpu.VMEM((length, 2 * width), F32),
            pltpu.VMEM((length, 3 * width), BF),
            pltpu.VMEM((seqs, n_context, half, width), BF),
            pltpu.VMEM((length, 256), F32),
            pltpu.VMEM((count, *part.shape[1:]), BF),
            sem((2, n)), sem((2, n)),
            sem((seqs, n_context)), sem((seqs, n_context)),
            sem((5,)), sem((3, 2)),
            *reduce_scratch(count, n_context),
        ],
        compiler_params=pltpu.CompilerParams(
            collective_id=2, has_side_effects=True, vmem_limit_bytes=VMEM_LIMIT
        ),
        name="attend_backward",
    )(d_attn, tok_a, qkv, att, lse, kmark, qmark, gain, wqkv, wout, out_m, part, sums)


def share_kernel(
    gq, go, gc, gg, gm, sq, sq_mix, live, last, part_in, dtok_in, sums_in,
    packed_o, misc_o, dtok_o, sums,
    pack, other, chip, corners, along, whole, own,
    core_s, core_r, chip_s, chip_r, dp_s, dp_r, dp2_s, dp2_r, out_s, out_r, fin_s, fin_r, tok_s, tok_r, own_s, *rest,
    n_expert, n_context, n_dp,
):
    e, c, z = (lax.axis_index(a) for a in ("expert", "context", "dp"))
    core = lax.rem(e, 2)
    chips = n_expert // 2 * n_context
    me = lax.div(e, 2) * n_context + c
    width = go.shape[1]
    total = pack.shape[0]
    part = total // 2
    piece = part // chips
    lanes = width // n_dp
    twin = {"expert": e + 1 - 2 * core}

    def chip_at(k):
        j = lax.rem(me + k, chips)
        return j, {"expert": lax.div(j, n_context) * 2 + core, "context": lax.rem(j, n_context)}

    barrier = pltpu.get_barrier_semaphore()
    count = own.shape[0]
    load = pltpu.make_async_copy(
        part_in.at[pl.ds(part_in.shape[0] - count, count)], own, own_s.at[0]
    )
    load.start()
    reduce = Reduce(own, *rest[:4], rest[4:], sums, sums.shape[1] - count, 2, n_dp, n_context)
    ticks = [0]

    def tick(times):
        for _ in range(times):
            if ticks[0] < count + 2 * (n_dp - 1):
                reduce.tick(ticks[0])
                ticks[0] += 1

    seq = dtok_o.shape[1] - 1
    where = [twin] + [chip_at(k)[1] for k in range(1, chips)]
    where += [{"dp": lax.rem(z + k, n_dp)} for k in range(1, n_dp)]
    for to in where:
        pl.semaphore_signal(barrier, inc=1, device_id=to, device_id_type=MESH)
    for b in range(3):
        pack[pl.ds(b * width, width), :] = gq[:, pl.ds(b * width, width)].astype(BF)
    pack[pl.ds(3 * width, width), :] = go[...].astype(BF)
    at = gc.shape[0]
    misc_o[...] = jnp.zeros_like(misc_o)
    misc_o[pl.ds(0, at), :] = gc[...]
    for row in (gg[...], gm[...], sq_mix[pl.ds(0, 1), :], sq[...], sq_mix[pl.ds(1, 1), :], live[...]):
        misc_o[pl.ds(at, 1), :] = row
        at += 1
    pack[pl.ds(4 * width, total - 4 * width), :] = jnp.zeros((total - 4 * width, width), BF)
    pack[pl.ds(4 * width, misc_o.shape[0]), :] = misc_o[...].astype(BF)
    pl.semaphore_wait(barrier, len(where))

    def remote(src, dst, ss, rs, to):
        cp = pltpu.make_async_remote_copy(
            src_ref=src, dst_ref=dst, send_sem=ss, recv_sem=rs, device_id=to, device_id_type=MESH
        )
        cp.start()
        return cp

    def rows(i, n):
        return pl.ds(pl.multiple_of(i * n, 16), n)

    bulk = [
        remote(
            last.at[lax.rem(c + k, n_context)], dtok_o.at[c, seq], tok_s.at[k], tok_r.at[k],
            {"context": lax.rem(c + k, n_context)},
        )
        for k in range(1, n_context)
    ]
    keep = pltpu.make_async_copy(last.at[c], dtok_o.at[c, seq], own_s.at[1])
    keep.start()
    sent = []
    for k in range(chips):
        j = lax.rem(me + k + 1, chips)
        at = pl.ds(pl.multiple_of((1 - core) * part + j * piece, 16), piece)
        sent.append(remote(pack.at[at], other.at[rows(j, piece)], core_s.at[k], core_r.at[k], twin))
    first = list(sent)
    for k in range(chips):
        j = lax.rem(me + k + 1, chips)
        first[k].wait_recv()
        at = pl.ds(pl.multiple_of(core * part + j * piece, 16), piece)
        chip[rows(j, piece), :] = (
            pack[at, :].astype(F32) + other[rows(j, piece), :].astype(F32)
        ).astype(BF)
        if k < chips - 1:
            _, to = chip_at(k + 1)
            sent.append(
                remote(chip.at[rows(j, piece)], corners.at[k], chip_s.at[k], chip_r.at[k], to)
            )
    load.wait()
    tick(4)
    acc = chip[rows(me, piece), :].astype(F32)
    for k in range(chips - 1):
        sent[chips + k].wait_recv()
        acc += corners[k].astype(F32)
    chip[rows(me, piece), :] = acc.astype(BF)
    mine = pl.ds(pl.multiple_of(z * lanes, lanes), lanes)
    steps = []
    for k in range(1, n_dp):
        to = lax.rem(z + k, n_dp)
        theirs = pl.ds(pl.multiple_of(to * lanes, lanes), lanes)
        steps.append(
            remote(
                chip.at[rows(me, piece), theirs], along.at[k - 1], dp_s.at[k - 1], dp_r.at[k - 1],
                {"dp": to},
            )
        )
    tick(2)
    acc = chip[rows(me, piece), mine].astype(F32)
    for k in range(1, n_dp):
        steps[k - 1].wait_recv()
        acc += along[k - 1].astype(F32)
    home = pl.ds(pl.multiple_of(core * part + me * piece, 16), piece)
    whole[home, mine] = acc.astype(BF)
    back = []
    for k in range(1, n_dp):
        to = lax.rem(z + k, n_dp)
        back.append(
            remote(
                whole.at[home, mine], whole.at[home, mine], dp2_s.at[k - 1], dp2_r.at[k - 1],
                {"dp": to},
            )
        )
    tick(2)
    for cp in back:
        cp.wait_recv()
    spread = [remote(whole.at[home], whole.at[home], fin_s.at[0], fin_r.at[0], twin)]
    outs = []
    for k in range(1, chips):
        _, to = chip_at(k)
        outs.append(remote(whole.at[home], whole.at[home], out_s.at[k - 1], out_r.at[k - 1], to))
    tick(3)
    for k in range(1, chips):
        outs[k - 1].wait_recv()
        tick(1)
        j = lax.rem(me + chips - k, chips)
        got = whole.at[pl.ds(pl.multiple_of(core * part + j * piece, 16), piece)]
        spread.append(remote(got, got, fin_s.at[k], fin_r.at[k], twin))
    for cp in spread:
        cp.wait_recv()
    stored = pltpu.make_async_copy(whole.at[pl.ds(0, 4 * width)], packed_o, own_s.at[2])
    stored.start()
    misc_o[...] = whole[pl.ds(4 * width, misc_o.shape[0]), :].astype(F32)
    reduce.finish(ticks[0])
    for cp in sent + steps + back + outs + spread:
        cp.wait_send()
    for cp in bulk:
        cp.wait()
    keep.wait()
    stored.wait()


def share(gq, go, gc, gg, gm, sq, sq_mix, live, last, part_in, dtok, sums, n_expert, n_context, n_dp, count):
    width = go.shape[1]
    chips = n_expert // 2 * n_context
    unit = 2 * chips * 16
    rows = -(-(gc.shape[0] + 6) // 16) * 16
    total = -(-(4 * width + rows) // unit) * unit
    part = total // 2
    piece = part // chips
    sem = pltpu.SemaphoreType.DMA
    return pl.pallas_call(
        functools.partial(share_kernel, n_expert=n_expert, n_context=n_context, n_dp=n_dp),
        out_shape=(
            jax.ShapeDtypeStruct((4 * width, width), BF),
            jax.ShapeDtypeStruct((rows, width), F32),
            jax.ShapeDtypeStruct(dtok.shape, BF),
            jax.ShapeDtypeStruct(sums.shape, BF),
        ),
        in_specs=[VM] * 8 + [ANY] * 4,
        out_specs=(ANY, VM, ANY, ANY),
        input_output_aliases={10: 2, 11: 3},
        scratch_shapes=[
            pltpu.VMEM((total, width), BF),
            pltpu.VMEM((part, width), BF),
            pltpu.VMEM((part, width), BF),
            pltpu.VMEM((max(1, chips - 1), piece, width), BF),
            pltpu.VMEM((max(1, n_dp - 1), piece, width // n_dp), BF),
            pltpu.VMEM((total, width), BF),
            pltpu.VMEM((count, *sums.shape[2:]), BF),
            sem((chips,)), sem((chips,)), sem((chips,)), sem((chips,)),
            sem((n_dp,)), sem((n_dp,)), sem((n_dp,)), sem((n_dp,)),
            sem((chips,)), sem((chips,)), sem((chips,)), sem((chips,)),
            sem((n_context,)), sem((n_context,)), sem((3,)),
            *reduce_scratch(count, n_context),
        ],
        compiler_params=pltpu.CompilerParams(
            collective_id=3, has_side_effects=True, vmem_limit_bytes=VMEM_LIMIT
        ),
        name="share_gradients",
    )(gq, go, gc, gg, gm, sq, sq_mix, live, last, part_in, dtok, sums)


def widen_kernel(src_in, src_back, packed, gi, gb, gq, go):
    gi[0] = src_in[0].reshape(gi.shape[1:]).astype(F32)
    gb[0] = src_back[0].reshape(gb.shape[1:]).astype(F32)
    width = go.shape[1]
    rows = go.shape[0]
    at = (pl.program_id(0) * pl.num_programs(1) + pl.program_id(1)) * rows
    for b in range(4):
        block = packed[pl.ds(pl.multiple_of(b * width + at, 16), rows), :].astype(F32)
        if b < 3:
            gq[:, pl.ds(b * width, width)] = block
        else:
            go[...] = block


def widen(sums, packed, width, ff):
    n_context, blocks = sums.shape[:2]
    tiles = ff // 512
    per = blocks // (2 * tiles)
    rows = width // (n_context * tiles)
    return pl.pallas_call(
        widen_kernel,
        grid=(n_context, tiles),
        out_shape=(
            jax.ShapeDtypeStruct((n_context, width, ff), F32),
            jax.ShapeDtypeStruct((n_context, ff, width), F32),
            jax.ShapeDtypeStruct((width, 3 * width), F32),
            jax.ShapeDtypeStruct((width, width), F32),
        ),
        in_specs=[
            pl.BlockSpec((1, per, 128, 512), lambda c, f: (c, f, 0, 0)),
            pl.BlockSpec((1, per, 128, 512), lambda c, f: (c, tiles + f, 0, 0)),
            pl.BlockSpec(packed.shape, lambda c, f: (0, 0)),
        ],
        out_specs=(
            pl.BlockSpec((1, width, 512), lambda c, f: (c, 0, f)),
            pl.BlockSpec((1, 512, width), lambda c, f: (c, f, 0)),
            pl.BlockSpec((rows, 3 * width), lambda c, f: (c * tiles + f, 0)),
            pl.BlockSpec((rows, width), lambda c, f: (c * tiles + f, 0)),
        ),
        compiler_params=pltpu.CompilerParams(vmem_limit_bytes=32 * 1024 * 1024),
        name="widen_sums",
    )(sums, sums, packed)


def per_device(n_expert, n_context, n_dp, tokens, gain_attn, wqkv, w_out, gain_mix, w_control, w_in, w_back, segments, valid, cotangent):
    reps, seqs, half, width = tokens.shape
    length = half * n_context
    slab = half // n_expert
    group = seqs * n_expert
    e, c = lax.axis_index("expert"), lax.axis_index("context")

    def pick(x, i, axis=0):
        return lax.dynamic_index_in_dim(x, i, axis, keepdims=False)

    seg_a, valid_a = pick(segments, c), pick(valid, c)
    kmark = jnp.where(valid_a > 0, seg_a, -1)[:, :, None]
    qmark = seg_a[:, None, :]
    lengths = jnp.sum((valid_a > 0).astype(F32), 1)
    live = jnp.broadcast_to(lengths[:, None, None], (seqs, 8, 128))
    resid_m, cot_m, live_m, tok_a, qkv, att, lse, sq = forward(
        tokens, cotangent, kmark, qmark, live, gain_attn[None], wqkv, w_out, n_expert, n_context
    )
    blocks = 2 * width * w_in.shape[-1] // (128 * 512)
    first, final = blocks * 11 // 32, blocks * 10 // 32
    d_attn, out_m, part, sums, grad_control, grad_gain_mix, sq_mix = mix(
        resid_m, cot_m, live_m, gain_mix[None], w_control, w_in, w_back,
        n_expert, n_context, n_dp, first,
    )
    d_tokens, last, output, sums, grad_qkv, grad_out, grad_gain = backward(
        d_attn.reshape(seqs, length, width), tok_a, qkv, att, lse, kmark, qmark, gain_attn[None],
        wqkv, w_out, out_m, part, sums, n_expert, n_context, n_dp, blocks - first - final,
    )
    n_all = grad_control.shape[0]
    count = jnp.pad(jnp.sum(lengths)[None, None], ((0, 0), (0, width - 1)))
    packed, misc, d_tokens, sums = share(
        grad_qkv, grad_out, grad_control, grad_gain, grad_gain_mix, sq, sq_mix, count,
        last, part, d_tokens, sums, n_expert, n_context, n_dp, final,
    )
    grad_control = misc[:n_all].T
    grad_gain, grad_gain_mix = misc[n_all], misc[n_all + 1]
    squares = jnp.sum(misc[n_all + 2 : n_all + 6], 1)
    grad_in, grad_back, grad_qkv, grad_out = widen(sums, packed, width, w_in.shape[-1])
    stats = jnp.sqrt(squares[:3] / (squares[3] * width))
    return (
        output, d_tokens, grad_gain, grad_qkv, grad_out, grad_gain_mix, grad_control,
        grad_in, grad_back, stats,
    )


def solution(mesh):
    shards = P("dp", "expert", "context", None)
    rows = P("dp", "expert", None)
    experts = P("expert", None, None)
    return jax.shard_map(
        functools.partial(
            per_device, mesh.shape["expert"], mesh.shape["context"], mesh.shape["dp"]
        ),
        mesh=mesh,
        in_specs=(shards, P(), P(), P(), P(), P(), experts, experts, rows, rows, shards),
        out_specs=(shards, shards, P(), P(), P(), P(), P(), experts, experts, P()),
        check_vma=False,
    )
```

```python
import functools
import jax
import jax.numpy as jnp
from jax import lax
from jax.experimental import pallas as pl
from jax.experimental.pallas import tpu as pltpu
from jax.sharding import PartitionSpec as P

HEADS = 8
NEG_FILL = -1e30
MESH = pl.DeviceIdType.MESH
BF = jnp.bfloat16
F32 = jnp.float32
ANY = pl.BlockSpec(memory_space=pl.ANY)
VM = pl.BlockSpec(memory_space=pltpu.VMEM)
VMEM_LIMIT = 60 * 1024 * 1024


def dot(a, b, dims=((1,), (0,))):
    return lax.dot_general(a, b, (dims, ((), ())), preferred_element_type=F32)


def normalized(x):
    center = x - jnp.mean(x, -1, keepdims=True)
    spread = jnp.mean(center * center, -1, keepdims=True)
    rstd = lax.rsqrt(spread + 1e-05)
    return center * rstd, rstd


def ring(n_expert, n_context):
    e = lax.axis_index("expert")
    c = lax.axis_index("context")
    n = n_expert * n_context
    me = e * n_context + c

    def peer(k):
        j = lax.rem(me + k, n)
        pe = lax.div(j, n_context)
        pc = lax.rem(j, n_context)
        return j, pe, pc

    return e, c, me, n, peer


def enter(peer, n, reduce=None):
    barrier = pltpu.get_barrier_semaphore()
    for k in range(1, n):
        _, pe, pc = peer(k)
        pl.semaphore_signal(
            barrier, inc=1, device_id={"expert": pe, "context": pc}, device_id_type=MESH
        )
    extra = 0 if reduce is None else reduce.greet()
    pl.semaphore_wait(barrier, n - 1 + extra)


class Reduce:
    def __init__(self, own, rin, lin, ring_r, ring_l, sems, sums, base, lag, n_dp, n_context):
        self.lag = lag
        self.own, self.ins, self.rings, self.sums = own, (rin, lin), (ring_r, ring_l), sums
        self.send, self.recv, self.swap_s, self.swap_r, self.keep = sems
        self.count, self.slots = own.shape[0], ring_r.shape[0]
        self.n_dp, self.n_context, self.base = n_dp, n_context, base
        self.z, self.c = lax.axis_index("dp"), lax.axis_index("context")

    def greet(self):
        barrier = pltpu.get_barrier_semaphore()
        z, last = self.z, self.n_dp - 1
        for here, to in ((z > 0, z - 1), (z < last, z + 1)):

            @pl.when(here)
            def _():
                pl.semaphore_signal(barrier, inc=1, device_id={"dp": to}, device_id_type=MESH)

        return jnp.minimum(z, 1) + jnp.minimum(last - z, 1)

    def hop(self, way, i):
        to = self.z + (1 if way == 0 else -1)
        slot = lax.rem(i, self.slots)
        return pltpu.make_async_remote_copy(
            src_ref=self.rings[way].at[slot], dst_ref=self.ins[way].at[i],
            send_sem=self.send.at[way, slot], recv_sem=self.recv.at[way, i],
            device_id={"dp": to}, device_id_type=MESH,
        )

    def swaps(self, i):
        out = []
        for k in range(1, self.n_context):
            pc = lax.rem(self.c + k, self.n_context)
            out.append(
                pltpu.make_async_remote_copy(
                    src_ref=self.own.at[i], dst_ref=self.sums.at[self.c, self.base + i],
                    send_sem=self.swap_s.at[k, i], recv_sem=self.swap_r.at[k, i],
                    device_id={"context": pc}, device_id_type=MESH,
                )
            )
        out.append(
            pltpu.make_async_copy(
                self.own.at[i], self.sums.at[self.c, self.base + i], self.keep.at[i]
            )
        )
        return out

    def tick(self, t, swap=True):
        last = self.n_dp - 1
        for way in range(2):
            behind = self.z if way == 0 else last - self.z
            i = t - self.lag * behind
            has_in, has_out = behind > 0, behind < last

            @pl.when((i >= 0) & (i < self.count))
            def _():
                @pl.when(has_in)
                def _():
                    self.hop(way, i).wait_recv()

                @pl.when(has_out)
                def _():
                    @pl.when(i >= self.slots)
                    def _():
                        self.hop(way, i - self.slots).wait_send()

                    slot = lax.rem(i, self.slots)

                    @pl.when(has_in)
                    def _():
                        self.rings[way][slot] = (
                            self.ins[way][i].astype(F32) + self.own[i].astype(F32)
                        ).astype(BF)

                    @pl.when(jnp.logical_not(has_in))
                    def _():
                        self.rings[way][slot] = self.own[i]

                    self.hop(way, i).start()

        m = t - self.lag * jnp.maximum(self.z, last - self.z)

        @pl.when((m >= 0) & (m < self.count))
        def _():
            first, final = self.z == 0, self.z == last

            @pl.when(first)
            def _():
                self.own[m] = (self.own[m].astype(F32) + self.ins[1][m].astype(F32)).astype(BF)

            @pl.when(final)
            def _():
                self.own[m] = (self.own[m].astype(F32) + self.ins[0][m].astype(F32)).astype(BF)

            @pl.when(jnp.logical_not(first | final))
            def _():
                self.own[m] = (
                    self.own[m].astype(F32) + self.ins[0][m].astype(F32) + self.ins[1][m].astype(F32)
                ).astype(BF)

            if swap:
                for cp in self.swaps(m):
                    cp.start()

    def release(self, t):
        done = jnp.minimum(t - self.lag * jnp.maximum(self.z, self.n_dp - 1 - self.z), self.count)

        def one(m, _):
            @pl.when(m < done)
            def _():
                for cp in self.swaps(m):
                    cp.start()

            return 0

        lax.fori_loop(0, self.count, one, 0)

    def finish(self, t):
        lax.fori_loop(t, self.count + self.lag * (self.n_dp - 1), lambda i, _: (self.tick(i), 0)[1], 0)
        last = self.n_dp - 1
        for way in range(2):

            @pl.when((self.z if way == 0 else last - self.z) < last)
            def _():
                for i in range(max(0, self.count - self.slots), self.count):
                    self.hop(way, i).wait_send()

        def drain(i, _):
            for cp in self.swaps(i):
                cp.wait()
            return 0

        lax.fori_loop(0, self.count, drain, 0)


def reduce_scratch(count, n_context, slots=4):
    sem = pltpu.SemaphoreType.DMA
    block = pltpu.VMEM((count, 128, 512), BF)
    ring_block = pltpu.VMEM((slots, 128, 512), BF)
    return [
        block, block, ring_block, ring_block,
        sem((2, slots)), sem((2, count)), sem((n_context, count)), sem((n_context, count)), sem((count,)),
    ]


def mask_bias(bias, kmark, qmark, s, q0, qn):
    kk = q0 + qn
    place_k = lax.broadcasted_iota(jnp.int32, (kk, qn), 0)
    place_q = lax.broadcasted_iota(jnp.int32, (kk, qn), 1) + q0
    same = kmark[s, pl.ds(0, kk), :] == qmark[s, :, pl.ds(q0, qn)]
    bias[pl.ds(0, kk), :] = jnp.where(same & (place_k <= place_q), 0.0, NEG_FILL)


def forward_kernel(
    tokens, cot, kmark, qmark, live, gain, wqkv, wout,
    resid_m, cot_m, live_m, tok_a, qkv_o, att_o, lse_o, sq_o,
    tok, qkv, vt, att, att_t, res, bias,
    tok_s, tok_r, cot_s, cot_r, res_s, res_r, live_s, live_r, own_s, save_s,
    *, n_expert, n_context,
):
    e, c, me, n, peer = ring(n_expert, n_context)
    seqs, length, width = qkv_o.shape[0], qkv_o.shape[1], tokens.shape[-1]
    half = length // n_context
    slab = half // n_expert
    qn = 256
    enter(peer, n)
    def outgoing(s):
        out = []
        for k in range(1, n_context):
            pc = lax.rem(c + k, n_context)
            out.append(
                pltpu.make_async_remote_copy(
                    src_ref=tokens.at[pc, s], dst_ref=tok.at[s, c],
                    send_sem=tok_s.at[s, k], recv_sem=tok_r.at[s, k],
                    device_id={"context": pc}, device_id_type=MESH,
                )
            )
        return out

    for cp in outgoing(0):
        cp.start()
    own = []
    for s in range(seqs):
        cp = pltpu.make_async_copy(tokens.at[c, s], tok.at[s, c], own_s.at[s])
        cp.start()
        own.append(cp)

    def project(s, h):
        x = tok[s, h].astype(F32)
        y, _ = normalized(x)
        a = (y * gain[...]).astype(BF)
        at = pl.ds(pl.multiple_of(h * half, half), half)
        qkv[s, at, :] = dot(a, wqkv[...]).astype(BF)
        vt[s, :, at] = dot(wqkv[:, pl.ds(2 * width, width)], a, ((0,), (1,))).astype(BF)

    for s in range(seqs):
        own[s].wait()
        project(s, c)
    for cp in outgoing(0):
        cp.wait()
    for s in range(1, seqs):
        for cp in outgoing(s):
            cp.start()
    mine = pl.ds(e * seqs, seqs)
    local = [pltpu.make_async_copy(live, live_m.at[mine], own_s.at[seqs + 1])]
    crossing = []
    for k in range(1, n_expert):
        pe = lax.rem(e + k, n_expert)
        crossing.append(
            pltpu.make_async_remote_copy(
                src_ref=live, dst_ref=live_m.at[mine], send_sem=live_s.at[k], recv_sem=live_r.at[k],
                device_id={"expert": pe}, device_id_type=MESH,
            )
        )
    for k in range(1, n):
        j, pe, pc = peer(k)
        crossing.append(
            pltpu.make_async_remote_copy(
                src_ref=cot.at[pc, :, pl.ds(pl.multiple_of(pe * slab, slab), slab), :],
                dst_ref=cot_m.at[mine, c],
                send_sem=cot_s.at[k], recv_sem=cot_r.at[k],
                device_id={"expert": pe, "context": pc}, device_id_type=MESH,
            )
        )
    local.append(
        pltpu.make_async_copy(
            cot.at[c, :, pl.ds(pl.multiple_of(e * slab, slab), slab), :],
            cot_m.at[mine, c], own_s.at[seqs],
        )
    )
    for cp in local + crossing:
        cp.start()
    saves = [
        pltpu.make_async_copy(qkv, qkv_o, save_s.at[0]),
        pltpu.make_async_copy(tok, tok_a, save_s.at[1]),
    ]
    lane = lax.broadcasted_iota(jnp.int32, (qn, 128), 1)
    moving = []
    total = jnp.zeros((1, width), F32)
    for s in range(seqs):
        if s > 0:
            for cp in outgoing(s):
                cp.wait()
        for k in range(1, n_context):
            project(s, lax.rem(c + k, n_context))
        if s == seqs - 1:
            for cp in saves:
                cp.start()
        for qb in range(length // qn):
            kk = (qb + 1) * qn
            rows = pl.ds(qb * qn, qn)
            mask_bias(bias, kmark, qmark, s, qb * qn, qn)

            for at in range(0, width, 128):
                q2 = qkv[s, rows, pl.ds(at, 128)] * BF(0.125)
                k2 = qkv[s, pl.ds(0, kk), pl.ds(width + at, 128)]
                outs = []
                for h in range(2):
                    mine = (lane >= 64) if h else (lane < 64)
                    qm = jnp.where(mine, q2, jnp.zeros_like(q2))
                    st = dot(k2, qm, ((1,), (1,))) + bias[pl.ds(0, kk), :]
                    top = jnp.max(st, 0, keepdims=True)
                    p = jnp.exp(st - top)
                    tot = jnp.sum(p, 0, keepdims=True)
                    lse_o[s, pl.ds(at // 64 + h, 1), rows] = top + jnp.log(tot)
                    vh = vt[s, pl.ds(at + 64 * h, 64), pl.ds(0, kk)]
                    outs.append(dot(vh, p.astype(BF)) * (1.0 / tot))
                both = jnp.concatenate(outs, 0)
                att_t[s, pl.ds(at, 128), rows] = both.astype(BF)
                att[s, rows, pl.ds(at, 128)] = both.T.astype(BF)
            h = qb * qn // half
            attn_out = dot(att[s, rows, :], wout[...])
            within = qb * qn - h * half
            x = tok[s, h, pl.ds(within, qn), :].astype(F32)
            res[s, h, pl.ds(within, qn), :] = (x + attn_out).astype(BF)
            ok = kmark[s, rows, :] >= 0
            total += jnp.sum(jnp.where(ok, attn_out * attn_out, 0.0), 0, keepdims=True)
            if (qb + 1) * qn == (h + 1) * half:
                for k in range(1, n_expert):
                    pe = lax.rem(e + k, n_expert)
                    cp = pltpu.make_async_remote_copy(
                        src_ref=res.at[s, h, pl.ds(pl.multiple_of(pe * slab, slab), slab), :],
                        dst_ref=resid_m.at[e * seqs + s, h],
                        send_sem=res_s.at[s, h, k], recv_sem=res_r.at[s, h, k],
                        device_id={"expert": pe}, device_id_type=MESH,
                    )
                    cp.start()
                    moving.append(cp)
                cp = pltpu.make_async_copy(
                    res.at[s, h, pl.ds(pl.multiple_of(e * slab, slab), slab), :],
                    resid_m.at[e * seqs + s, h], res_s.at[s, h, 0],
                )
                cp.start()
                moving.append(cp)
    sq_o[...] = total
    keep = pltpu.make_async_copy(att_t, att_o, save_s.at[2])
    keep.start()
    for cp in saves + moving + crossing + local + [keep]:
        cp.wait()


def forward(tokens, cot, kmark, qmark, live, gain, wqkv, wout, n_expert, n_context):
    reps, seqs, half, width = tokens.shape
    length = half * n_context
    slab = half // n_expert
    group = seqs * n_expert
    n = n_expert * n_context
    sem = pltpu.SemaphoreType.DMA
    return pl.pallas_call(
        functools.partial(forward_kernel, n_expert=n_expert, n_context=n_context),
        out_shape=(
            jax.ShapeDtypeStruct((group, n_context, slab, width), BF),
            jax.ShapeDtypeStruct((group, n_context, slab, width), BF),
            jax.ShapeDtypeStruct((group, *live.shape[1:]), F32),
            jax.ShapeDtypeStruct((seqs, n_context, half, width), BF),
            jax.ShapeDtypeStruct((seqs, length, 3 * width), BF),
            jax.ShapeDtypeStruct((seqs, width, length), BF),
            jax.ShapeDtypeStruct((seqs, HEADS, length), F32),
            jax.ShapeDtypeStruct((1, width), F32),
        ),
        in_specs=[ANY, ANY, VM, VM, VM, VM, VM, VM],
        out_specs=(ANY, ANY, ANY, ANY, ANY, ANY, VM, VM),
        scratch_shapes=[
            pltpu.VMEM((seqs, n_context, half, width), BF),
            pltpu.VMEM((seqs, length, 3 * width), BF),
            pltpu.VMEM((seqs, width, length), BF),
            pltpu.VMEM((seqs, length, width), BF),
            pltpu.VMEM((seqs, width, length), BF),
            pltpu.VMEM((seqs, n_context, half, width), BF),
            pltpu.VMEM((length, 256), F32),
            sem((seqs, n_context)), sem((seqs, n_context)),
            sem((n,)), sem((n,)),
            sem((seqs, n_context, n_expert)), sem((seqs, n_context, n_expert)),
            sem((n_expert,)), sem((n_expert,)),
            sem((seqs + 2,)), sem((3,)),
        ],
        compiler_params=pltpu.CompilerParams(
            collective_id=0, has_side_effects=True, vmem_limit_bytes=VMEM_LIMIT
        ),
        name="attend_forward",
    )(tokens, cot, kmark, qmark, live, gain, wqkv, wout)


def mix_kernel(
    resid_m, cot_m, live_m, gain, wc, w_in, w_back,
    d_attn, out_m, part_o, sums, gc_o, gm_o, sq_o,
    res, cot, u, wts, mixed, dexp, xs, des, eos, dms, eor, dmr, win, wback, acts, d_pres, glow,
    go_s, go_r, back_s, back_r, at_s, at_r, in_s, save_s, *rest,
    n_expert, n_context, n_dp, early,
):
    e, c, me, n, peer = ring(n_expert, n_context)
    group, halves, slab, width = res.shape
    seqs = group // n_expert
    ff = win.shape[1]
    experts = n
    span = max(16, 256 // group)
    parts, sub = xs.shape[0], xs.shape[2]
    per_half = parts // halves
    steps = sub // span
    reduce = Reduce(
        glow.at[pl.ds(0, early)], *rest[:4], rest[4:], sums, 0, 2, n_dp, n_context
    )
    loads = [
        pltpu.make_async_copy(resid_m, res, in_s.at[0]),
        pltpu.make_async_copy(cot_m, cot, in_s.at[1]),
        pltpu.make_async_copy(w_in.at[c], win, in_s.at[2]),
        pltpu.make_async_copy(w_back.at[c], wback, in_s.at[3]),
    ]
    for cp in loads:
        cp.start()
    enter(peer, n, reduce)
    rows, cols = group * span, experts * span
    spread = (
        lax.broadcasted_iota(jnp.int32, (experts, cols), 1) // span
        == lax.broadcasted_iota(jnp.int32, (experts, cols), 0)
    ).astype(BF)
    gather = (
        lax.broadcasted_iota(jnp.int32, (cols, experts), 0) // span
        == lax.broadcasted_iota(jnp.int32, (cols, experts), 1)
    ).astype(BF)
    diag = lax.rem(lax.broadcasted_iota(jnp.int32, (rows, cols), 0), span) == lax.rem(
        lax.broadcasted_iota(jnp.int32, (rows, cols), 1), span
    )

    def within(b, g):
        return pl.ds(pl.multiple_of(b % per_half * sub + g * span, span), span)

    def filled(b, g):
        place = lax.broadcasted_iota(jnp.int32, (group, span, 1), 1) + (
            (b // per_half * n_expert + e) * slab + b % per_half * sub + g * span
        )
        ok = place.astype(F32) < live_m[:, pl.ds(0, 1), pl.ds(0, 1)]
        return jnp.where(ok, 1.0, 0.0).reshape(rows, 1) > 0

    loads[0].wait()
    loads[1].wait()
    sent = []
    for b in range(parts):
        h = b // per_half

        def first(g, _):
            at, here = pl.ds(pl.multiple_of(g * span, span), span), within(b, g)
            r = res[:, h, here, :].reshape(rows, width).astype(F32)
            normed, _ = normalized(r)
            ug = (normed * gain[...]).astype(BF)
            u[:, h, here, :] = ug.reshape(group, span, width)
            logits = jnp.where(filled(b, g), dot(ug, wc[...]), NEG_FILL).reshape(group, span, experts)
            ex = jnp.exp(logits - jnp.max(logits, 0, keepdims=True))
            w = (ex / jnp.sum(ex, 0, keepdims=True)).reshape(rows, experts)
            wts[b * steps + g] = w
            wide = jnp.where(diag, dot(w.astype(BF), spread), 0.0).astype(BF)
            cg = cot[:, h, here, :].reshape(rows, width)
            mixed[b, :, at, :] = dot(wide, ug, ((0,), (0,))).astype(BF).reshape(experts, span, width)
            dexp[b, :, at, :] = dot(wide, cg, ((0,), (0,))).astype(BF).reshape(experts, span, width)
            return 0

        lax.fori_loop(0, steps, first, 0)
        for i, (src, dst) in enumerate(((mixed, xs), (dexp, des))):
            dst[b, 0] = src[b, me]
            for k in range(1, n):
                j, pe, pc = peer(k)
                cp = pltpu.make_async_remote_copy(
                    src_ref=src.at[b, j], dst_ref=dst.at[b, k],
                    send_sem=go_s.at[i, b, k], recv_sem=go_r.at[i, b, k],
                    device_id={"expert": pe, "context": pc}, device_id_type=MESH,
                )
                cp.start()
                sent.append((b, cp))
    loads[2].wait()
    loads[3].wait()
    tile = 512
    returned = []
    rows_in = n * sub
    for b in range(parts):
        for bb, cp in sent:
            if bb == b:
                cp.wait_recv()
        x = xs[b].reshape(rows_in, width)
        de = des[b].reshape(rows_in, width)

        def expert_tile(f, carry):
            eo, dm = carry
            at = pl.ds(pl.multiple_of(f * tile, tile), tile)
            pre = dot(x, win[:, at])
            sq = pre * pre
            t = jnp.tanh(0.7978845608028654 * pre * (1.0 + 0.044715 * sq))
            act = (0.5 * pre * (1.0 + t)).astype(BF)
            slope = 0.5 * (1.0 + t) + 0.5 * pre * (1.0 - t * t) * (
                0.7978845608028654 * (1.0 + 3 * 0.044715 * sq)
            )
            d_pre = (slope * dot(de, wback[at, :], ((1,), (1,)))).astype(BF)
            acts[pl.ds(b * rows_in, rows_in), at] = act
            d_pres[pl.ds(b * rows_in, rows_in), at] = d_pre
            return eo + dot(act, wback[at, :]), dm + dot(d_pre, win[:, at], ((1,), (1,)))

        zero = jnp.zeros((rows_in, width), F32)
        eo, dm = lax.fori_loop(0, ff // tile, expert_tile, (zero, zero))
        eos[b] = eo.astype(BF).reshape(n, sub, width)
        dms[b] = dm.astype(BF).reshape(n, sub, width)
        for i, (src, dst) in enumerate(((eos, eor), (dms, dmr))):
            dst[b, me] = src[b, 0]
            for k in range(1, n):
                j, pe, pc = peer(n - k)
                cp = pltpu.make_async_remote_copy(
                    src_ref=src.at[b, k], dst_ref=dst.at[b, me],
                    send_sem=back_s.at[i, b, k], recv_sem=back_r.at[i, b, k],
                    device_id={"expert": pe, "context": pc}, device_id_type=MESH,
                )
                cp.start()
                returned.append((b, cp))
    per = width // 128
    tokens = parts * rows_in

    def grad_tile(f, _):
        at = pl.ds(pl.multiple_of(f * tile, tile), tile)
        g = dot(xs[...].reshape(tokens, width), d_pres[:, at], ((0,), (0,)))
        glow[pl.ds(f * per, per)] = g.astype(BF).reshape(per, 128, tile)
        g = dot(acts[:, at], des[...].reshape(tokens, width), ((0,), (0,)))
        glow[pl.ds((ff // tile + f) * per, per)] = g.astype(BF).reshape(per, 128, width)
        reduce.tick(f, swap=False)
        return 0

    lax.fori_loop(0, ff // tile, grad_tile, 0)
    blocks = glow.shape[0]
    out, dat = mixed, dexp
    for _, sending in sent:
        sending.wait_send()
    keep = [
        pltpu.make_async_copy(glow.at[pl.ds(early, blocks - early)], part_o, save_s.at[0])
    ]
    keep[0].start()
    gc_o[...] = jnp.zeros_like(gc_o)
    gm_o[...] = jnp.zeros_like(gm_o)
    sq_o[...] = jnp.zeros_like(sq_o)
    moving = []
    for b in range(parts):
        h = b // per_half
        for bb, cp in returned:
            if bb == b:
                cp.wait_recv()
        if b == parts - 1:
            reduce.release(ff // tile + b * steps)

        def second(g, _):
            at, here = pl.ds(pl.multiple_of(g * span, span), span), within(b, g)
            r = res[:, h, here, :].reshape(rows, width).astype(F32)
            normed, rstd = normalized(r)
            ug = u[:, h, here, :].reshape(rows, width)
            cg = cot[:, h, here, :].reshape(rows, width)
            ok = filled(b, g)
            eg = eor[b, :, at, :].reshape(cols, width)
            dg = dmr[b, :, at, :].reshape(cols, width)
            w = wts[b * steps + g]
            wide = jnp.where(diag, dot(w.astype(BF), spread), 0.0).astype(BF)
            mix = dot(wide, eg)
            full = r + mix
            out[b, :, at, :] = full.astype(BF).reshape(group, span, width)
            sq_o[pl.ds(0, 1), :] += jnp.sum(jnp.where(ok, full * full, 0.0), 0, keepdims=True)
            sq_o[pl.ds(1, 1), :] += jnp.sum(jnp.where(ok, mix * mix, 0.0), 0, keepdims=True)
            dw = jnp.where(diag, dot(cg, eg, ((1,), (1,))) + dot(ug, dg, ((1,), (1,))), 0.0)
            high = dw.astype(BF)
            rest = (dw - high.astype(F32)).astype(BF)
            dw = dot(high, gather) + dot(rest, gather)
            inner = jnp.sum((w * dw).reshape(group, span, experts), 0, keepdims=True)
            d_log = (
                (w.reshape(group, span, experts) * (dw.reshape(group, span, experts) - inner))
                .reshape(rows, experts)
                .astype(BF)
            )
            gc_o[...] += dot(d_log, ug, ((0,), (0,)))
            d_u = dot(d_log, wc[...], ((1,), (1,))) + dot(wide, dg)
            gm_o[...] += jnp.sum(d_u * normed, 0, keepdims=True)
            q = d_u * gain[...]
            d_res = cg.astype(F32) + rstd * (
                q - jnp.mean(q, -1, keepdims=True) - normed * jnp.mean(q * normed, -1, keepdims=True)
            )
            dat[b, :, at, :] = d_res.astype(BF).reshape(group, span, width)
            reduce.tick(ff // tile + b * steps + g, swap=b == parts - 1)
            return 0

        lax.fori_loop(0, steps, second, 0)
        mine = pl.ds(pl.multiple_of(e * slab + b % per_half * sub, sub), sub)
        for k in range(1, n_expert):
            pe = lax.rem(e + k, n_expert)
            cp = pltpu.make_async_remote_copy(
                src_ref=dat.at[b, pl.ds(pe * seqs, seqs)], dst_ref=d_attn.at[:, h, mine, :],
                send_sem=at_s.at[b, k], recv_sem=at_r.at[b, k],
                device_id={"expert": pe}, device_id_type=MESH,
            )
            cp.start()
            moving.append(cp)
        cp = pltpu.make_async_copy(
            dat.at[b, pl.ds(e * seqs, seqs)], d_attn.at[:, h, mine, :], at_s.at[b, 0]
        )
        cp.start()
        moving.append(cp)
    cp = pltpu.make_async_copy(out, out_m, save_s.at[2])
    cp.start()
    for _, sending in returned:
        sending.wait_send()
    reduce.finish(ff // tile + parts * steps)
    for cp in moving + keep + [cp]:
        cp.wait()


def mix(resid_m, cot_m, live_m, gain, wc, w_in, w_back, n_expert, n_context, n_dp, early):
    group, halves, slab, width = resid_m.shape
    seqs = group // n_expert
    n = n_expert * n_context
    ff = w_in.shape[-1]
    span = max(16, 256 // group)
    parts, sub = halves * 2, slab // 2
    steps = sub // span
    blocks = 2 * width * ff // (128 * 512)
    sem = pltpu.SemaphoreType.DMA
    block = pltpu.VMEM((group, halves, slab, width), BF)
    turned = pltpu.VMEM((parts, n, sub, width), BF)
    return pl.pallas_call(
        functools.partial(
            mix_kernel, n_expert=n_expert, n_context=n_context, n_dp=n_dp, early=early
        ),
        out_shape=(
            jax.ShapeDtypeStruct((seqs, halves, slab * n_expert, width), BF),
            jax.ShapeDtypeStruct((parts, group, sub, width), BF),
            jax.ShapeDtypeStruct((blocks - early, 128, 512), BF),
            jax.ShapeDtypeStruct((n_context, blocks, 128, 512), BF),
            jax.ShapeDtypeStruct((n, width), F32),
            jax.ShapeDtypeStruct((1, width), F32),
            jax.ShapeDtypeStruct((2, width), F32),
        ),
        in_specs=[ANY, ANY, VM, VM, VM, ANY, ANY],
        out_specs=(ANY, ANY, ANY, ANY, VM, VM, VM),
        scratch_shapes=[
            block, block, block,
            pltpu.VMEM((parts * steps, group * span, n), F32),
            turned, turned, turned, turned, turned, turned, turned, turned,
            pltpu.VMEM((width, ff), BF), pltpu.VMEM((ff, width), BF),
            pltpu.VMEM((halves * n * slab, ff), BF), pltpu.VMEM((halves * n * slab, ff), BF),
            pltpu.VMEM((blocks, 128, 512), BF),
            sem((2, parts, n)), sem((2, parts, n)),
            sem((2, parts, n)), sem((2, parts, n)),
            sem((parts, n_expert)), sem((parts, n_expert)),
            sem((4,)), sem((3,)),
            *reduce_scratch(early, n_context),
        ],
        compiler_params=pltpu.CompilerParams(
            collective_id=1, has_side_effects=True, vmem_limit_bytes=63 * 1024 * 1024
        ),
        name="mix_and_experts",
    )(resid_m, cot_m, live_m, gain, wc, w_in, w_back)


def backward_kernel(
    d_attn, tok_a, qkv_a, att_a, lse, kmark, qmark, gain, wqkv, wout, out_m, part, sums_in,
    dtok_o, last_o, out_o, sums, gq_o, go_o, gg_o,
    da, tok, qkv, att, datt, delta, dkv, dqkv, dtok, bias, own,
    out_s, out_r, tok_s, tok_r, in_s, own_s, *rest,
    n_expert, n_context, n_dp, base,
):
    e, c, me, n, peer = ring(n_expert, n_context)
    seqs, length, width = da.shape
    half = length // n_context
    slab = half // n_expert
    qn = 256
    loads = [
        pltpu.make_async_copy(src, dst, in_s.at[i])
        for i, (src, dst) in enumerate(
            ((d_attn, da), (att_a, att), (qkv_a, qkv), (tok_a, tok),
             (part.at[pl.ds(0, own.shape[0])], own))
        )
    ]
    reduce = Reduce(own, *rest[:4], rest[4:], sums, base, 2, n_dp, n_context)
    for cp in loads:
        cp.start()
    enter(peer, n, reduce)
    crossing = []
    per_half = out_m.shape[0] // n_context
    sub = slab // per_half
    for b in range(per_half):
        mine = pl.ds(pl.multiple_of(e * slab + b * sub, sub), sub)
        for k in range(1, n):
            j, pe, pc = peer(k)
            cp = pltpu.make_async_remote_copy(
                src_ref=out_m.at[pc * per_half + b, pl.ds(pe * seqs, seqs)],
                dst_ref=out_o.at[c, :, mine, :],
                send_sem=out_s.at[b, k], recv_sem=out_r.at[b, k],
                device_id={"expert": pe, "context": pc}, device_id_type=MESH,
            )
            cp.start()
            crossing.append(cp)
        cp = pltpu.make_async_copy(
            out_m.at[c * per_half + b, pl.ds(e * seqs, seqs)], out_o.at[c, :, mine, :], own_s.at[2, b]
        )
        cp.start()
        crossing.append(cp)
    lane = lax.broadcasted_iota(jnp.int32, (qn, 128), 1)
    gg_o[...] = jnp.zeros_like(gg_o)
    for cp in loads:
        cp.wait()
    pairs = width // 128
    for s in range(seqs):
        datt[...] = dot(da[s], wout[...], ((1,), (1,))).astype(BF)
        turned = dot(wout[...], da[s], ((1,), (1,))).astype(BF).astype(F32) * att[s].astype(F32)
        delta[...] = jnp.sum(turned.reshape(HEADS, width // HEADS, length), 1)
        go = dot(att[s], da[s])
        go_o[...] = go if s == 0 else go_o[...] + go
        dkv[...] = jnp.zeros_like(dkv)
        for qb in range(length // qn):
            kk = (qb + 1) * qn
            rows = pl.ds(qb * qn, qn)
            mask_bias(bias, kmark, qmark, s, qb * qn, qn)

            def pair(hp, _):
                at = pl.multiple_of(hp * 128, 128)
                q2 = qkv[s, rows, pl.ds(at, 128)] * BF(0.125)
                k2 = qkv[s, pl.ds(0, kk), pl.ds(width + at, 128)]
                v2 = qkv[s, pl.ds(0, kk), pl.ds(2 * width + at, 128)]
                do2 = datt[rows, pl.ds(at, 128)]
                kt = k2.T
                dqs, dss, lows, qms, doms = [], [], [], [], []
                for h in range(2):
                    mine = (lane >= 64) if h else (lane < 64)
                    qm = jnp.where(mine, q2, jnp.zeros_like(q2))
                    dom = jnp.where(mine, do2, jnp.zeros_like(do2))
                    st = dot(k2, qm, ((1,), (1,))) + bias[pl.ds(0, kk), :]
                    p = jnp.exp(st - lse[s, pl.ds(2 * hp + h, 1), rows])
                    dp = dot(v2, dom, ((1,), (1,)))
                    ds = (p * (dp - delta[pl.ds(2 * hp + h, 1), rows])).astype(BF)
                    dqs.append(dot(kt[h * 64 : h * 64 + 64], ds))
                    dss.append(ds)
                    lows.append(p.astype(BF))
                    qms.append(qm)
                    doms.append(dom)
                dqkv[rows, pl.ds(at, 128)] = (
                    (jnp.concatenate(dqs, 0) * 0.125).T.astype(BF)
                )
                dkv[pl.ds(0, kk), pl.ds(at, 128)] += dot(dss[0], qms[0]) + dot(dss[1], qms[1])
                dkv[pl.ds(0, kk), pl.ds(width + at, 128)] += dot(lows[0], doms[0]) + dot(
                    lows[1], doms[1]
                )
                @pl.when(lax.rem(hp, 2) == 1)
                def _():
                    reduce.tick(((s * (length // qn) + qb) * pairs + hp) // 2)

                return 0

            lax.fori_loop(0, pairs, pair, 0)
        dqkv[:, pl.ds(width, 2 * width)] = dkv[...].astype(BF)
        for h in range(n_context):
            rows = pl.ds(h * half, half)
            normed, rstd = normalized(tok[s, h].astype(F32))
            a = (normed * gain[...]).astype(BF)
            gq = dot(a, dqkv[rows, :], ((0,), (0,)))
            gq_o[...] = gq if s == 0 and h == 0 else gq_o[...] + gq
            d_a = dot(dqkv[rows, :], wqkv[...], ((1,), (1,)))
            gg_o[...] += jnp.sum(d_a * normed, 0, keepdims=True)
            q = d_a * gain[...]
            dt = da[s, rows, :].astype(F32) + rstd * (
                q - jnp.mean(q, -1, keepdims=True) - normed * jnp.mean(q * normed, -1, keepdims=True)
            )
            dtok[s, h] = dt.astype(BF)
        if s == seqs - 1:
            cp = pltpu.make_async_copy(dtok.at[s], last_o, own_s.at[0, 1])
            cp.start()
            crossing.append(cp)
            continue
        for k in range(1, n_context):
            pc = lax.rem(c + k, n_context)
            cp = pltpu.make_async_remote_copy(
                src_ref=dtok.at[s, pc], dst_ref=dtok_o.at[c, s],
                send_sem=tok_s.at[s, k], recv_sem=tok_r.at[s, k],
                device_id={"context": pc}, device_id_type=MESH,
            )
            cp.start()
            crossing.append(cp)
        cp = pltpu.make_async_copy(dtok.at[s, c], dtok_o.at[c, s], own_s.at[1, s])
        cp.start()
        crossing.append(cp)
    reduce.finish(seqs * (length // qn) * pairs // 2)
    for cp in crossing:
        cp.wait()


def backward(
    d_attn, tok_a, qkv, att, lse, kmark, qmark, gain, wqkv, wout, out_m, part, sums,
    n_expert, n_context, n_dp, count,
):
    seqs, length, width = d_attn.shape
    half = length // n_context
    n = n_expert * n_context
    sem = pltpu.SemaphoreType.DMA
    return pl.pallas_call(
        functools.partial(
            backward_kernel, n_expert=n_expert, n_context=n_context, n_dp=n_dp,
            base=sums.shape[1] - part.shape[0],
        ),
        out_shape=(
            jax.ShapeDtypeStruct((n_context, seqs, half, width), BF),
            jax.ShapeDtypeStruct((n_context, half, width), BF),
            jax.ShapeDtypeStruct((n_context, seqs, half, width), BF),
            jax.ShapeDtypeStruct(sums.shape, BF),
            jax.ShapeDtypeStruct((width, 3 * width), F32),
            jax.ShapeDtypeStruct((width, width), F32),
            jax.ShapeDtypeStruct((1, width), F32),
        ),
        in_specs=[ANY, ANY, ANY, ANY, VM, VM, VM, VM, VM, VM, ANY, ANY, ANY],
        out_specs=(ANY, ANY, ANY, ANY, VM, VM, VM),
        input_output_aliases={12: 3},
        scratch_shapes=[
            pltpu.VMEM((seqs, length, width), BF),
            pltpu.VMEM((seqs, n_context, half, width), BF),
            pltpu.VMEM((seqs, length, 3 * width), BF),
            pltpu.VMEM((seqs, width, length), BF),
            pltpu.VMEM((length, width), BF),
            pltpu.VMEM((HEADS, length), F32),
            pltpu.VMEM((length, 2 * width), F32),
            pltpu.VMEM((length, 3 * width), BF),
            pltpu.VMEM((seqs, n_context, half, width), BF),
            pltpu.VMEM((length, 256), F32),
            pltpu.VMEM((count, *part.shape[1:]), BF),
            sem((2, n)), sem((2, n)),
            sem((seqs, n_context)), sem((seqs, n_context)),
            sem((5,)), sem((3, 2)),
            *reduce_scratch(count, n_context),
        ],
        compiler_params=pltpu.CompilerParams(
            collective_id=2, has_side_effects=True, vmem_limit_bytes=VMEM_LIMIT
        ),
        name="attend_backward",
    )(d_attn, tok_a, qkv, att, lse, kmark, qmark, gain, wqkv, wout, out_m, part, sums)


def share_kernel(
    gq, go, gc, gg, gm, sq, sq_mix, live, last, part_in, dtok_in, sums_in,
    packed_o, misc_o, dtok_o, sums,
    pack, other, chip, corners, along, whole, own,
    core_s, core_r, chip_s, chip_r, dp_s, dp_r, dp2_s, dp2_r, out_s, out_r, fin_s, fin_r, tok_s, tok_r, own_s, *rest,
    n_expert, n_context, n_dp,
):
    e, c, z = (lax.axis_index(a) for a in ("expert", "context", "dp"))
    core = lax.rem(e, 2)
    chips = n_expert // 2 * n_context
    me = lax.div(e, 2) * n_context + c
    width = go.shape[1]
    total = pack.shape[0]
    part = total // 2
    piece = part // chips
    lanes = width // n_dp
    twin = {"expert": e + 1 - 2 * core}

    def chip_at(k):
        j = lax.rem(me + k, chips)
        return j, {"expert": lax.div(j, n_context) * 2 + core, "context": lax.rem(j, n_context)}

    barrier = pltpu.get_barrier_semaphore()
    count = own.shape[0]
    load = pltpu.make_async_copy(
        part_in.at[pl.ds(part_in.shape[0] - count, count)], own, own_s.at[0]
    )
    load.start()
    reduce = Reduce(own, *rest[:4], rest[4:], sums, sums.shape[1] - count, 2, n_dp, n_context)
    ticks = [0]

    def tick(times):
        for _ in range(times):
            if ticks[0] < count + 2 * (n_dp - 1):
                reduce.tick(ticks[0])
                ticks[0] += 1

    seq = dtok_o.shape[1] - 1
    where = [twin] + [chip_at(k)[1] for k in range(1, chips)]
    where += [{"dp": lax.rem(z + k, n_dp)} for k in range(1, n_dp)]
    for to in where:
        pl.semaphore_signal(barrier, inc=1, device_id=to, device_id_type=MESH)
    for b in range(3):
        pack[pl.ds(b * width, width), :] = gq[:, pl.ds(b * width, width)].astype(BF)
    pack[pl.ds(3 * width, width), :] = go[...].astype(BF)
    at = gc.shape[0]
    misc_o[...] = jnp.zeros_like(misc_o)
    misc_o[pl.ds(0, at), :] = gc[...]
    for row in (gg[...], gm[...], sq_mix[pl.ds(0, 1), :], sq[...], sq_mix[pl.ds(1, 1), :], live[...]):
        misc_o[pl.ds(at, 1), :] = row
        at += 1
    pack[pl.ds(4 * width, total - 4 * width), :] = jnp.zeros((total - 4 * width, width), BF)
    pack[pl.ds(4 * width, misc_o.shape[0]), :] = misc_o[...].astype(BF)
    pl.semaphore_wait(barrier, len(where))

    def remote(src, dst, ss, rs, to):
        cp = pltpu.make_async_remote_copy(
            src_ref=src, dst_ref=dst, send_sem=ss, recv_sem=rs, device_id=to, device_id_type=MESH
        )
        cp.start()
        return cp

    def rows(i, n):
        return pl.ds(pl.multiple_of(i * n, 16), n)

    bulk = [
        remote(
            last.at[lax.rem(c + k, n_context)], dtok_o.at[c, seq], tok_s.at[k], tok_r.at[k],
            {"context": lax.rem(c + k, n_context)},
        )
        for k in range(1, n_context)
    ]
    keep = pltpu.make_async_copy(last.at[c], dtok_o.at[c, seq], own_s.at[1])
    keep.start()
    sent = []
    for k in range(chips):
        j = lax.rem(me + k + 1, chips)
        at = pl.ds(pl.multiple_of((1 - core) * part + j * piece, 16), piece)
        sent.append(remote(pack.at[at], other.at[rows(j, piece)], core_s.at[k], core_r.at[k], twin))
    first = list(sent)
    for k in range(chips):
        j = lax.rem(me + k + 1, chips)
        first[k].wait_recv()
        at = pl.ds(pl.multiple_of(core * part + j * piece, 16), piece)
        chip[rows(j, piece), :] = (
            pack[at, :].astype(F32) + other[rows(j, piece), :].astype(F32)
        ).astype(BF)
        if k < chips - 1:
            _, to = chip_at(k + 1)
            sent.append(
                remote(chip.at[rows(j, piece)], corners.at[k], chip_s.at[k], chip_r.at[k], to)
            )
    load.wait()
    tick(4)
    acc = chip[rows(me, piece), :].astype(F32)
    for k in range(chips - 1):
        sent[chips + k].wait_recv()
        acc += corners[k].astype(F32)
    chip[rows(me, piece), :] = acc.astype(BF)
    mine = pl.ds(pl.multiple_of(z * lanes, lanes), lanes)
    steps = []
    for k in range(1, n_dp):
        to = lax.rem(z + k, n_dp)
        theirs = pl.ds(pl.multiple_of(to * lanes, lanes), lanes)
        steps.append(
            remote(
                chip.at[rows(me, piece), theirs], along.at[k - 1], dp_s.at[k - 1], dp_r.at[k - 1],
                {"dp": to},
            )
        )
    tick(2)
    acc = chip[rows(me, piece), mine].astype(F32)
    for k in range(1, n_dp):
        steps[k - 1].wait_recv()
        acc += along[k - 1].astype(F32)
    home = pl.ds(pl.multiple_of(core * part + me * piece, 16), piece)
    whole[home, mine] = acc.astype(BF)
    back = []
    for k in range(1, n_dp):
        to = lax.rem(z + k, n_dp)
        back.append(
            remote(
                whole.at[home, mine], whole.at[home, mine], dp2_s.at[k - 1], dp2_r.at[k - 1],
                {"dp": to},
            )
        )
    tick(2)
    for cp in back:
        cp.wait_recv()
    spread = [remote(whole.at[home], whole.at[home], fin_s.at[0], fin_r.at[0], twin)]
    outs = []
    for k in range(1, chips):
        _, to = chip_at(k)
        outs.append(remote(whole.at[home], whole.at[home], out_s.at[k - 1], out_r.at[k - 1], to))
    tick(3)
    for k in range(1, chips):
        outs[k - 1].wait_recv()
        tick(1)
        j = lax.rem(me + chips - k, chips)
        got = whole.at[pl.ds(pl.multiple_of(core * part + j * piece, 16), piece)]
        spread.append(remote(got, got, fin_s.at[k], fin_r.at[k], twin))
    for cp in spread:
        cp.wait_recv()
    stored = pltpu.make_async_copy(whole.at[pl.ds(0, 4 * width)], packed_o, own_s.at[2])
    stored.start()
    misc_o[...] = whole[pl.ds(4 * width, misc_o.shape[0]), :].astype(F32)
    reduce.finish(ticks[0])
    for cp in sent + steps + back + outs + spread:
        cp.wait_send()
    for cp in bulk:
        cp.wait()
    keep.wait()
    stored.wait()


def share(gq, go, gc, gg, gm, sq, sq_mix, live, last, part_in, dtok, sums, n_expert, n_context, n_dp, count):
    width = go.shape[1]
    chips = n_expert // 2 * n_context
    unit = 2 * chips * 16
    rows = -(-(gc.shape[0] + 6) // 16) * 16
    total = -(-(4 * width + rows) // unit) * unit
    part = total // 2
    piece = part // chips
    sem = pltpu.SemaphoreType.DMA
    return pl.pallas_call(
        functools.partial(share_kernel, n_expert=n_expert, n_context=n_context, n_dp=n_dp),
        out_shape=(
            jax.ShapeDtypeStruct((4 * width, width), BF),
            jax.ShapeDtypeStruct((rows, width), F32),
            jax.ShapeDtypeStruct(dtok.shape, BF),
            jax.ShapeDtypeStruct(sums.shape, BF),
        ),
        in_specs=[VM] * 8 + [ANY] * 4,
        out_specs=(ANY, VM, ANY, ANY),
        input_output_aliases={10: 2, 11: 3},
        scratch_shapes=[
            pltpu.VMEM((total, width), BF),
            pltpu.VMEM((part, width), BF),
            pltpu.VMEM((part, width), BF),
            pltpu.VMEM((max(1, chips - 1), piece, width), BF),
            pltpu.VMEM((max(1, n_dp - 1), piece, width // n_dp), BF),
            pltpu.VMEM((total, width), BF),
            pltpu.VMEM((count, *sums.shape[2:]), BF),
            sem((chips,)), sem((chips,)), sem((chips,)), sem((chips,)),
            sem((n_dp,)), sem((n_dp,)), sem((n_dp,)), sem((n_dp,)),
            sem((chips,)), sem((chips,)), sem((chips,)), sem((chips,)),
            sem((n_context,)), sem((n_context,)), sem((3,)),
            *reduce_scratch(count, n_context),
        ],
        compiler_params=pltpu.CompilerParams(
            collective_id=3, has_side_effects=True, vmem_limit_bytes=VMEM_LIMIT
        ),
        name="share_gradients",
    )(gq, go, gc, gg, gm, sq, sq_mix, live, last, part_in, dtok, sums)


def widen_kernel(src_in, src_back, packed, gi, gb, gq, go):
    gi[0] = src_in[0].reshape(gi.shape[1:]).astype(F32)
    gb[0] = src_back[0].reshape(gb.shape[1:]).astype(F32)
    width = go.shape[1]
    rows = go.shape[0]
    at = (pl.program_id(0) * pl.num_programs(1) + pl.program_id(1)) * rows
    for b in range(4):
        block = packed[pl.ds(pl.multiple_of(b * width + at, 16), rows), :].astype(F32)
        if b < 3:
            gq[:, pl.ds(b * width, width)] = block
        else:
            go[...] = block


def widen(sums, packed, width, ff):
    n_context, blocks = sums.shape[:2]
    tiles = ff // 512
    per = blocks // (2 * tiles)
    rows = width // (n_context * tiles)
    return pl.pallas_call(
        widen_kernel,
        grid=(n_context, tiles),
        out_shape=(
            jax.ShapeDtypeStruct((n_context, width, ff), F32),
            jax.ShapeDtypeStruct((n_context, ff, width), F32),
            jax.ShapeDtypeStruct((width, 3 * width), F32),
            jax.ShapeDtypeStruct((width, width), F32),
        ),
        in_specs=[
            pl.BlockSpec((1, per, 128, 512), lambda c, f: (c, f, 0, 0)),
            pl.BlockSpec((1, per, 128, 512), lambda c, f: (c, tiles + f, 0, 0)),
            pl.BlockSpec(packed.shape, lambda c, f: (0, 0)),
        ],
        out_specs=(
            pl.BlockSpec((1, width, 512), lambda c, f: (c, 0, f)),
            pl.BlockSpec((1, 512, width), lambda c, f: (c, f, 0)),
            pl.BlockSpec((rows, 3 * width), lambda c, f: (c * tiles + f, 0)),
            pl.BlockSpec((rows, width), lambda c, f: (c * tiles + f, 0)),
        ),
        compiler_params=pltpu.CompilerParams(vmem_limit_bytes=32 * 1024 * 1024),
        name="widen_sums",
    )(sums, sums, packed)


def per_device(n_expert, n_context, n_dp, tokens, gain_attn, wqkv, w_out, gain_mix, w_control, w_in, w_back, segments, valid, cotangent):
    reps, seqs, half, width = tokens.shape
    length = half * n_context
    slab = half // n_expert
    group = seqs * n_expert
    e, c = lax.axis_index("expert"), lax.axis_index("context")

    def pick(x, i, axis=0):
        return lax.dynamic_index_in_dim(x, i, axis, keepdims=False)

    seg_a, valid_a = pick(segments, c), pick(valid, c)
    kmark = jnp.where(valid_a > 0, seg_a, -1)[:, :, None]
    qmark = seg_a[:, None, :]
    lengths = jnp.sum((valid_a > 0).astype(F32), 1)
    live = jnp.broadcast_to(lengths[:, None, None], (seqs, 8, 128))
    resid_m, cot_m, live_m, tok_a, qkv, att, lse, sq = forward(
        tokens, cotangent, kmark, qmark, live, gain_attn[None], wqkv, w_out, n_expert, n_context
    )
    blocks = 2 * width * w_in.shape[-1] // (128 * 512)
    first, final = blocks * 11 // 32, blocks * 10 // 32
    d_attn, out_m, part, sums, grad_control, grad_gain_mix, sq_mix = mix(
        resid_m, cot_m, live_m, gain_mix[None], w_control, w_in, w_back,
        n_expert, n_context, n_dp, first,
    )
    d_tokens, last, output, sums, grad_qkv, grad_out, grad_gain = backward(
        d_attn.reshape(seqs, length, width), tok_a, qkv, att, lse, kmark, qmark, gain_attn[None],
        wqkv, w_out, out_m, part, sums, n_expert, n_context, n_dp, blocks - first - final,
    )
    n_all = grad_control.shape[0]
    count = jnp.pad(jnp.sum(lengths)[None, None], ((0, 0), (0, width - 1)))
    packed, misc, d_tokens, sums = share(
        grad_qkv, grad_out, grad_control, grad_gain, grad_gain_mix, sq, sq_mix, count,
        last, part, d_tokens, sums, n_expert, n_context, n_dp, final,
    )
    grad_control = misc[:n_all].T
    grad_gain, grad_gain_mix = misc[n_all], misc[n_all + 1]
    squares = jnp.sum(misc[n_all + 2 : n_all + 6], 1)
    grad_in, grad_back, grad_qkv, grad_out = widen(sums, packed, width, w_in.shape[-1])
    stats = jnp.sqrt(squares[:3] / (squares[3] * width))
    return (
        output, d_tokens, grad_gain, grad_qkv, grad_out, grad_gain_mix, grad_control,
        grad_in, grad_back, stats,
    )


def solution(mesh):
    shards = P("dp", "expert", "context", None)
    rows = P("dp", "expert", None)
    experts = P("expert", None, None)
    return jax.shard_map(
        functools.partial(
            per_device, mesh.shape["expert"], mesh.shape["context"], mesh.shape["dp"]
        ),
        mesh=mesh,
        in_specs=(shards, P(), P(), P(), P(), P(), experts, experts, rows, rows, shards),
        out_specs=(shards, shards, P(), P(), P(), P(), P(), experts, experts, P()),
        check_vma=False,
    )
```

```python
import functools
import jax
import jax.numpy as jnp
from jax import lax
from jax.experimental import pallas as pl
from jax.experimental.pallas import tpu as pltpu
from jax.sharding import PartitionSpec as P

HEADS = 8
NEG_FILL = -1e30
MESH = pl.DeviceIdType.MESH
BF = jnp.bfloat16
F32 = jnp.float32
ANY = pl.BlockSpec(memory_space=pl.ANY)
VM = pl.BlockSpec(memory_space=pltpu.VMEM)
VMEM_LIMIT = 60 * 1024 * 1024


def dot(a, b, dims=((1,), (0,))):
    return lax.dot_general(a, b, (dims, ((), ())), preferred_element_type=F32)


def normalized(x):
    center = x - jnp.mean(x, -1, keepdims=True)
    spread = jnp.mean(center * center, -1, keepdims=True)
    rstd = lax.rsqrt(spread + 1e-05)
    return center * rstd, rstd


def ring(n_expert, n_context):
    e = lax.axis_index("expert")
    c = lax.axis_index("context")
    n = n_expert * n_context
    me = e * n_context + c

    def peer(k):
        j = lax.rem(me + k, n)
        pe = lax.div(j, n_context)
        pc = lax.rem(j, n_context)
        return j, pe, pc

    return e, c, me, n, peer


def enter(peer, n, reduce=None):
    barrier = pltpu.get_barrier_semaphore()
    for k in range(1, n):
        _, pe, pc = peer(k)
        pl.semaphore_signal(
            barrier, inc=1, device_id={"expert": pe, "context": pc}, device_id_type=MESH
        )
    extra = 0 if reduce is None else reduce.greet()
    pl.semaphore_wait(barrier, n - 1 + extra)


class Reduce:
    def __init__(self, own, rin, lin, ring_r, ring_l, sems, sums, base, lag, n_dp, n_context):
        self.lag = lag
        self.own, self.ins, self.rings, self.sums = own, (rin, lin), (ring_r, ring_l), sums
        self.send, self.recv, self.swap_s, self.swap_r, self.keep = sems
        self.count, self.slots = own.shape[0], ring_r.shape[0]
        self.n_dp, self.n_context, self.base = n_dp, n_context, base
        self.z, self.c = lax.axis_index("dp"), lax.axis_index("context")

    def greet(self):
        barrier = pltpu.get_barrier_semaphore()
        z, last = self.z, self.n_dp - 1
        for here, to in ((z > 0, z - 1), (z < last, z + 1)):

            @pl.when(here)
            def _():
                pl.semaphore_signal(barrier, inc=1, device_id={"dp": to}, device_id_type=MESH)

        return jnp.minimum(z, 1) + jnp.minimum(last - z, 1)

    def hop(self, way, i):
        to = self.z + (1 if way == 0 else -1)
        slot = lax.rem(i, self.slots)
        return pltpu.make_async_remote_copy(
            src_ref=self.rings[way].at[slot], dst_ref=self.ins[way].at[i],
            send_sem=self.send.at[way, slot], recv_sem=self.recv.at[way, i],
            device_id={"dp": to}, device_id_type=MESH,
        )

    def swaps(self, i):
        out = []
        for k in range(1, self.n_context):
            pc = lax.rem(self.c + k, self.n_context)
            out.append(
                pltpu.make_async_remote_copy(
                    src_ref=self.own.at[i], dst_ref=self.sums.at[self.c, self.base + i],
                    send_sem=self.swap_s.at[k, i], recv_sem=self.swap_r.at[k, i],
                    device_id={"context": pc}, device_id_type=MESH,
                )
            )
        out.append(
            pltpu.make_async_copy(
                self.own.at[i], self.sums.at[self.c, self.base + i], self.keep.at[i]
            )
        )
        return out

    def tick(self, t, swap=True):
        last = self.n_dp - 1
        for way in range(2):
            behind = self.z if way == 0 else last - self.z
            i = t - self.lag * behind
            has_in, has_out = behind > 0, behind < last

            @pl.when((i >= 0) & (i < self.count))
            def _():
                @pl.when(has_in)
                def _():
                    self.hop(way, i).wait_recv()

                @pl.when(has_out)
                def _():
                    @pl.when(i >= self.slots)
                    def _():
                        self.hop(way, i - self.slots).wait_send()

                    slot = lax.rem(i, self.slots)

                    @pl.when(has_in)
                    def _():
                        self.rings[way][slot] = (
                            self.ins[way][i].astype(F32) + self.own[i].astype(F32)
                        ).astype(BF)

                    @pl.when(jnp.logical_not(has_in))
                    def _():
                        self.rings[way][slot] = self.own[i]

                    self.hop(way, i).start()

        m = t - self.lag * jnp.maximum(self.z, last - self.z)

        @pl.when((m >= 0) & (m < self.count))
        def _():
            first, final = self.z == 0, self.z == last

            @pl.when(first)
            def _():
                self.own[m] = (self.own[m].astype(F32) + self.ins[1][m].astype(F32)).astype(BF)

            @pl.when(final)
            def _():
                self.own[m] = (self.own[m].astype(F32) + self.ins[0][m].astype(F32)).astype(BF)

            @pl.when(jnp.logical_not(first | final))
            def _():
                self.own[m] = (
                    self.own[m].astype(F32) + self.ins[0][m].astype(F32) + self.ins[1][m].astype(F32)
                ).astype(BF)

            if swap:
                for cp in self.swaps(m):
                    cp.start()

    def release(self, t):
        done = jnp.minimum(t - self.lag * jnp.maximum(self.z, self.n_dp - 1 - self.z), self.count)

        def one(m, _):
            @pl.when(m < done)
            def _():
                for cp in self.swaps(m):
                    cp.start()

            return 0

        lax.fori_loop(0, self.count, one, 0)

    def finish(self, t):
        lax.fori_loop(t, self.count + self.lag * (self.n_dp - 1), lambda i, _: (self.tick(i), 0)[1], 0)
        last = self.n_dp - 1
        for way in range(2):

            @pl.when((self.z if way == 0 else last - self.z) < last)
            def _():
                for i in range(max(0, self.count - self.slots), self.count):
                    self.hop(way, i).wait_send()

        def drain(i, _):
            for cp in self.swaps(i):
                cp.wait()
            return 0

        lax.fori_loop(0, self.count, drain, 0)


def reduce_scratch(count, n_context, slots=4):
    sem = pltpu.SemaphoreType.DMA
    block = pltpu.VMEM((count, 128, 512), BF)
    ring_block = pltpu.VMEM((slots, 128, 512), BF)
    return [
        block, block, ring_block, ring_block,
        sem((2, slots)), sem((2, count)), sem((n_context, count)), sem((n_context, count)), sem((count,)),
    ]


def mask_bias(bias, kmark, qmark, s, q0, qn):
    kk = q0 + qn
    place_k = lax.broadcasted_iota(jnp.int32, (kk, qn), 0)
    place_q = lax.broadcasted_iota(jnp.int32, (kk, qn), 1) + q0
    same = kmark[s, pl.ds(0, kk), :] == qmark[s, :, pl.ds(q0, qn)]
    bias[pl.ds(0, kk), :] = jnp.where(same & (place_k <= place_q), 0.0, NEG_FILL)


def forward_kernel(
    tokens, cot, kmark, qmark, live, gain, wqkv, wout,
    resid_m, cot_m, live_m, tok_a, qkv_o, att_o, lse_o, sq_o,
    tok, qkv, vt, att, att_t, res, bias,
    tok_s, tok_r, cot_s, cot_r, res_s, res_r, live_s, live_r, own_s, save_s,
    *, n_expert, n_context,
):
    e, c, me, n, peer = ring(n_expert, n_context)
    seqs, length, width = qkv_o.shape[0], qkv_o.shape[1], tokens.shape[-1]
    half = length // n_context
    slab = half // n_expert
    qn = 256
    enter(peer, n)
    def outgoing(s):
        out = []
        for k in range(1, n_context):
            pc = lax.rem(c + k, n_context)
            out.append(
                pltpu.make_async_remote_copy(
                    src_ref=tokens.at[pc, s], dst_ref=tok.at[s, c],
                    send_sem=tok_s.at[s, k], recv_sem=tok_r.at[s, k],
                    device_id={"context": pc}, device_id_type=MESH,
                )
            )
        return out

    for s in range(seqs):
        for cp in outgoing(s):
            cp.start()
    own = []
    for s in range(seqs):
        cp = pltpu.make_async_copy(tokens.at[c, s], tok.at[s, c], own_s.at[s])
        cp.start()
        own.append(cp)

    def project(s, h):
        x = tok[s, h].astype(F32)
        y, _ = normalized(x)
        a = (y * gain[...]).astype(BF)
        at = pl.ds(pl.multiple_of(h * half, half), half)
        qkv[s, at, :] = dot(a, wqkv[...]).astype(BF)
        vt[s, :, at] = dot(wqkv[:, pl.ds(2 * width, width)], a, ((0,), (1,))).astype(BF)

    for s in range(seqs):
        own[s].wait()
        project(s, c)
    for cp in outgoing(0):
        cp.wait()
    mine = pl.ds(e * seqs, seqs)
    local = [pltpu.make_async_copy(live, live_m.at[mine], own_s.at[seqs + 1])]
    crossing = []
    for k in range(1, n_expert):
        pe = lax.rem(e + k, n_expert)
        crossing.append(
            pltpu.make_async_remote_copy(
                src_ref=live, dst_ref=live_m.at[mine], send_sem=live_s.at[k], recv_sem=live_r.at[k],
                device_id={"expert": pe}, device_id_type=MESH,
            )
        )
    for k in range(1, n):
        j, pe, pc = peer(k)
        crossing.append(
            pltpu.make_async_remote_copy(
                src_ref=cot.at[pc, :, pl.ds(pl.multiple_of(pe * slab, slab), slab), :],
                dst_ref=cot_m.at[mine, c],
                send_sem=cot_s.at[k], recv_sem=cot_r.at[k],
                device_id={"expert": pe, "context": pc}, device_id_type=MESH,
            )
        )
    local.append(
        pltpu.make_async_copy(
            cot.at[c, :, pl.ds(pl.multiple_of(e * slab, slab), slab), :],
            cot_m.at[mine, c], own_s.at[seqs],
        )
    )
    for cp in local + crossing:
        cp.start()
    saves = [
        pltpu.make_async_copy(qkv, qkv_o, save_s.at[0]),
        pltpu.make_async_copy(tok, tok_a, save_s.at[1]),
    ]
    lane = lax.broadcasted_iota(jnp.int32, (qn, 128), 1)
    moving = []
    total = jnp.zeros((1, width), F32)
    for s in range(seqs):
        if s > 0:
            for cp in outgoing(s):
                cp.wait()
        for k in range(1, n_context):
            project(s, lax.rem(c + k, n_context))
        if s == seqs - 1:
            for cp in saves:
                cp.start()
        for qb in range(length // qn):
            kk = (qb + 1) * qn
            rows = pl.ds(qb * qn, qn)
            mask_bias(bias, kmark, qmark, s, qb * qn, qn)

            for at in range(0, width, 128):
                q2 = qkv[s, rows, pl.ds(at, 128)] * BF(0.125)
                k2 = qkv[s, pl.ds(0, kk), pl.ds(width + at, 128)]
                outs = []
                for h in range(2):
                    mine = (lane >= 64) if h else (lane < 64)
                    qm = jnp.where(mine, q2, jnp.zeros_like(q2))
                    st = dot(k2, qm, ((1,), (1,))) + bias[pl.ds(0, kk), :]
                    top = jnp.max(st, 0, keepdims=True)
                    p = jnp.exp(st - top)
                    tot = jnp.sum(p, 0, keepdims=True)
                    lse_o[s, pl.ds(at // 64 + h, 1), rows] = top + jnp.log(tot)
                    vh = vt[s, pl.ds(at + 64 * h, 64), pl.ds(0, kk)]
                    outs.append(dot(vh, p.astype(BF)) * (1.0 / tot))
                both = jnp.concatenate(outs, 0)
                att_t[s, pl.ds(at, 128), rows] = both.astype(BF)
                att[s, rows, pl.ds(at, 128)] = both.T.astype(BF)
            h = qb * qn // half
            attn_out = dot(att[s, rows, :], wout[...])
            within = qb * qn - h * half
            x = tok[s, h, pl.ds(within, qn), :].astype(F32)
            res[s, h, pl.ds(within, qn), :] = (x + attn_out).astype(BF)
            ok = kmark[s, rows, :] >= 0
            total += jnp.sum(jnp.where(ok, attn_out * attn_out, 0.0), 0, keepdims=True)
            if (qb + 1) * qn == (h + 1) * half:
                for k in range(1, n_expert):
                    pe = lax.rem(e + k, n_expert)
                    cp = pltpu.make_async_remote_copy(
                        src_ref=res.at[s, h, pl.ds(pl.multiple_of(pe * slab, slab), slab), :],
                        dst_ref=resid_m.at[e * seqs + s, h],
                        send_sem=res_s.at[s, h, k], recv_sem=res_r.at[s, h, k],
                        device_id={"expert": pe}, device_id_type=MESH,
                    )
                    cp.start()
                    moving.append(cp)
                cp = pltpu.make_async_copy(
                    res.at[s, h, pl.ds(pl.multiple_of(e * slab, slab), slab), :],
                    resid_m.at[e * seqs + s, h], res_s.at[s, h, 0],
                )
                cp.start()
                moving.append(cp)
    sq_o[...] = total
    keep = pltpu.make_async_copy(att_t, att_o, save_s.at[2])
    keep.start()
    for cp in saves + moving + crossing + local + [keep]:
        cp.wait()


def forward(tokens, cot, kmark, qmark, live, gain, wqkv, wout, n_expert, n_context):
    reps, seqs, half, width = tokens.shape
    length = half * n_context
    slab = half // n_expert
    group = seqs * n_expert
    n = n_expert * n_context
    sem = pltpu.SemaphoreType.DMA
    return pl.pallas_call(
        functools.partial(forward_kernel, n_expert=n_expert, n_context=n_context),
        out_shape=(
            jax.ShapeDtypeStruct((group, n_context, slab, width), BF),
            jax.ShapeDtypeStruct((group, n_context, slab, width), BF),
            jax.ShapeDtypeStruct((group, *live.shape[1:]), F32),
            jax.ShapeDtypeStruct((seqs, n_context, half, width), BF),
            jax.ShapeDtypeStruct((seqs, length, 3 * width), BF),
            jax.ShapeDtypeStruct((seqs, width, length), BF),
            jax.ShapeDtypeStruct((seqs, HEADS, length), F32),
            jax.ShapeDtypeStruct((1, width), F32),
        ),
        in_specs=[ANY, ANY, VM, VM, VM, VM, VM, VM],
        out_specs=(ANY, ANY, ANY, ANY, ANY, ANY, VM, VM),
        scratch_shapes=[
            pltpu.VMEM((seqs, n_context, half, width), BF),
            pltpu.VMEM((seqs, length, 3 * width), BF),
            pltpu.VMEM((seqs, width, length), BF),
            pltpu.VMEM((seqs, length, width), BF),
            pltpu.VMEM((seqs, width, length), BF),
            pltpu.VMEM((seqs, n_context, half, width), BF),
            pltpu.VMEM((length, 256), F32),
            sem((seqs, n_context)), sem((seqs, n_context)),
            sem((n,)), sem((n,)),
            sem((seqs, n_context, n_expert)), sem((seqs, n_context, n_expert)),
            sem((n_expert,)), sem((n_expert,)),
            sem((seqs + 2,)), sem((3,)),
        ],
        compiler_params=pltpu.CompilerParams(
            collective_id=0, has_side_effects=True, vmem_limit_bytes=VMEM_LIMIT
        ),
        name="attend_forward",
    )(tokens, cot, kmark, qmark, live, gain, wqkv, wout)


def mix_kernel(
    resid_m, cot_m, live_m, gain, wc, w_in, w_back,
    d_attn, out_m, part_o, sums, gc_o, gm_o, sq_o,
    res, cot, u, wts, mixed, dexp, xs, des, eos, dms, eor, dmr, win, wback, acts, d_pres, glow,
    go_s, go_r, back_s, back_r, at_s, at_r, in_s, save_s, *rest,
    n_expert, n_context, n_dp, early,
):
    e, c, me, n, peer = ring(n_expert, n_context)
    group, halves, slab, width = res.shape
    seqs = group // n_expert
    ff = win.shape[1]
    experts = n
    span = max(16, 256 // group)
    parts, sub = xs.shape[0], xs.shape[2]
    per_half = parts // halves
    steps = sub // span
    reduce = Reduce(
        glow.at[pl.ds(0, early)], *rest[:4], rest[4:], sums, 0, 2, n_dp, n_context
    )
    loads = [
        pltpu.make_async_copy(resid_m, res, in_s.at[0]),
        pltpu.make_async_copy(cot_m, cot, in_s.at[1]),
        pltpu.make_async_copy(w_in.at[c], win, in_s.at[2]),
        pltpu.make_async_copy(w_back.at[c], wback, in_s.at[3]),
    ]
    for cp in loads:
        cp.start()
    enter(peer, n, reduce)
    rows, cols = group * span, experts * span
    spread = (
        lax.broadcasted_iota(jnp.int32, (experts, cols), 1) // span
        == lax.broadcasted_iota(jnp.int32, (experts, cols), 0)
    ).astype(BF)
    gather = (
        lax.broadcasted_iota(jnp.int32, (cols, experts), 0) // span
        == lax.broadcasted_iota(jnp.int32, (cols, experts), 1)
    ).astype(BF)
    diag = lax.rem(lax.broadcasted_iota(jnp.int32, (rows, cols), 0), span) == lax.rem(
        lax.broadcasted_iota(jnp.int32, (rows, cols), 1), span
    )

    def within(b, g):
        return pl.ds(pl.multiple_of(b % per_half * sub + g * span, span), span)

    def filled(b, g):
        place = lax.broadcasted_iota(jnp.int32, (group, span, 1), 1) + (
            (b // per_half * n_expert + e) * slab + b % per_half * sub + g * span
        )
        ok = place.astype(F32) < live_m[:, pl.ds(0, 1), pl.ds(0, 1)]
        return jnp.where(ok, 1.0, 0.0).reshape(rows, 1) > 0

    loads[0].wait()
    loads[1].wait()
    sent = []
    for b in range(parts):
        h = b // per_half

        def first(g, _):
            at, here = pl.ds(pl.multiple_of(g * span, span), span), within(b, g)
            r = res[:, h, here, :].reshape(rows, width).astype(F32)
            normed, _ = normalized(r)
            ug = (normed * gain[...]).astype(BF)
            u[:, h, here, :] = ug.reshape(group, span, width)
            logits = jnp.where(filled(b, g), dot(ug, wc[...]), NEG_FILL).reshape(group, span, experts)
            ex = jnp.exp(logits - jnp.max(logits, 0, keepdims=True))
            w = (ex / jnp.sum(ex, 0, keepdims=True)).reshape(rows, experts)
            wts[b * steps + g] = w
            wide = jnp.where(diag, dot(w.astype(BF), spread), 0.0).astype(BF)
            cg = cot[:, h, here, :].reshape(rows, width)
            mixed[b, :, at, :] = dot(wide, ug, ((0,), (0,))).astype(BF).reshape(experts, span, width)
            dexp[b, :, at, :] = dot(wide, cg, ((0,), (0,))).astype(BF).reshape(experts, span, width)
            return 0

        lax.fori_loop(0, steps, first, 0)
        for i, (src, dst) in enumerate(((mixed, xs), (dexp, des))):
            dst[b, 0] = src[b, me]
            for k in range(1, n):
                j, pe, pc = peer(k)
                cp = pltpu.make_async_remote_copy(
                    src_ref=src.at[b, j], dst_ref=dst.at[b, k],
                    send_sem=go_s.at[i, b, k], recv_sem=go_r.at[i, b, k],
                    device_id={"expert": pe, "context": pc}, device_id_type=MESH,
                )
                cp.start()
                sent.append((b, cp))
    loads[2].wait()
    loads[3].wait()
    tile = 512
    returned = []
    rows_in = n * sub
    for b in range(parts):
        for bb, cp in sent:
            if bb == b:
                cp.wait_recv()
        x = xs[b].reshape(rows_in, width)
        de = des[b].reshape(rows_in, width)

        def expert_tile(f, carry):
            eo, dm = carry
            at = pl.ds(pl.multiple_of(f * tile, tile), tile)
            pre = dot(x, win[:, at])
            sq = pre * pre
            t = jnp.tanh(0.7978845608028654 * pre * (1.0 + 0.044715 * sq))
            act = (0.5 * pre * (1.0 + t)).astype(BF)
            slope = 0.5 * (1.0 + t) + 0.5 * pre * (1.0 - t * t) * (
                0.7978845608028654 * (1.0 + 3 * 0.044715 * sq)
            )
            d_pre = (slope * dot(de, wback[at, :], ((1,), (1,)))).astype(BF)
            acts[pl.ds(b * rows_in, rows_in), at] = act
            d_pres[pl.ds(b * rows_in, rows_in), at] = d_pre
            return eo + dot(act, wback[at, :]), dm + dot(d_pre, win[:, at], ((1,), (1,)))

        zero = jnp.zeros((rows_in, width), F32)
        eo, dm = lax.fori_loop(0, ff // tile, expert_tile, (zero, zero))
        eos[b] = eo.astype(BF).reshape(n, sub, width)
        dms[b] = dm.astype(BF).reshape(n, sub, width)
        for i, (src, dst) in enumerate(((eos, eor), (dms, dmr))):
            dst[b, me] = src[b, 0]
            for k in range(1, n):
                j, pe, pc = peer(n - k)
                cp = pltpu.make_async_remote_copy(
                    src_ref=src.at[b, k], dst_ref=dst.at[b, me],
                    send_sem=back_s.at[i, b, k], recv_sem=back_r.at[i, b, k],
                    device_id={"expert": pe, "context": pc}, device_id_type=MESH,
                )
                cp.start()
                returned.append((b, cp))
    per = width // 128
    tokens = parts * rows_in

    def grad_tile(f, _):
        at = pl.ds(pl.multiple_of(f * tile, tile), tile)
        g = dot(xs[...].reshape(tokens, width), d_pres[:, at], ((0,), (0,)))
        glow[pl.ds(f * per, per)] = g.astype(BF).reshape(per, 128, tile)
        g = dot(acts[:, at], des[...].reshape(tokens, width), ((0,), (0,)))
        glow[pl.ds((ff // tile + f) * per, per)] = g.astype(BF).reshape(per, 128, width)
        reduce.tick(f, swap=False)
        return 0

    lax.fori_loop(0, ff // tile, grad_tile, 0)
    blocks = glow.shape[0]
    out, dat = mixed, dexp
    for _, sending in sent:
        sending.wait_send()
    keep = [
        pltpu.make_async_copy(glow.at[pl.ds(early, blocks - early)], part_o, save_s.at[0])
    ]
    keep[0].start()
    gc_o[...] = jnp.zeros_like(gc_o)
    gm_o[...] = jnp.zeros_like(gm_o)
    sq_o[...] = jnp.zeros_like(sq_o)
    moving = []
    for b in range(parts):
        h = b // per_half
        for bb, cp in returned:
            if bb == b:
                cp.wait_recv()
        if b == parts - 1:
            reduce.release(ff // tile + b * steps)

        def second(g, _):
            at, here = pl.ds(pl.multiple_of(g * span, span), span), within(b, g)
            r = res[:, h, here, :].reshape(rows, width).astype(F32)
            normed, rstd = normalized(r)
            ug = u[:, h, here, :].reshape(rows, width)
            cg = cot[:, h, here, :].reshape(rows, width)
            ok = filled(b, g)
            eg = eor[b, :, at, :].reshape(cols, width)
            dg = dmr[b, :, at, :].reshape(cols, width)
            w = wts[b * steps + g]
            wide = jnp.where(diag, dot(w.astype(BF), spread), 0.0).astype(BF)
            mix = dot(wide, eg)
            full = r + mix
            out[b, :, at, :] = full.astype(BF).reshape(group, span, width)
            sq_o[pl.ds(0, 1), :] += jnp.sum(jnp.where(ok, full * full, 0.0), 0, keepdims=True)
            sq_o[pl.ds(1, 1), :] += jnp.sum(jnp.where(ok, mix * mix, 0.0), 0, keepdims=True)
            dw = jnp.where(diag, dot(cg, eg, ((1,), (1,))) + dot(ug, dg, ((1,), (1,))), 0.0)
            high = dw.astype(BF)
            rest = (dw - high.astype(F32)).astype(BF)
            dw = dot(high, gather) + dot(rest, gather)
            inner = jnp.sum((w * dw).reshape(group, span, experts), 0, keepdims=True)
            d_log = (
                (w.reshape(group, span, experts) * (dw.reshape(group, span, experts) - inner))
                .reshape(rows, experts)
                .astype(BF)
            )
            gc_o[...] += dot(d_log, ug, ((0,), (0,)))
            d_u = dot(d_log, wc[...], ((1,), (1,))) + dot(wide, dg)
            gm_o[...] += jnp.sum(d_u * normed, 0, keepdims=True)
            q = d_u * gain[...]
            d_res = cg.astype(F32) + rstd * (
                q - jnp.mean(q, -1, keepdims=True) - normed * jnp.mean(q * normed, -1, keepdims=True)
            )
            dat[b, :, at, :] = d_res.astype(BF).reshape(group, span, width)
            reduce.tick(ff // tile + b * steps + g, swap=b == parts - 1)
            return 0

        lax.fori_loop(0, steps, second, 0)
        mine = pl.ds(pl.multiple_of(e * slab + b % per_half * sub, sub), sub)
        for k in range(1, n_expert):
            pe = lax.rem(e + k, n_expert)
            cp = pltpu.make_async_remote_copy(
                src_ref=dat.at[b, pl.ds(pe * seqs, seqs)], dst_ref=d_attn.at[:, h, mine, :],
                send_sem=at_s.at[b, k], recv_sem=at_r.at[b, k],
                device_id={"expert": pe}, device_id_type=MESH,
            )
            cp.start()
            moving.append(cp)
        cp = pltpu.make_async_copy(
            dat.at[b, pl.ds(e * seqs, seqs)], d_attn.at[:, h, mine, :], at_s.at[b, 0]
        )
        cp.start()
        moving.append(cp)
    cp = pltpu.make_async_copy(out, out_m, save_s.at[2])
    cp.start()
    for _, sending in returned:
        sending.wait_send()
    reduce.finish(ff // tile + parts * steps)
    for cp in moving + keep + [cp]:
        cp.wait()


def mix(resid_m, cot_m, live_m, gain, wc, w_in, w_back, n_expert, n_context, n_dp, early):
    group, halves, slab, width = resid_m.shape
    seqs = group // n_expert
    n = n_expert * n_context
    ff = w_in.shape[-1]
    span = max(16, 256 // group)
    parts, sub = halves * 2, slab // 2
    steps = sub // span
    blocks = 2 * width * ff // (128 * 512)
    sem = pltpu.SemaphoreType.DMA
    block = pltpu.VMEM((group, halves, slab, width), BF)
    turned = pltpu.VMEM((parts, n, sub, width), BF)
    return pl.pallas_call(
        functools.partial(
            mix_kernel, n_expert=n_expert, n_context=n_context, n_dp=n_dp, early=early
        ),
        out_shape=(
            jax.ShapeDtypeStruct((seqs, halves, slab * n_expert, width), BF),
            jax.ShapeDtypeStruct((parts, group, sub, width), BF),
            jax.ShapeDtypeStruct((blocks - early, 128, 512), BF),
            jax.ShapeDtypeStruct((n_context, blocks, 128, 512), BF),
            jax.ShapeDtypeStruct((n, width), F32),
            jax.ShapeDtypeStruct((1, width), F32),
            jax.ShapeDtypeStruct((2, width), F32),
        ),
        in_specs=[ANY, ANY, VM, VM, VM, ANY, ANY],
        out_specs=(ANY, ANY, ANY, ANY, VM, VM, VM),
        scratch_shapes=[
            block, block, block,
            pltpu.VMEM((parts * steps, group * span, n), F32),
            turned, turned, turned, turned, turned, turned, turned, turned,
            pltpu.VMEM((width, ff), BF), pltpu.VMEM((ff, width), BF),
            pltpu.VMEM((halves * n * slab, ff), BF), pltpu.VMEM((halves * n * slab, ff), BF),
            pltpu.VMEM((blocks, 128, 512), BF),
            sem((2, parts, n)), sem((2, parts, n)),
            sem((2, parts, n)), sem((2, parts, n)),
            sem((parts, n_expert)), sem((parts, n_expert)),
            sem((4,)), sem((3,)),
            *reduce_scratch(early, n_context),
        ],
        compiler_params=pltpu.CompilerParams(
            collective_id=1, has_side_effects=True, vmem_limit_bytes=63 * 1024 * 1024
        ),
        name="mix_and_experts",
    )(resid_m, cot_m, live_m, gain, wc, w_in, w_back)


def backward_kernel(
    d_attn, tok_a, qkv_a, att_a, lse, kmark, qmark, gain, wqkv, wout, out_m, part, sums_in,
    dtok_o, last_o, out_o, sums, gq_o, go_o, gg_o,
    da, tok, qkv, att, datt, delta, dkv, dqkv, dtok, bias, own,
    out_s, out_r, tok_s, tok_r, in_s, own_s, *rest,
    n_expert, n_context, n_dp, base,
):
    e, c, me, n, peer = ring(n_expert, n_context)
    seqs, length, width = da.shape
    half = length // n_context
    slab = half // n_expert
    qn = 256
    loads = [
        pltpu.make_async_copy(src, dst, in_s.at[i])
        for i, (src, dst) in enumerate(
            ((d_attn, da), (att_a, att), (qkv_a, qkv), (tok_a, tok),
             (part.at[pl.ds(0, own.shape[0])], own))
        )
    ]
    reduce = Reduce(own, *rest[:4], rest[4:], sums, base, 2, n_dp, n_context)
    for cp in loads:
        cp.start()
    enter(peer, n, reduce)
    crossing = []
    per_half = out_m.shape[0] // n_context
    sub = slab // per_half
    for b in range(per_half):
        mine = pl.ds(pl.multiple_of(e * slab + b * sub, sub), sub)
        for k in range(1, n):
            j, pe, pc = peer(k)
            cp = pltpu.make_async_remote_copy(
                src_ref=out_m.at[pc * per_half + b, pl.ds(pe * seqs, seqs)],
                dst_ref=out_o.at[c, :, mine, :],
                send_sem=out_s.at[b, k], recv_sem=out_r.at[b, k],
                device_id={"expert": pe, "context": pc}, device_id_type=MESH,
            )
            cp.start()
            crossing.append(cp)
        cp = pltpu.make_async_copy(
            out_m.at[c * per_half + b, pl.ds(e * seqs, seqs)], out_o.at[c, :, mine, :], own_s.at[2, b]
        )
        cp.start()
        crossing.append(cp)
    lane = lax.broadcasted_iota(jnp.int32, (qn, 128), 1)
    gg_o[...] = jnp.zeros_like(gg_o)
    for cp in loads:
        cp.wait()
    pairs = width // 128
    for s in range(seqs):
        datt[...] = dot(da[s], wout[...], ((1,), (1,))).astype(BF)
        turned = dot(wout[...], da[s], ((1,), (1,))).astype(BF).astype(F32) * att[s].astype(F32)
        delta[...] = jnp.sum(turned.reshape(HEADS, width // HEADS, length), 1)
        go = dot(att[s], da[s])
        go_o[...] = go if s == 0 else go_o[...] + go
        dkv[...] = jnp.zeros_like(dkv)
        for qb in range(length // qn):
            kk = (qb + 1) * qn
            rows = pl.ds(qb * qn, qn)
            mask_bias(bias, kmark, qmark, s, qb * qn, qn)

            def pair(hp, _):
                at = pl.multiple_of(hp * 128, 128)
                q2 = qkv[s, rows, pl.ds(at, 128)] * BF(0.125)
                k2 = qkv[s, pl.ds(0, kk), pl.ds(width + at, 128)]
                v2 = qkv[s, pl.ds(0, kk), pl.ds(2 * width + at, 128)]
                do2 = datt[rows, pl.ds(at, 128)]
                kt = k2.T
                dqs, dss, lows, qms, doms = [], [], [], [], []
                for h in range(2):
                    mine = (lane >= 64) if h else (lane < 64)
                    qm = jnp.where(mine, q2, jnp.zeros_like(q2))
                    dom = jnp.where(mine, do2, jnp.zeros_like(do2))
                    st = dot(k2, qm, ((1,), (1,))) + bias[pl.ds(0, kk), :]
                    p = jnp.exp(st - lse[s, pl.ds(2 * hp + h, 1), rows])
                    dp = dot(v2, dom, ((1,), (1,)))
                    ds = (p * (dp - delta[pl.ds(2 * hp + h, 1), rows])).astype(BF)
                    dqs.append(dot(kt[h * 64 : h * 64 + 64], ds))
                    dss.append(ds)
                    lows.append(p.astype(BF))
                    qms.append(qm)
                    doms.append(dom)
                dqkv[rows, pl.ds(at, 128)] = (
                    (jnp.concatenate(dqs, 0) * 0.125).T.astype(BF)
                )
                dkv[pl.ds(0, kk), pl.ds(at, 128)] += dot(dss[0], qms[0]) + dot(dss[1], qms[1])
                dkv[pl.ds(0, kk), pl.ds(width + at, 128)] += dot(lows[0], doms[0]) + dot(
                    lows[1], doms[1]
                )
                @pl.when(lax.rem(hp, 2) == 1)
                def _():
                    reduce.tick(((s * (length // qn) + qb) * pairs + hp) // 2)

                return 0

            lax.fori_loop(0, pairs, pair, 0)
        dqkv[:, pl.ds(width, 2 * width)] = dkv[...].astype(BF)
        for h in range(n_context):
            rows = pl.ds(h * half, half)
            normed, rstd = normalized(tok[s, h].astype(F32))
            a = (normed * gain[...]).astype(BF)
            gq = dot(a, dqkv[rows, :], ((0,), (0,)))
            gq_o[...] = gq if s == 0 and h == 0 else gq_o[...] + gq
            d_a = dot(dqkv[rows, :], wqkv[...], ((1,), (1,)))
            gg_o[...] += jnp.sum(d_a * normed, 0, keepdims=True)
            q = d_a * gain[...]
            dt = da[s, rows, :].astype(F32) + rstd * (
                q - jnp.mean(q, -1, keepdims=True) - normed * jnp.mean(q * normed, -1, keepdims=True)
            )
            dtok[s, h] = dt.astype(BF)
        if s == seqs - 1:
            cp = pltpu.make_async_copy(dtok.at[s], last_o, own_s.at[0, 1])
            cp.start()
            crossing.append(cp)
            continue
        for k in range(1, n_context):
            pc = lax.rem(c + k, n_context)
            cp = pltpu.make_async_remote_copy(
                src_ref=dtok.at[s, pc], dst_ref=dtok_o.at[c, s],
                send_sem=tok_s.at[s, k], recv_sem=tok_r.at[s, k],
                device_id={"context": pc}, device_id_type=MESH,
            )
            cp.start()
            crossing.append(cp)
        cp = pltpu.make_async_copy(dtok.at[s, c], dtok_o.at[c, s], own_s.at[1, s])
        cp.start()
        crossing.append(cp)
    reduce.finish(seqs * (length // qn) * pairs // 2)
    for cp in crossing:
        cp.wait()


def backward(
    d_attn, tok_a, qkv, att, lse, kmark, qmark, gain, wqkv, wout, out_m, part, sums,
    n_expert, n_context, n_dp, count,
):
    seqs, length, width = d_attn.shape
    half = length // n_context
    n = n_expert * n_context
    sem = pltpu.SemaphoreType.DMA
    return pl.pallas_call(
        functools.partial(
            backward_kernel, n_expert=n_expert, n_context=n_context, n_dp=n_dp,
            base=sums.shape[1] - part.shape[0],
        ),
        out_shape=(
            jax.ShapeDtypeStruct((n_context, seqs, half, width), BF),
            jax.ShapeDtypeStruct((n_context, half, width), BF),
            jax.ShapeDtypeStruct((n_context, seqs, half, width), BF),
            jax.ShapeDtypeStruct(sums.shape, BF),
            jax.ShapeDtypeStruct((width, 3 * width), F32),
            jax.ShapeDtypeStruct((width, width), F32),
            jax.ShapeDtypeStruct((1, width), F32),
        ),
        in_specs=[ANY, ANY, ANY, ANY, VM, VM, VM, VM, VM, VM, ANY, ANY, ANY],
        out_specs=(ANY, ANY, ANY, ANY, VM, VM, VM),
        input_output_aliases={12: 3},
        scratch_shapes=[
            pltpu.VMEM((seqs, length, width), BF),
            pltpu.VMEM((seqs, n_context, half, width), BF),
            pltpu.VMEM((seqs, length, 3 * width), BF),
            pltpu.VMEM((seqs, width, length), BF),
            pltpu.VMEM((length, width), BF),
            pltpu.VMEM((HEADS, length), F32),
            pltpu.VMEM((length, 2 * width), F32),
            pltpu.VMEM((length, 3 * width), BF),
            pltpu.VMEM((seqs, n_context, half, width), BF),
            pltpu.VMEM((length, 256), F32),
            pltpu.VMEM((count, *part.shape[1:]), BF),
            sem((2, n)), sem((2, n)),
            sem((seqs, n_context)), sem((seqs, n_context)),
            sem((5,)), sem((3, 2)),
            *reduce_scratch(count, n_context),
        ],
        compiler_params=pltpu.CompilerParams(
            collective_id=2, has_side_effects=True, vmem_limit_bytes=VMEM_LIMIT
        ),
        name="attend_backward",
    )(d_attn, tok_a, qkv, att, lse, kmark, qmark, gain, wqkv, wout, out_m, part, sums)


def share_kernel(
    gq, go, gc, gg, gm, sq, sq_mix, live, last, part_in, dtok_in, sums_in,
    packed_o, misc_o, dtok_o, sums,
    pack, other, chip, corners, along, whole, own,
    core_s, core_r, chip_s, chip_r, dp_s, dp_r, dp2_s, dp2_r, out_s, out_r, fin_s, fin_r, tok_s, tok_r, own_s, *rest,
    n_expert, n_context, n_dp,
):
    e, c, z = (lax.axis_index(a) for a in ("expert", "context", "dp"))
    core = lax.rem(e, 2)
    chips = n_expert // 2 * n_context
    me = lax.div(e, 2) * n_context + c
    width = go.shape[1]
    total = pack.shape[0]
    part = total // 2
    piece = part // chips
    lanes = width // n_dp
    twin = {"expert": e + 1 - 2 * core}

    def chip_at(k):
        j = lax.rem(me + k, chips)
        return j, {"expert": lax.div(j, n_context) * 2 + core, "context": lax.rem(j, n_context)}

    barrier = pltpu.get_barrier_semaphore()
    count = own.shape[0]
    load = pltpu.make_async_copy(
        part_in.at[pl.ds(part_in.shape[0] - count, count)], own, own_s.at[0]
    )
    load.start()
    reduce = Reduce(own, *rest[:4], rest[4:], sums, sums.shape[1] - count, 2, n_dp, n_context)
    ticks = [0]

    def tick(times):
        for _ in range(times):
            if ticks[0] < count + 2 * (n_dp - 1):
                reduce.tick(ticks[0])
                ticks[0] += 1

    seq = dtok_o.shape[1] - 1
    where = [twin] + [chip_at(k)[1] for k in range(1, chips)]
    where += [{"dp": lax.rem(z + k, n_dp)} for k in range(1, n_dp)]
    for to in where:
        pl.semaphore_signal(barrier, inc=1, device_id=to, device_id_type=MESH)
    for b in range(3):
        pack[pl.ds(b * width, width), :] = gq[:, pl.ds(b * width, width)].astype(BF)
    pack[pl.ds(3 * width, width), :] = go[...].astype(BF)
    at = gc.shape[0]
    misc_o[...] = jnp.zeros_like(misc_o)
    misc_o[pl.ds(0, at), :] = gc[...]
    for row in (gg[...], gm[...], sq_mix[pl.ds(0, 1), :], sq[...], sq_mix[pl.ds(1, 1), :], live[...]):
        misc_o[pl.ds(at, 1), :] = row
        at += 1
    pack[pl.ds(4 * width, total - 4 * width), :] = jnp.zeros((total - 4 * width, width), BF)
    pack[pl.ds(4 * width, misc_o.shape[0]), :] = misc_o[...].astype(BF)
    pl.semaphore_wait(barrier, len(where))

    def remote(src, dst, ss, rs, to):
        cp = pltpu.make_async_remote_copy(
            src_ref=src, dst_ref=dst, send_sem=ss, recv_sem=rs, device_id=to, device_id_type=MESH
        )
        cp.start()
        return cp

    def rows(i, n):
        return pl.ds(pl.multiple_of(i * n, 16), n)

    bulk = [
        remote(
            last.at[lax.rem(c + k, n_context)], dtok_o.at[c, seq], tok_s.at[k], tok_r.at[k],
            {"context": lax.rem(c + k, n_context)},
        )
        for k in range(1, n_context)
    ]
    keep = pltpu.make_async_copy(last.at[c], dtok_o.at[c, seq], own_s.at[1])
    keep.start()
    sent = []
    for k in range(chips):
        j = lax.rem(me + k + 1, chips)
        at = pl.ds(pl.multiple_of((1 - core) * part + j * piece, 16), piece)
        sent.append(remote(pack.at[at], other.at[rows(j, piece)], core_s.at[k], core_r.at[k], twin))
    first = list(sent)
    for k in range(chips):
        j = lax.rem(me + k + 1, chips)
        first[k].wait_recv()
        at = pl.ds(pl.multiple_of(core * part + j * piece, 16), piece)
        chip[rows(j, piece), :] = (
            pack[at, :].astype(F32) + other[rows(j, piece), :].astype(F32)
        ).astype(BF)
        if k < chips - 1:
            _, to = chip_at(k + 1)
            sent.append(
                remote(chip.at[rows(j, piece)], corners.at[k], chip_s.at[k], chip_r.at[k], to)
            )
    load.wait()
    tick(4)
    acc = chip[rows(me, piece), :].astype(F32)
    for k in range(chips - 1):
        sent[chips + k].wait_recv()
        acc += corners[k].astype(F32)
    chip[rows(me, piece), :] = acc.astype(BF)
    mine = pl.ds(pl.multiple_of(z * lanes, lanes), lanes)
    steps = []
    for k in range(1, n_dp):
        to = lax.rem(z + k, n_dp)
        theirs = pl.ds(pl.multiple_of(to * lanes, lanes), lanes)
        steps.append(
            remote(
                chip.at[rows(me, piece), theirs], along.at[k - 1], dp_s.at[k - 1], dp_r.at[k - 1],
                {"dp": to},
            )
        )
    tick(2)
    acc = chip[rows(me, piece), mine].astype(F32)
    for k in range(1, n_dp):
        steps[k - 1].wait_recv()
        acc += along[k - 1].astype(F32)
    home = pl.ds(pl.multiple_of(core * part + me * piece, 16), piece)
    whole[home, mine] = acc.astype(BF)
    back = []
    for k in range(1, n_dp):
        to = lax.rem(z + k, n_dp)
        back.append(
            remote(
                whole.at[home, mine], whole.at[home, mine], dp2_s.at[k - 1], dp2_r.at[k - 1],
                {"dp": to},
            )
        )
    tick(2)
    for cp in back:
        cp.wait_recv()
    spread = [remote(whole.at[home], whole.at[home], fin_s.at[0], fin_r.at[0], twin)]
    outs = []
    for k in range(1, chips):
        _, to = chip_at(k)
        outs.append(remote(whole.at[home], whole.at[home], out_s.at[k - 1], out_r.at[k - 1], to))
    tick(3)
    for k in range(1, chips):
        outs[k - 1].wait_recv()
        tick(1)
        j = lax.rem(me + chips - k, chips)
        got = whole.at[pl.ds(pl.multiple_of(core * part + j * piece, 16), piece)]
        spread.append(remote(got, got, fin_s.at[k], fin_r.at[k], twin))
    for cp in spread:
        cp.wait_recv()
    stored = pltpu.make_async_copy(whole.at[pl.ds(0, 4 * width)], packed_o, own_s.at[2])
    stored.start()
    misc_o[...] = whole[pl.ds(4 * width, misc_o.shape[0]), :].astype(F32)
    reduce.finish(ticks[0])
    for cp in sent + steps + back + outs + spread:
        cp.wait_send()
    for cp in bulk:
        cp.wait()
    keep.wait()
    stored.wait()


def share(gq, go, gc, gg, gm, sq, sq_mix, live, last, part_in, dtok, sums, n_expert, n_context, n_dp, count):
    width = go.shape[1]
    chips = n_expert // 2 * n_context
    unit = 2 * chips * 16
    rows = -(-(gc.shape[0] + 6) // 16) * 16
    total = -(-(4 * width + rows) // unit) * unit
    part = total // 2
    piece = part // chips
    sem = pltpu.SemaphoreType.DMA
    return pl.pallas_call(
        functools.partial(share_kernel, n_expert=n_expert, n_context=n_context, n_dp=n_dp),
        out_shape=(
            jax.ShapeDtypeStruct((4 * width, width), BF),
            jax.ShapeDtypeStruct((rows, width), F32),
            jax.ShapeDtypeStruct(dtok.shape, BF),
            jax.ShapeDtypeStruct(sums.shape, BF),
        ),
        in_specs=[VM] * 8 + [ANY] * 4,
        out_specs=(ANY, VM, ANY, ANY),
        input_output_aliases={10: 2, 11: 3},
        scratch_shapes=[
            pltpu.VMEM((total, width), BF),
            pltpu.VMEM((part, width), BF),
            pltpu.VMEM((part, width), BF),
            pltpu.VMEM((max(1, chips - 1), piece, width), BF),
            pltpu.VMEM((max(1, n_dp - 1), piece, width // n_dp), BF),
            pltpu.VMEM((total, width), BF),
            pltpu.VMEM((count, *sums.shape[2:]), BF),
            sem((chips,)), sem((chips,)), sem((chips,)), sem((chips,)),
            sem((n_dp,)), sem((n_dp,)), sem((n_dp,)), sem((n_dp,)),
            sem((chips,)), sem((chips,)), sem((chips,)), sem((chips,)),
            sem((n_context,)), sem((n_context,)), sem((3,)),
            *reduce_scratch(count, n_context),
        ],
        compiler_params=pltpu.CompilerParams(
            collective_id=3, has_side_effects=True, vmem_limit_bytes=VMEM_LIMIT
        ),
        name="share_gradients",
    )(gq, go, gc, gg, gm, sq, sq_mix, live, last, part_in, dtok, sums)


def widen_kernel(src_in, src_back, packed, gi, gb, gq, go):
    gi[0] = src_in[0].reshape(gi.shape[1:]).astype(F32)
    gb[0] = src_back[0].reshape(gb.shape[1:]).astype(F32)
    width = go.shape[1]
    rows = go.shape[0]
    at = (pl.program_id(0) * pl.num_programs(1) + pl.program_id(1)) * rows
    for b in range(4):
        block = packed[pl.ds(pl.multiple_of(b * width + at, 16), rows), :].astype(F32)
        if b < 3:
            gq[:, pl.ds(b * width, width)] = block
        else:
            go[...] = block


def widen(sums, packed, width, ff):
    n_context, blocks = sums.shape[:2]
    tiles = ff // 512
    per = blocks // (2 * tiles)
    rows = width // (n_context * tiles)
    return pl.pallas_call(
        widen_kernel,
        grid=(n_context, tiles),
        out_shape=(
            jax.ShapeDtypeStruct((n_context, width, ff), F32),
            jax.ShapeDtypeStruct((n_context, ff, width), F32),
            jax.ShapeDtypeStruct((width, 3 * width), F32),
            jax.ShapeDtypeStruct((width, width), F32),
        ),
        in_specs=[
            pl.BlockSpec((1, per, 128, 512), lambda c, f: (c, f, 0, 0)),
            pl.BlockSpec((1, per, 128, 512), lambda c, f: (c, tiles + f, 0, 0)),
            pl.BlockSpec(packed.shape, lambda c, f: (0, 0)),
        ],
        out_specs=(
            pl.BlockSpec((1, width, 512), lambda c, f: (c, 0, f)),
            pl.BlockSpec((1, 512, width), lambda c, f: (c, f, 0)),
            pl.BlockSpec((rows, 3 * width), lambda c, f: (c * tiles + f, 0)),
            pl.BlockSpec((rows, width), lambda c, f: (c * tiles + f, 0)),
        ),
        compiler_params=pltpu.CompilerParams(vmem_limit_bytes=32 * 1024 * 1024),
        name="widen_sums",
    )(sums, sums, packed)


def per_device(n_expert, n_context, n_dp, tokens, gain_attn, wqkv, w_out, gain_mix, w_control, w_in, w_back, segments, valid, cotangent):
    reps, seqs, half, width = tokens.shape
    length = half * n_context
    slab = half // n_expert
    group = seqs * n_expert
    e, c = lax.axis_index("expert"), lax.axis_index("context")

    def pick(x, i, axis=0):
        return lax.dynamic_index_in_dim(x, i, axis, keepdims=False)

    seg_a, valid_a = pick(segments, c), pick(valid, c)
    kmark = jnp.where(valid_a > 0, seg_a, -1)[:, :, None]
    qmark = seg_a[:, None, :]
    lengths = jnp.sum((valid_a > 0).astype(F32), 1)
    live = jnp.broadcast_to(lengths[:, None, None], (seqs, 8, 128))
    resid_m, cot_m, live_m, tok_a, qkv, att, lse, sq = forward(
        tokens, cotangent, kmark, qmark, live, gain_attn[None], wqkv, w_out, n_expert, n_context
    )
    blocks = 2 * width * w_in.shape[-1] // (128 * 512)
    first, final = blocks * 11 // 32, blocks * 10 // 32
    d_attn, out_m, part, sums, grad_control, grad_gain_mix, sq_mix = mix(
        resid_m, cot_m, live_m, gain_mix[None], w_control, w_in, w_back,
        n_expert, n_context, n_dp, first,
    )
    d_tokens, last, output, sums, grad_qkv, grad_out, grad_gain = backward(
        d_attn.reshape(seqs, length, width), tok_a, qkv, att, lse, kmark, qmark, gain_attn[None],
        wqkv, w_out, out_m, part, sums, n_expert, n_context, n_dp, blocks - first - final,
    )
    n_all = grad_control.shape[0]
    count = jnp.pad(jnp.sum(lengths)[None, None], ((0, 0), (0, width - 1)))
    packed, misc, d_tokens, sums = share(
        grad_qkv, grad_out, grad_control, grad_gain, grad_gain_mix, sq, sq_mix, count,
        last, part, d_tokens, sums, n_expert, n_context, n_dp, final,
    )
    grad_control = misc[:n_all].T
    grad_gain, grad_gain_mix = misc[n_all], misc[n_all + 1]
    squares = jnp.sum(misc[n_all + 2 : n_all + 6], 1)
    grad_in, grad_back, grad_qkv, grad_out = widen(sums, packed, width, w_in.shape[-1])
    stats = jnp.sqrt(squares[:3] / (squares[3] * width))
    return (
        output, d_tokens, grad_gain, grad_qkv, grad_out, grad_gain_mix, grad_control,
        grad_in, grad_back, stats,
    )


def solution(mesh):
    shards = P("dp", "expert", "context", None)
    rows = P("dp", "expert", None)
    experts = P("expert", None, None)
    return jax.shard_map(
        functools.partial(
            per_device, mesh.shape["expert"], mesh.shape["context"], mesh.shape["dp"]
        ),
        mesh=mesh,
        in_specs=(shards, P(), P(), P(), P(), P(), experts, experts, rows, rows, shards),
        out_specs=(shards, shards, P(), P(), P(), P(), P(), experts, experts, P()),
        check_vma=False,
    )
```
